32 devices in a mesh: row: 16 (over z, x, core), col: 2 (over y).
Axes of the slice: x: 2, y: 2, z: 4, core: 2. Of those that a mesh axis runs over, the one named last changes fastest.
Arguments:
- tokens: bfloat16 [27696, 1024], P('row', 'col'), may hold values from -80 to 80
- cotangent: bfloat16 [27696, 1024], P('row', 'col'), may hold values from -80 to 80
- ln1_gain: float32 [1024], replicated, may hold values from 0.2 to 4
- ln1_bias: float32 [1024], replicated, may hold values from -3 to 3
- ln2_gain: float32 [1024], replicated, may hold values from 0.2 to 4
- ln2_bias: float32 [1024], replicated, may hold values from -3 to 3
- w_qkv: bfloat16 [3, 1024, 1024], P(None, 'row', 'col'), may hold values from -0.1875 to 0.1875
- qv_bias: float32 [2, 1024], P(None, 'col'), may hold values from -3 to 3
- w_out: bfloat16 [1024, 1024], P('col', 'row'), may hold values from -0.75 to 0.75
- out_bias: float32 [1024], replicated, may hold values from -3 to 3
- w_up: bfloat16 [1024, 4096], P('row', 'col'), may hold values from -0.1875 to 0.1875
- up_bias: float32 [4096], P('col'), may hold values from -3 to 3
- w_down: bfloat16 [4096, 1024], P('col', 'row'), may hold values from -0.1875 to 0.1875
- down_bias: float32 [1024], replicated, may hold values from -3 to 3
- adapter_ids: int32 [48], P('row'), may hold values from 0 to 7
- a_qkv: bfloat16 [1024, 384], replicated, may hold values from -0.1875 to 0.1875
- b_qkv: bfloat16 [3, 128, 1024], P(None, None, 'col'), may hold values from -0.75 to 0.75
- a_out: bfloat16 [1024, 128], P('col'), may hold values from -0.1875 to 0.1875
- b_out: bfloat16 [128, 1024], replicated, may hold values from -0.75 to 0.75
- a_up: bfloat16 [1024, 128], replicated, may hold values from -0.1875 to 0.1875
- b_up: bfloat16 [128, 4096], P(None, 'col'), may hold values from -0.75 to 0.75
- a_down: bfloat16 [4096, 128], P('col'), may hold values from -0.09375 to 0.09375
- b_down: bfloat16 [128, 1024], replicated, may hold values from -0.75 to 0.75
Outputs:
- layer_out: bfloat16 [27696, 1024], P('row', 'col')
- tokens_grad: float32 [27696, 1024], P('row', 'col')
- grad_a_qkv: float32 [1024, 384], replicated
- grad_b_qkv: float32 [3, 128, 1024], P(None, None, 'col')
- grad_a_out: float32 [1024, 128], P('col')
- grad_b_out: float32 [128, 1024], replicated
- grad_a_up: float32 [1024, 128], replicated
- grad_b_up: float32 [128, 4096], P(None, 'col')
- grad_a_down: float32 [4096, 128], P('col')
- grad_b_down: float32 [128, 1024], replicated
The draws below stay inside these ranges and needn't reach their ends.
Inputs may be any that keep to these rules, and one draw needn't show every extreme that they name: `adapter_ids`: each image's adapter number.
All inputs are finite; a program needn't handle non-finite values.
Results may differ from the reference program's by a relative error of at most 0.019.
The reference program's roundings to bfloat16 on the way count: a program that leaves them out, or rounds other values in their place, can miss the bound.
Values may be sent and summed in bfloat16 or wider, within the bound.
No kernel may reach another device: no remote copies, remote signals or barrier semaphores. Data moves between devices by JAX's collectives and lax.ppermute only.
A program may use at most 320 MiB of HBM per device.

```python
import jax
import jax.numpy as jnp
from jax import lax

D = 1024
FF = 4096
HD = 64
HEADS = 16
SEQ = 577
IMG_DEV = 3
IMAGES = 48
TOKENS = 27696
ADAPTERS = 8
RANK = 16
ADAPT_COLS = 128
N_ROW = 16
N_COL = 2


def rising_rows(key, with_offset):
    keys = jax.random.split(key, 4)
    place = jnp.arange(D, dtype=jnp.float32) / D
    count = IMAGES * SEQ
    ratio = 3.0
    core = jax.random.truncated_normal(keys[0], -4.0, 4.0, (count, D), jnp.float32)
    row_scale = jnp.exp(jax.random.uniform(keys[1], (count, 1), jnp.float32, -0.7, 0.7))
    column_scale = ratio ** place * jnp.exp(jax.random.uniform(keys[2], (D,), jnp.float32, -0.35, 0.35))
    shift = 0.5 * jax.random.truncated_normal(keys[3], -3.0, 3.0, (D,), jnp.float32) * with_offset
    return core * row_scale * column_scale[None, :] + shift[None, :]


def rising_gain(key):
    place = jnp.arange(D, dtype=jnp.float32) / D
    jitter = jnp.exp(jax.random.uniform(key, (D,), jnp.float32, -0.3, 0.3))
    return 0.6 * 3.0 ** place * jitter


def draw_tokens(key, part):
    return rising_rows(jax.random.fold_in(key, 1), 1.0).astype(jnp.bfloat16)


def draw_cotangent(key, part):
    return rising_rows(jax.random.fold_in(key, 2), 0.0).astype(jnp.bfloat16)


def draw_ln1_gain(key, part):
    return rising_gain(jax.random.fold_in(key, 3))


def draw_ln2_gain(key, part):
    return rising_gain(jax.random.fold_in(key, 4))


def place_ends(result, rng, smallest, largest):
    spot = [jax.random.randint(jax.random.fold_in(rng, axis), (), 0, length) for axis, length in enumerate(result.shape)]
    widest = result.shape.index(max(result.shape))
    neighbour = spot[:widest] + [(spot[widest] + 1) % result.shape[widest]] + spot[widest + 1:]
    return result.at[tuple(spot)].set(smallest).at[tuple(neighbour)].set(largest)


def steps_of(key, dims, pieces, smallest, top_value):
    level, own = 1.0, jax.random.fold_in(key, 6)
    for position, blocks in pieces:
        draws = jnp.exp(jax.random.uniform(jax.random.fold_in(own, position), (blocks,), jnp.float32, smallest / len(pieces), top_value / len(pieces)))
        level = level * jnp.repeat(draws, dims[position] // blocks).reshape([-1 if axis == position else 1 for axis in range(len(dims))])
    return level


def scatter_about(rng, shape, deviation, limit, shards=(), kind=jnp.bfloat16):
    factor_of = steps_of(rng, shape, shards, -0.22, 0.18) if shards else 1.0
    entries = jax.random.normal(rng, shape, jnp.float32) * deviation * factor_of
    return jnp.minimum(jnp.maximum(entries, -limit), limit).astype(kind)


def setup_inputs(seed: int = 0) -> dict:
    seeds = jax.random.split(jax.random.key(seed), 24)
    tokens = draw_tokens(jax.random.fold_in(seeds[23], 71), 0)
    cotangent = draw_cotangent(jax.random.fold_in(seeds[23], 71), 0)
    ln1_gain = draw_ln1_gain(jax.random.fold_in(seeds[23], 71), 0)
    ln1_bias = scatter_about(seeds[3], (D,), 0.3, 3.0, (), jnp.float32)
    ln2_gain = draw_ln2_gain(jax.random.fold_in(seeds[23], 71), 0)
    ln2_bias = scatter_about(seeds[5], (D,), 0.3, 3.0, (), jnp.float32)
    w_qkv = scatter_about(seeds[6], (3, D, D), D ** -0.5, 0.1875, ((1, 16), (2, 2)))
    qv_bias = scatter_about(seeds[7], (2, D), 0.5, 3.0, ((1, 2),), jnp.float32)
    w_out = scatter_about(seeds[8], (D, D), (D // 16) ** -0.5, 0.75, ((0, 2), (1, 16)))
    out_bias = scatter_about(seeds[9], (D,), 0.5, 3.0, (), jnp.float32)
    w_up = scatter_about(seeds[10], (D, FF), D ** -0.5, 0.1875, ((0, 16), (1, 2)))
    up_bias = scatter_about(seeds[11], (FF,), 0.5, 3.0, ((0, 2),), jnp.float32)
    w_down = scatter_about(seeds[12], (FF, D), (FF // 4) ** -0.5, 0.1875, ((0, 2), (1, 16)))
    down_bias = scatter_about(seeds[13], (D,), 0.5, 3.0, (), jnp.float32)
    adapter_ids = place_ends(jax.random.randint(seeds[14], (IMAGES,), 0, ADAPTERS), jax.random.fold_in(seeds[14], 1), 0, ADAPTERS - 1).astype(jnp.int32)
    a_qkv = scatter_about(seeds[15], (D, 3 * ADAPT_COLS), D ** -0.5, 0.1875)
    b_qkv = scatter_about(seeds[16], (3, ADAPT_COLS, D), (4 * RANK) ** -0.5, 0.75, ((2, 2),))
    a_out = scatter_about(seeds[17], (D, ADAPT_COLS), D ** -0.5, 0.1875, ((0, 2),))
    b_out = scatter_about(seeds[18], (ADAPT_COLS, D), (4 * RANK) ** -0.5, 0.75)
    a_up = scatter_about(seeds[19], (D, ADAPT_COLS), D ** -0.5, 0.1875)
    b_up = scatter_about(seeds[20], (ADAPT_COLS, FF), (4 * RANK) ** -0.5, 0.75, ((1, 2),))
    a_down = scatter_about(seeds[21], (FF, ADAPT_COLS), FF ** -0.5, 0.09375, ((0, 2),))
    b_down = scatter_about(seeds[22], (ADAPT_COLS, D), (4 * RANK) ** -0.5, 0.75)
    return {"tokens": tokens, "cotangent": cotangent, "ln1_gain": ln1_gain, "ln1_bias": ln1_bias, "ln2_gain": ln2_gain, "ln2_bias": ln2_bias, "w_qkv": w_qkv, "qv_bias": qv_bias, "w_out": w_out, "out_bias": out_bias, "w_up": w_up, "up_bias": up_bias, "w_down": w_down, "down_bias": down_bias, "adapter_ids": adapter_ids, "a_qkv": a_qkv, "b_qkv": b_qkv, "a_out": a_out, "b_out": b_out, "a_up": a_up, "b_up": b_up, "a_down": a_down, "b_down": b_down}


@jax.custom_vjp
def low(v):
    return lax.optimization_barrier(v.astype(jnp.bfloat16)).astype(jnp.float32)

@jax.custom_vjp
def low_back(v):
    return v

def low_keep(v):
    return (low(v), None)

def low_pass(kept, grad):
    return (grad,)

def back_keep(v):
    return (v, None)

def back_low(kept, grad):
    return (low(grad),)
low.defvjp(low_keep, low_pass)
low_back.defvjp(back_keep, back_low)
EPS = 1e-05
GELU_SCALE = 1.702

def exact_einsum(form, first, second):
    return jnp.einsum(form, first, second, precision=lax.Precision.HIGHEST)

def norm_rows(values, gain, offset):
    centre = lax.optimization_barrier(jnp.mean(values, axis=1, keepdims=True))
    centred = values - centre
    spread = lax.optimization_barrier(jnp.mean(centred * centred, axis=1, keepdims=True))
    return centred * lax.rsqrt(spread + EPS) * gain + offset

def attend(blocks):
    queries, key_rows, value_rows = blocks
    raw_scores = exact_einsum('qhd,khd->hqk', queries, key_rows)
    scores = low_back(raw_scores * HD ** (-0.5))
    weights = jax.nn.softmax(scores, axis=-1)
    return exact_einsum('hqk,khd->qhd', low(weights), value_rows)

def block_forward(inputs, adapters, frozen, select):
    a_qkv, b_qkv, a_out, b_out, a_up, b_up, a_down, b_down = adapters
    ln1_gain, ln1_bias, ln2_gain, ln2_bias, w_qkv, qv_bias, w_out, out_bias, w_up, up_bias, w_down, down_bias = frozen
    row_count = inputs.shape[0]
    part_width = D // N_COL
    hidden_part = FF // N_COL
    normed = low(norm_rows(inputs, ln1_gain, ln1_bias))
    copies = low_back(jnp.broadcast_to(normed, (N_COL, row_count, D)))
    projected = exact_einsum('ctd,kdce->kcte', copies, w_qkv.reshape(3, D, N_COL, part_width))
    low_qkv = exact_einsum('ctd,dj->ctj', copies, a_qkv).reshape(N_COL, row_count, 3, ADAPT_COLS)
    low_qkv = low(low_back(low_qkv * select[None, :, None, :]))
    projected = projected + exact_einsum('ctkj,kjce->kcte', low_qkv, b_qkv.reshape(3, ADAPT_COLS, N_COL, part_width))
    bias_rows = jnp.stack([qv_bias[0], jnp.zeros_like(qv_bias[0]), qv_bias[1]]).reshape(3, N_COL, 1, part_width)
    qkv = low(low_back(projected + bias_rows))
    qkv = jnp.transpose(qkv, (0, 2, 1, 3)).reshape(3, row_count // SEQ, SEQ, HEADS, HD)
    attended = lax.map(jax.checkpoint(attend), (qkv[0], qkv[1], qkv[2]))
    attended = low(low_back(attended.reshape(row_count, N_COL, part_width)))
    out_terms = exact_einsum('tcp,cpe->cte', attended, w_out.reshape(N_COL, part_width, D))
    low_out = exact_einsum('tcp,cpj->ctj', attended, a_out.reshape(N_COL, part_width, ADAPT_COLS)) * select[None]
    low_out = low(low_back(low_out))
    out_terms = out_terms + exact_einsum('ctj,je->cte', low_out, b_out)
    hidden = inputs + low_back(lax.optimization_barrier(jnp.sum(low(out_terms), axis=0)) + out_bias)
    normed_two = low(norm_rows(hidden, ln2_gain, ln2_bias))
    copies_two = low_back(jnp.broadcast_to(normed_two, (N_COL, row_count, D)))
    pre_up = exact_einsum('ctd,dcf->ctf', copies_two, w_up.reshape(D, N_COL, hidden_part))
    low_up = low(low_back(exact_einsum('ctd,dj->ctj', copies_two, a_up) * select[None]))
    pre_up = pre_up + exact_einsum('ctj,jcf->ctf', low_up, b_up.reshape(ADAPT_COLS, N_COL, hidden_part))
    pre_up = low_back(pre_up + up_bias.reshape(N_COL, 1, hidden_part))
    activated = low(pre_up * jax.nn.sigmoid(GELU_SCALE * pre_up))
    down_terms = exact_einsum('ctf,cfe->cte', activated, w_down.reshape(N_COL, hidden_part, D))
    low_down = exact_einsum('ctf,cfj->ctj', activated, a_down.reshape(N_COL, hidden_part, ADAPT_COLS)) * select[None]
    low_down = low(low_back(low_down))
    down_terms = down_terms + exact_einsum('ctj,je->cte', low_down, b_down)
    return hidden + low_back(lax.optimization_barrier(jnp.sum(low(down_terms), axis=0)) + down_bias)

def reference(tokens, cotangent, ln1_gain, ln1_bias, ln2_gain, ln2_bias, w_qkv, qv_bias, w_out, out_bias, w_up, up_bias, w_down, down_bias, adapter_ids, a_qkv, b_qkv, a_out, b_out, a_up, b_up, a_down, b_down):
    frozen = tuple((value.astype(jnp.float32) for value in (ln1_gain, ln1_bias, ln2_gain, ln2_bias, w_qkv, qv_bias, w_out, out_bias, w_up, up_bias, w_down, down_bias)))
    adapters = tuple((value.astype(jnp.float32) for value in (a_qkv, b_qkv, a_out, b_out, a_up, b_up, a_down, b_down)))
    group_rows = IMG_DEV * SEQ
    inputs_all = tokens.astype(jnp.float32).reshape(N_ROW, group_rows, D)
    cotangents = cotangent.astype(jnp.float32).reshape(N_ROW, group_rows, D)
    group_ids = adapter_ids.reshape(N_ROW, IMG_DEV)
    owners = jnp.arange(ADAPT_COLS, dtype=jnp.int32) // RANK

    def one_group(carry, blocks):
        inputs, grad_out, image_ids = blocks
        select = jnp.repeat((image_ids[:, None] == owners[None, :]).astype(jnp.float32), SEQ, axis=0)
        output, pull = jax.vjp(lambda values, params: block_forward(values, params, frozen, select), inputs, adapters)
        grad_inputs, grad_params = pull(grad_out)
        carry = jax.tree.map(lambda total, term: total + term, carry, grad_params)
        return (carry, (output.astype(jnp.bfloat16), grad_inputs))
    initial = tuple((jnp.zeros_like(value) for value in adapters))
    totals, (outputs, grads) = lax.scan(one_group, initial, (inputs_all, cotangents, group_ids))
    return (outputs.reshape(TOKENS, D), grads.reshape(TOKENS, D), totals[0], totals[1], totals[2], totals[3], totals[4], totals[5], totals[6], totals[7])
```

```python
import functools

import jax
import jax.numpy as jnp
from jax import lax
from jax.experimental import pallas as pl
from jax.experimental.pallas import tpu as pltpu
from jax.sharding import PartitionSpec as P

HD = 64
RANK = 16


EPS = 1e-05
GELU_SCALE = 1.702


def column_sums(first, second):
    return lax.psum((first, second), "col")


def gather_features(values):
    return lax.all_gather(values, "col", axis=1, tiled=True)


def sum_partials(terms):
    return lax.psum_scatter(
        terms.astype(jnp.bfloat16), "col", scatter_dimension=1, tiled=True
    ).astype(jnp.float32)


def norm_split(values, feature_width):
    first, second = column_sums(jnp.sum(values, axis=1), jnp.sum(values * values, axis=1))
    centre = first / feature_width
    inverse = lax.rsqrt(second / feature_width - centre * centre + EPS)
    return ((values - centre[:, None]) * inverse[:, None], inverse)


def norm_back(grad_normed, normal_rows, inverse, gain_part, feature_width):
    scaled = grad_normed * gain_part
    first, second = column_sums(jnp.sum(scaled, axis=1), jnp.sum(scaled * normal_rows, axis=1))
    return inverse[:, None] * (
        scaled - first[:, None] / feature_width - normal_rows * second[:, None] / feature_width
    )


def select_rows(low_rank, onehot, image_len):
    image_count, stack_width = onehot.shape
    shaped = low_rank.reshape(image_count, image_len, -1, stack_width)
    return (shaped * onehot[:, None, None, :]).reshape(low_rank.shape).astype(jnp.bfloat16)


def mult(form, first, second):
    return jnp.einsum(form, first, second, preferred_element_type=jnp.float32)


def on_device(
    tokens,
    cotangent,
    ln1_gain,
    ln1_bias,
    ln2_gain,
    ln2_bias,
    w_qkv,
    qv_bias,
    w_out,
    out_bias,
    w_up,
    up_bias,
    w_down,
    down_bias,
    adapter_ids,
    a_qkv,
    b_qkv,
    a_out,
    b_out,
    a_up,
    b_up,
    a_down,
    b_down,
):
    row_count, part_width = tokens.shape
    feature_width = a_qkv.shape[0]
    stack_width = a_qkv.shape[1] // 3
    image_count = adapter_ids.shape[0]
    image_len = row_count // image_count
    head_count = part_width // HD
    scale = HD ** (-0.5)
    offset = lax.axis_index("col") * part_width

    def own_part(values, axis):
        return lax.dynamic_slice_in_dim(values, offset, part_width, axis)

    owners = lax.iota(jnp.int32, stack_width) // RANK
    onehot = (adapter_ids[:, None] == owners[None, :]).astype(jnp.float32)
    wide_qkv, wide_out, wide_up, wide_down = (
        lax.all_gather(w_qkv, "row", axis=1, tiled=True),
        lax.all_gather(w_out, "row", axis=1, tiled=True),
        lax.all_gather(w_up, "row", axis=0, tiled=True),
        lax.all_gather(w_down, "row", axis=1, tiled=True),
    )
    inputs = tokens.astype(jnp.float32)
    normal_one, inverse_one = norm_split(inputs, feature_width)
    normed_part = (normal_one * own_part(ln1_gain, 0) + own_part(ln1_bias, 0)).astype(jnp.bfloat16)
    normed_one = gather_features(normed_part)
    projected = mult("td,kde->kte", normed_one, wide_qkv)
    kept_qkv = select_rows(mult("td,dj->tj", normed_one, a_qkv), onehot, image_len)
    projected = projected + mult("tkj,kje->kte", kept_qkv.reshape(row_count, 3, stack_width), b_qkv)
    bias_rows = jnp.stack([qv_bias[0], jnp.zeros_like(qv_bias[0]), qv_bias[1]])[:, None, :]
    qkv = (projected + bias_rows).astype(jnp.bfloat16)
    shaped = qkv.reshape(3, image_count, image_len, head_count, HD)
    queries, key_rows, value_rows = (shaped[0], shaped[1], shaped[2])
    scores = mult("bqhd,bkhd->bhqk", queries, key_rows) * scale
    highest = jnp.max(scores, axis=-1, keepdims=True)
    log_total = highest + jnp.log(jnp.sum(jnp.exp(scores - highest), axis=-1, keepdims=True))
    weights_low = jnp.exp(scores - log_total).astype(jnp.bfloat16)
    attended = mult("bhqk,bkhd->bqhd", weights_low, value_rows)
    attended = attended.reshape(row_count, part_width).astype(jnp.bfloat16)
    kept_out = select_rows(mult("tc,cj->tj", attended, a_out), onehot, image_len)
    out_terms = mult("tc,cd->td", attended, wide_out) + mult("tj,jd->td", kept_out, b_out)
    hidden = inputs + sum_partials(out_terms) + own_part(out_bias, 0)
    normal_two, inverse_two = norm_split(hidden, feature_width)
    normed_part_two = (normal_two * own_part(ln2_gain, 0) + own_part(ln2_bias, 0)).astype(
        jnp.bfloat16
    )
    normed_two = gather_features(normed_part_two)
    kept_up = select_rows(mult("td,dj->tj", normed_two, a_up), onehot, image_len)
    pre_up = mult("td,df->tf", normed_two, wide_up) + mult("tj,jf->tf", kept_up, b_up) + up_bias
    logistic = jax.nn.sigmoid(GELU_SCALE * pre_up)
    activated = (pre_up * logistic).astype(jnp.bfloat16)
    kept_down = select_rows(mult("tf,fj->tj", activated, a_down), onehot, image_len)
    down_terms = mult("tf,fd->td", activated, wide_down) + mult("tj,jd->td", kept_down, b_down)
    layer_out = (hidden + sum_partials(down_terms) + own_part(down_bias, 0)).astype(jnp.bfloat16)
    wide_qkv, wide_out, wide_up, wide_down = (
        lax.all_gather(w_qkv, "row", axis=1, tiled=True),
        lax.all_gather(w_out, "row", axis=1, tiled=True),
        lax.all_gather(w_up, "row", axis=0, tiled=True),
        lax.all_gather(w_down, "row", axis=1, tiled=True),
    )
    grad_layer = cotangent.astype(jnp.float32)
    grad_full = gather_features(cotangent)
    d_low_down = select_rows(mult("td,jd->tj", grad_full, b_down), onehot, image_len)
    d_activated = mult("td,fd->tf", grad_full, wide_down) + mult("tj,fj->tf", d_low_down, a_down)
    grad_b_down = mult("tj,td->jd", kept_down, grad_full)
    grad_a_down = mult("tf,tj->fj", activated, d_low_down)
    d_pre_up = (
        d_activated * (logistic + GELU_SCALE * pre_up * logistic * (1.0 - logistic))
    ).astype(jnp.bfloat16)
    d_low_up = select_rows(mult("tf,jf->tj", d_pre_up, b_up), onehot, image_len)
    grad_b_up = mult("tj,tf->jf", kept_up, d_pre_up)
    grad_a_up = mult("td,tj->dj", normed_two, d_low_up)
    normed_two_terms = mult("tf,df->td", d_pre_up, wide_up) + mult("tj,dj->td", d_low_up, a_up)
    d_normed_two = sum_partials(normed_two_terms)
    grad_hidden = grad_layer + norm_back(
        d_normed_two, normal_two, inverse_two, own_part(ln2_gain, 0), feature_width
    )
    hidden_full_grad = gather_features(grad_hidden.astype(jnp.bfloat16))
    d_low_out = select_rows(mult("td,jd->tj", hidden_full_grad, b_out), onehot, image_len)
    d_attended = mult("td,cd->tc", hidden_full_grad, wide_out) + mult("tj,cj->tc", d_low_out, a_out)
    grad_b_out = mult("tj,td->jd", kept_out, hidden_full_grad)
    grad_a_out = mult("tc,tj->cj", attended, d_low_out)
    d_heads = d_attended.astype(jnp.bfloat16).reshape(image_count, image_len, head_count, HD)
    scores_again = mult("bqhd,bkhd->bhqk", queries, key_rows) * scale
    weights_again = jnp.exp(scores_again - log_total)
    weights_again_low = weights_again.astype(jnp.bfloat16)
    d_weights = mult("bqhd,bkhd->bhqk", d_heads, value_rows)
    d_values = mult("bhqk,bqhd->bkhd", weights_again_low, d_heads)
    d_scores = weights_again * (
        d_weights - jnp.sum(weights_again * d_weights, axis=-1, keepdims=True)
    )
    d_scores = d_scores.astype(jnp.bfloat16)
    d_queries = scale * mult("bhqk,bkhd->bqhd", d_scores, key_rows)
    d_keys = scale * mult("bhqk,bqhd->bkhd", d_scores, queries)
    d_qkv = (
        jnp.stack([d_queries, d_keys, d_values])
        .reshape(3, row_count, part_width)
        .astype(jnp.bfloat16)
    )
    d_low_qkv = mult("kte,kje->tkj", d_qkv, b_qkv)
    d_low_qkv = select_rows(d_low_qkv.reshape(row_count, 3 * stack_width), onehot, image_len)
    grad_b_qkv = mult("tkj,kte->kje", kept_qkv.reshape(row_count, 3, stack_width), d_qkv)
    grad_a_qkv = mult("td,tj->dj", normed_one, d_low_qkv)
    normed_one_terms = mult("kte,kde->td", d_qkv, wide_qkv) + mult("tj,dj->td", d_low_qkv, a_qkv)
    d_normed_one = sum_partials(normed_one_terms)
    tokens_grad = grad_hidden + norm_back(
        d_normed_one, normal_one, inverse_one, own_part(ln1_gain, 0), feature_width
    )
    grad_a_qkv, grad_b_out, grad_a_up, grad_b_down = lax.psum(
        (grad_a_qkv, grad_b_out, grad_a_up, grad_b_down), ("row", "col")
    )
    grad_b_qkv, grad_a_out, grad_b_up, grad_a_down = (
        lax.psum(grad_b_qkv.astype(jnp.bfloat16), "row").astype(jnp.float32),
        lax.psum(grad_a_out.astype(jnp.bfloat16), "row").astype(jnp.float32),
        lax.psum(grad_b_up.astype(jnp.bfloat16), "row").astype(jnp.float32),
        lax.psum(grad_a_down.astype(jnp.bfloat16), "row").astype(jnp.float32),
    )
    return (
        layer_out,
        tokens_grad,
        grad_a_qkv,
        grad_b_qkv,
        grad_a_out,
        grad_b_out,
        grad_a_up,
        grad_b_up,
        grad_a_down,
        grad_b_down,
    )


NT = (((1,), (1,)), ((), ()))
NN = (((1,), (0,)), ((), ()))
F32 = jnp.float32
BF16 = jnp.bfloat16
VMEM_LIMIT = 60 * 1024 * 1024
SPOT = pl.BlockSpec(memory_space=pltpu.SMEM)


def dot(first, second, dims=NN):
    return lax.dot_general(first, second, dims, preferred_element_type=F32)


def dot_rows(first, second):
    return dot(first.T, second)


def call(body, grid, in_specs, out_specs, out_shape, scratch=()):
    return pl.pallas_call(
        body,
        grid=grid,
        in_specs=in_specs,
        out_specs=out_specs,
        out_shape=out_shape,
        scratch_shapes=list(scratch),
        compiler_params=pltpu.CompilerParams(
            dimension_semantics=("arbitrary",) * len(grid), vmem_limit_bytes=VMEM_LIMIT
        ),
    )


def fixed(shape):
    zeros = (0,) * len(shape)
    return pl.BlockSpec(shape, lambda *_: zeros, pipeline_mode=pl.Buffered(1))


def struct(shape, kind):
    return jax.ShapeDtypeStruct(shape, kind)


def norm_of(values):
    centred = values - jnp.mean(values, axis=1, keepdims=True)
    inverse = lax.rsqrt(jnp.mean(centred * centred, axis=1, keepdims=True) + EPS)
    return centred * inverse, inverse


def norm_pull(grad, normal, inverse, gain):
    scaled = grad * gain
    return inverse * (
        scaled
        - jnp.mean(scaled, axis=1, keepdims=True)
        - normal * jnp.mean(scaled * normal, axis=1, keepdims=True)
    )


def settle(place, pieces, side_first, store):
    depth = pieces[0].shape[0]
    n_far = depth // 2
    for group, piece in enumerate(pieces):
        for index in range(depth):
            other, outer, inner, back = (
                group // 2, group % 2, index // n_far, index % n_far
            )
            x_off, y_off = (outer, inner) if side_first else (inner, outer)
            far = lax.rem(place[0] + (n_far - back), n_far)
            x = place[1] if x_off == 0 else 1 - place[1]
            core = place[2] if other == 0 else 1 - place[2]
            y = place[3] if y_off == 0 else 1 - place[3]
            store(far * 4 + x * 2 + core, y, piece[index])


def settle_qkv(place, pieces0, pieces1, w_ref):
    half = pieces1[0].shape[2]

    def lanes(y):
        return pl.ds(pl.multiple_of(y * half, half), half)

    def first(row, y, block):
        w_ref[0, row, :, lanes(y)] = block[:, :half]
        w_ref[1, row, :, lanes(y)] = block[:, half:]

    def last(row, y, block):
        w_ref[2, row, :, lanes(y)] = block

    settle(place, pieces0, False, first)
    settle(place, pieces1, True, last)


def settle_out(place, pieces1, w_ref):
    half = pieces1[0].shape[2]

    def store(row, y, block):
        w_ref[row, :, pl.ds(pl.multiple_of(y * half, half), half)] = block

    settle(place, pieces1, True, store)


def chosen(index, first, second):
    return jnp.where(index == 0, first, second)


def both_halves(place, own, near, far):
    diagonal = place[2] == place[3]
    mine = jnp.where(diagonal, own, near)
    other = jnp.where(diagonal, near, far)
    return chosen(place[3], mine, other), chosen(place[3], other, mine)


def halves_out(place, values, rows, own_ref, near_ref, far_ref):
    half = values.shape[1] // 2
    left, right = values[:, :half], values[:, half:]
    mine, other = chosen(place[3], left, right), chosen(place[3], right, left)
    own_ref[rows, :] = mine
    near_ref[rows, :] = jnp.where(place[2] == place[3], other, mine)
    far_ref[rows, :] = other


def spread_body(length, cut, own_rows, tb, place, t_ref, own_ref, near_ref, far_ref, wide_ref):
    wide_ref[...] = t_ref[...].astype(F32)

    def put(ref, start, shared, shared_count):
        ref[:length, :] = wide_ref[start : start + length, :].astype(BF16)
        ref[own_rows : own_rows + shared_count, :] = wide_ref[
            shared : shared + shared_count, :
        ].astype(BF16)

    for ref, index in ((own_ref, place[2]), (near_ref, 1 - place[3]), (far_ref, 1 - place[2])):
        ref[...] = jnp.zeros_like(ref)

        @pl.when(index == 0)
        def _():
            put(ref, 0, length, cut)

        @pl.when(index == 1)
        def _():
            put(ref, 2 * length, length + cut, length - cut)


def join_body(length, cut, own_rows, place, own_ref, near_ref, far_ref, out_ref, wide_ref):
    diagonal = place[2] == place[3]
    mine = jnp.where(diagonal, own_ref[...], near_ref[...])
    mate = jnp.where(diagonal, near_ref[...], far_ref[...])
    first = chosen(place[2], mine, mate).astype(F32)
    second = chosen(place[2], mate, mine).astype(F32)
    wide_ref[:length, :] = first[:length]
    wide_ref[length : length + cut, :] = first[own_rows : own_rows + cut]
    wide_ref[length + cut : 2 * length, :] = second[own_rows : own_rows + length - cut]
    wide_ref[2 * length :, :] = second[:length]
    out_ref[...] = wide_ref[...].astype(out_ref.dtype)


def qkv_body(
    scale, place, own_ref, near_ref, far_ref, gain, bias, p0, p1, p2, p3, r0, r1, r2, r3, a_ref,
    b_ref, qv_ref, sel_ref, x_ref, z_ref, u_ref, out_ref, keep_out, send_out, w_ref,
):
    width = x_ref.shape[1]
    half = width // 2
    stack = sel_ref.shape[1]

    @pl.when(pl.program_id(0) == 0)
    def _():
        settle_qkv(place, (p0, p1, p2, p3), (r0, r1, r2, r3), w_ref)

    left, right = both_halves(place, own_ref[...], near_ref[...], far_ref[...])
    x = jnp.concatenate([left, right], axis=1)
    x_ref[...] = x
    normal, _ = norm_of(x.astype(F32))
    z = (normal * gain[...] + bias[...]).astype(BF16)
    z_ref[...] = z
    low = dot(z, a_ref[...])
    for k in range(3):
        kept = (low[:, k * stack : (k + 1) * stack] * sel_ref[...]).astype(BF16)
        u_ref[:, k * stack : (k + 1) * stack] = kept
        w = w_ref[k].reshape(width, width)
        parts = []
        for y in range(2):
            lanes = slice(y * half, (y + 1) * half)
            acc = dot(z, w[:, lanes]) + dot(kept, b_ref[y, :, k * half : (k + 1) * half])
            out = (acc + qv_ref[k, :, lanes]).astype(BF16)
            if k == 0:
                out = out * jnp.asarray(scale, BF16)
            out_ref[k, :, lanes] = out
            parts.append(out)
        keep_out[k] = chosen(place[2], parts[0], parts[1])
        send_out[k] = chosen(place[2], parts[1], parts[0])


def attend_one(q, k, v, mask, p_ref):
    lane = lax.broadcasted_iota(jnp.int32, q.shape, 1)
    one, zero = jnp.ones_like(q), jnp.zeros_like(q)
    parts = []
    for head in range(2):
        spare = HD if head == 0 else 0
        here = lane < HD if head == 0 else lane >= HD
        mine = jnp.where(here, q, jnp.where(lane == spare, one, zero))
        s = dot(mine, jnp.where(lane == spare, mask, k), NT)
        e = jnp.exp(s - jnp.max(s, axis=1, keepdims=True))
        p = (e * (1.0 / jnp.sum(e, axis=1, keepdims=True))).astype(BF16)
        p_ref[head] = p
        parts.append(dot(p, v))
    return jnp.where(lane < HD, parts[0], parts[1]).astype(BF16)


def attend_body(q_ref, k_ref, v_ref, mask_ref, out_ref, p_ref):
    out_ref[...] = attend_one(q_ref[0], k_ref[0], v_ref[0], mask_ref[...], p_ref)


def attend_shared_body(mine_ref, mate_ref, mask_ref, keep_ref, send_ref, p_ref):
    q, k, v = (jnp.concatenate([mine_ref[i], mate_ref[i]]) for i in range(3))
    out = attend_one(q, k, v, mask_ref[...], p_ref)
    keep_ref[...] = out[: keep_ref.shape[0]]
    send_ref[...] = out[keep_ref.shape[0] :]


def attend_back_one(scale, q, k, v, p_ref, att, do):
    low_lanes = lax.broadcasted_iota(jnp.int32, q.shape, 1) < HD
    zero = jnp.zeros_like(q)
    product = att.astype(F32) * do.astype(F32)
    dq = dk = dv = 0.0
    for head in range(2):
        here = low_lanes if head == 0 else ~low_lanes
        my_q, my_k, my_do = (jnp.where(here, t, zero) for t in (q, k, do))
        delta = jnp.sum(jnp.where(here, product, 0.0), axis=1, keepdims=True)
        p = p_ref[head]
        dp = dot(my_do, v, NT)
        ds = (p.astype(F32) * (dp - delta)).astype(BF16)
        dq = dq + dot(ds, my_k)
        dk = dk + dot(ds, my_q, (((0,), (0,)), ((), ())))
        dv = dv + dot(p, my_do, (((0,), (0,)), ((), ())))
    return (dq * scale).astype(BF16), dk.astype(BF16), dv.astype(BF16)


def attend_back_body(scale, q_ref, k_ref, v_ref, p_ref, att_ref, do_ref, out_ref):
    parts = attend_back_one(
        scale, q_ref[0], k_ref[0], v_ref[0], p_ref, att_ref[...], do_ref[...]
    )
    for i in range(3):
        out_ref[i] = parts[i]


def attend_back_shared_body(
    scale, mine_ref, mate_ref, p_ref, att_keep, att_send, do_keep, do_mate, keep_ref, send_ref
):
    q, k, v = (jnp.concatenate([mine_ref[i], mate_ref[i]]) for i in range(3))
    att = jnp.concatenate([att_keep[...], att_send[...]])
    do = jnp.concatenate([do_keep[...], do_mate[...]])
    parts = attend_back_one(scale, q, k, v, p_ref, att, do)
    count = keep_ref.shape[1]
    for i in range(3):
        keep_ref[i] = parts[i][:count]
        send_ref[i] = parts[i][count:]


def out_body(
    place, own_ref, keep_ref, mate_ref, x_ref, r0, r1, r2, r3, a_ref, b_ref, bias_ref, gain,
    lbias, aup_ref, sel_ref, hid_ref, z_ref, u_ref, uup_ref, w_ref,
):
    width = x_ref.shape[1]
    half = width // 2

    @pl.when(pl.program_id(0) == 0)
    def _():
        settle_out(place, (r0, r1, r2, r3), w_ref)

    keep, mate = keep_ref[...], mate_ref[...]
    shared = jnp.concatenate(
        [chosen(place[2], keep, mate), chosen(place[2], mate, keep)], axis=1
    )
    att = jnp.where(pl.program_id(0) < 2, own_ref[...], shared)
    sel = sel_ref[...]
    low = dot(att[:, :half], a_ref[0], NT) + dot(att[:, half:], a_ref[1], NT)
    kept = (low * sel).astype(BF16)
    u_ref[...] = kept
    acc = dot(att, w_ref[...].reshape(width, width), NT) + dot(kept, b_ref[...])
    hidden = x_ref[...].astype(F32) + acc + bias_ref[...]
    hid_ref[...] = hidden
    normal, _ = norm_of(hidden)
    z = (normal * gain[...] + lbias[...]).astype(BF16)
    z_ref[...] = z
    uup_ref[...] = (dot(z, aup_ref[...]) * sel).astype(BF16)


def mlp_body(
    rows, place, z_ref, gown_ref, gnear_ref, gfar_ref, uup_ref, sel_ref, hid_ref, wup_ref,
    wdn_ref, bup_own, bup_near, bup_far, adn_own, adn_near, adn_far, upb_ref, bdn_ref, aup_ref,
    dnb_ref, gain,
    own_ref, near_ref, far_ref, gh_ref, ghb_ref, ekeep_ref, esend_ref,
    down_acc, dz_acc, udn_acc, eup_acc, edn_ref, uup_t, edn_t, act_ref, dup_ref, gy_ref,
):
    total, width = z_ref.shape
    step = pl.program_id(0)
    blocks = [slice(i, i + rows) for i in range(0, total, rows)]

    @pl.when(step == 0)
    def _():
        for b in blocks:
            left, right = both_halves(place, gown_ref[b, :], gnear_ref[b, :], gfar_ref[b, :])
            gy = jnp.concatenate([left, right], axis=1)
            gy_ref[b, :] = gy
            edn_ref[b, :] = (dot(gy, bdn_ref[...], NT) * sel_ref[b, :]).astype(BF16)
        edn_t[...] = edn_ref[...].T
        uup_t[...] = uup_ref[...].T
        down_acc[...] = jnp.zeros_like(down_acc)
        dz_acc[...] = jnp.zeros_like(dz_acc)
        udn_acc[...] = jnp.zeros_like(udn_acc)
        eup_acc[...] = jnp.zeros_like(eup_acc)

    chunk = upb_ref.shape[1]
    wup = wup_ref[...].reshape(width, chunk)
    wdn = wdn_ref[...].reshape(width, chunk)
    parts = pl.num_programs(0) // 2
    y = step // parts

    def adapter(own_ref, near_ref, far_ref):
        near, far = near_ref[...], far_ref[...]
        other = jnp.concatenate([chosen(place[2], near, far), chosen(place[2], far, near)])
        return jnp.where(place[3] == y, own_ref[...], other)

    bup = adapter(bup_own, bup_near, bup_far)
    adn = adapter(adn_own, adn_near, adn_far)
    for b in blocks:
        pre = dot(z_ref[b, :], wup) + dot(uup_ref[b, :], bup) + upb_ref[...]
        q = 1.0 / (1.0 + jnp.exp(-GELU_SCALE * pre))
        act = (pre * q).astype(BF16)
        d_act = dot(gy_ref[b, :], wdn) + dot(edn_ref[b, :], adn)
        d_up = (d_act * (q + GELU_SCALE * pre * q * (1.0 - q))).astype(BF16)
        act_ref[b, :] = act
        dup_ref[b, :] = d_up
        down_acc[b, :] += dot(act, wdn, NT)
        dz_acc[b, :] += dot(d_up, wup, NT)
        udn_acc[b, :] += dot(act, adn, NT)
        eup_acc[b, :] += dot(d_up, bup, NT)
    hidden_half = parts * chunk
    for i, (low, high) in enumerate(((uup_t, dup_ref), (edn_t, act_ref))):
        rows = split_rows(place, dot(low[...], high[...]).astype(BF16))
        lanes = pl.ds(pl.multiple_of(i * hidden_half + step % parts * chunk, chunk), chunk)
        ekeep_ref[y, :, lanes], esend_ref[y, :, lanes] = rows

    @pl.when(step == pl.num_programs(0) - 1)
    def _():
        gbdn = gaup = 0.0
        for b in blocks:
            sel = sel_ref[b, :]
            e_up = (eup_acc[b, :] * sel).astype(BF16)
            u_dn = (udn_acc[b, :] * sel).astype(BF16)
            hidden = hid_ref[b, :]
            y = hidden + down_acc[b, :] + dot(u_dn, bdn_ref[...]) + dnb_ref[...]
            halves_out(place, y.astype(BF16), b, own_ref, near_ref, far_ref)
            dz = dz_acc[b, :] + dot(e_up, aup_ref[...], NT)
            normal, inverse = norm_of(hidden)
            grad = gy_ref[b, :].astype(F32) + norm_pull(dz, normal, inverse, gain[...])
            gh_ref[b, :] = grad
            ghb_ref[b, :] = grad.astype(BF16)
            gbdn = gbdn + dot_rows(u_dn, gy_ref[b, :])
            gaup = gaup + dot_rows(e_up, z_ref[b, :])
        half = width // 2
        for i, grad in enumerate((gaup, gbdn)):
            start = 2 * hidden_half + i * half
            for column in range(2):
                rows = split_rows(place, grad[:, column * half : (column + 1) * half].astype(BF16))
                lanes = slice(start, start + half)
                ekeep_ref[column, :, lanes], esend_ref[column, :, lanes] = rows


def split_rows(place, grad):
    part = grad.shape[0] // 2
    low, high = grad[:part], grad[part:]
    return chosen(place[2], low, high), chosen(place[2], high, low)


def out_back_body(
    place, g_ref, own_ref, keep_ref, mate_ref, r0, r1, r2, r3, a_ref, b_ref, sel_ref, u_ref,
    d_own, d_keep, d_send, g_keep, g_send, w_ref, e_ref, e_t,
):
    width = g_ref.shape[1]
    half = width // 2
    count = keep_ref.shape[0]
    y = pl.program_id(0)

    @pl.when(y == 0)
    def _():
        def store(row, column, block):
            w_ref[column, row] = block

        settle(place, (r0, r1, r2, r3), True, store)
        e = (dot(g_ref[...], b_ref[...], NT) * sel_ref[...]).astype(BF16)
        e_ref[...] = e
        e_t[...] = e.T
        gb = dot(u_ref[...].T, g_ref[...]).astype(BF16)
        for column in range(2):
            rows = split_rows(place, gb[:, column * half : (column + 1) * half])
            g_keep[column, :, half:], g_send[column, :, half:] = rows

    w = w_ref[y].reshape(width, half)
    d = (dot(g_ref[...], w) + dot(e_ref[...], a_ref[0])).astype(BF16)
    d_own[...] = d[: 2 * count]

    shared = jnp.where(place[2] == y, keep_ref[...], mate_ref[...])
    ga = dot(e_t[...], jnp.concatenate([own_ref[...], shared])).astype(BF16)
    g_keep[y, :, :half], g_send[y, :, :half] = split_rows(place, ga)

    @pl.when(place[2] == y)
    def _():
        d_keep[...] = d[2 * count :]

    @pl.when(place[2] != y)
    def _():
        d_send[...] = d[2 * count :]


def whole_rows(place, own, keep, mate):
    shared = jnp.concatenate(
        [chosen(place[2], keep, mate), chosen(place[2], mate, keep)], axis=1
    )
    return jnp.concatenate([own, shared])


def qkv_grads_body(
    place, own_ref, keep_ref, mate_ref, b_ref, sel_ref, u_ref, z_ref, e_ref, keep_out, send_out
):
    width = z_ref.shape[1]
    half = width // 2
    stack = sel_ref.shape[1]
    part = stack // 2
    d = whole_rows(place, own_ref[0], keep_ref[0], mate_ref[0])
    u_t = u_ref[...].T
    low = dot(d[:, :half], b_ref[0], NT) + dot(d[:, half:], b_ref[1], NT)
    e = (low * sel_ref[...]).astype(BF16)
    e_ref[...] = e
    gb = dot(u_t, d).astype(BF16)
    ga = dot(e.T, z_ref[...]).astype(BF16)
    for y in range(2):
        for i, grad in enumerate((gb, ga)):
            low_rows, high_rows = (
                grad[r * part : (r + 1) * part, y * half : (y + 1) * half] for r in range(2)
            )
            keep_out[y, i, 0] = chosen(place[2], low_rows, high_rows)
            send_out[y, i, 0] = chosen(place[2], high_rows, low_rows)


def qkv_back_body(
    place, own_ref, keep_ref, mate_ref, p0, p1, p2, p3, r0, r1, r2, r3, a_ref, e_ref, x_ref,
    gh_ref, gain, own_out, near_out, far_out, w_ref,
):
    width = x_ref.shape[1]
    step = pl.program_id(0)

    @pl.when(step == 0)
    def _():
        settle_qkv(place, (p0, p1, p2, p3), (r0, r1, r2, r3), w_ref)

    dz = dot(e_ref[...], a_ref[...], NT)
    for k in range(3):
        keep, mate = keep_ref[k], mate_ref[k]
        shared = jnp.concatenate(
            [chosen(place[2], keep, mate), chosen(place[2], mate, keep)], axis=1
        )
        d = jnp.where(step < 2, own_ref[k], shared)
        dz = dz + dot(d, w_ref[k].reshape(width, width), NT)
    normal, inverse = norm_of(x_ref[...].astype(F32))
    grad = gh_ref[...] + norm_pull(dz, normal, inverse, gain[...])
    halves_out(place, grad.astype(BF16), slice(None), own_out, near_out, far_out)


def on_chip_pair(
    mesh_shape, tokens, cotangent, ln1_gain, ln1_bias, ln2_gain, ln2_bias, w_qkv, qv_bias, w_out,
    out_bias, w_up, up_bias, w_down, down_bias, adapter_ids, a_qkv, b_qkv, a_out, b_out, a_up,
    b_up, a_down, b_down,
):
    n_row, n_col = mesh_shape
    count, half = tokens.shape
    width = half * 2
    stack = b_out.shape[0]
    part = stack // 2
    hidden_half = w_up.shape[1]
    hidden = hidden_half * 2
    length = count // adapter_ids.shape[0]
    cut = length // 2
    heads = width // HD
    tb = -(-(length + 1) // 32) * 16
    own_rows, total = 2 * tb, 3 * tb
    scale = HD ** (-0.5)
    both = ("row", "col")
    row, col = lax.axis_index("row"), lax.axis_index("col")
    core, side, n_far = row % 2, row // 2 % 2, n_row // 4
    place = jnp.stack([row // 4, side, core, col]).astype(jnp.int32)

    def device(r, c):
        return r * n_col + c

    far_swaps = [[] for _ in range(n_far.bit_length() - 1)]
    far_turns = [[] for _ in range(n_far - 1)]
    ring_in, ring_back, cross, cores, cols_swap, sides_swap = [], [], [], [], [], []
    for r in range(n_row):
        for c in range(n_col):
            k, mate = r % 2, r + 1 - 2 * (r % 2)
            cores.append((device(r, c), device(mate, c)))
            cols_swap.append((device(r, c), device(r, 1 - c)))
            sides_swap.append((device(r, c), device(r ^ 2, c)))
            for turn, pairs in enumerate(far_turns):
                pairs.append((device(r, c), device((r + 4 * (turn + 1)) % n_row, c)))
            for bit, pairs in enumerate(far_swaps):
                pairs.append((device(r, c), device(r ^ (4 << bit), c)))
            if k != c:
                ring_in.append((device(r, c), device(r, 1 - c)))
                ring_back.append((device(r, c), device(mate, c)))
                cross.append((device(r, c), device(mate, 1 - c)))
            else:
                ring_in.append((device(r, c), device(mate, c)))
                ring_back.append((device(r, c), device(r, 1 - c)))

    def move(values, pairs):
        return lax.ppermute(values, both, pairs)

    def pick(pair, index):
        return jnp.where(index == 0, pair[0], pair[1])

    def ordered(mine, other, index, axis):
        return jnp.where(
            index == 0,
            jnp.concatenate([mine, other], axis),
            jnp.concatenate([other, mine], axis),
        )

    def tie(*values):
        return lax.optimization_barrier(values)

    thirds = [struct((total, half), BF16)] * 3
    third_specs = [fixed((total, half))] * 3

    def spread(values):
        return call(
            functools.partial(spread_body, length, cut, own_rows, tb),
            (1,),
            [SPOT, fixed((count, half))],
            third_specs,
            thirds,
            scratch=[pltpu.VMEM((count, half), F32)],
        )(place, values)

    def join(own, near, far, kind):
        return call(
            functools.partial(join_body, length, cut, own_rows),
            (1,),
            [SPOT] + third_specs,
            fixed((count, half)),
            struct((count, half), kind),
            scratch=[pltpu.VMEM((count, half), F32)],
        )(place, own, near, far)

    x_own, x_near, x_far = spread(tokens)
    x_near, x_far, w_qkv, w_out = tie(x_near, x_far, w_qkv, w_out)
    mine_first = jnp.concatenate(
        [jnp.swapaxes(w_qkv, 0, 1).reshape(-1, 3 * half), w_out.T], axis=1
    )
    mine_second = jnp.concatenate([w_up, w_down.T], axis=1)
    adapt_first = jnp.concatenate(
        [jnp.swapaxes(b_qkv, 0, 1).reshape(stack, 3 * half), a_out.T], axis=1
    )
    adapt_second = jnp.concatenate([b_up, a_down.T], axis=1)
    deep = width // n_row

    def turned(block):
        return jnp.stack([block] + [move(block, pairs) for pairs in far_turns])

    def doubled(found, pairs):
        return jnp.concatenate([found, move(found, pairs)])

    def part_of(values):
        return lax.dynamic_slice_in_dim(values, core * part, part, 0)

    def widened(values, near, far):
        return ordered(values[None], ordered(near, far, core, 0)[None], col, 0)

    x_near, x_far = move(x_near, ring_in), move(x_far, cross)
    near0, near1 = turned(mine_first[:, :width]), turned(mine_first[:, width:])
    near0, near1, x_near, x_far, mine_second = tie(near0, near1, x_near, x_far, mine_second)
    x_parts = (x_own, x_near, x_far)
    big_second = lax.all_gather(mine_second, both, axis=0, tiled=False)
    big_second = big_second.reshape(n_row, n_col, deep, 2 * hidden_half)
    near0, near1 = doubled(near0, sides_swap), doubled(near1, cols_swap)
    ad_near = move(part_of(adapt_first), cols_swap)
    biases = jnp.concatenate([qv_bias[0], qv_bias[1], up_bias])[None]
    bias_pair = ordered(biases, move(biases, cols_swap), col, 0)
    ids = jnp.where(core == col, adapter_ids, move(adapter_ids, cores))
    g_own, g_near, g_far = spread(cotangent)
    near0, near1, bias_pair, ids, ad_near = tie(near0, near1, bias_pair, ids, ad_near)
    ad_first = widened(adapt_first, ad_near, move(ad_near, cores))
    last0, last1 = move(near0, cols_swap), move(near1, sides_swap)
    far0, far1 = move(near0, cores), move(near1, cores)
    last0, last1, far0, far1, ad_first, g_near, g_far = tie(
        last0, last1, far0, far1, ad_first, g_near, g_far
    )
    blocks0 = (near0, last0, far0, move(last0, cores))
    blocks1 = (near1, last1, far1, move(last1, cores))
    qv_rows = jnp.stack(
        [
            bias_pair[:, :half].reshape(1, width),
            jnp.zeros((1, width), F32),
            bias_pair[:, half:width].reshape(1, width),
        ]
    )
    up_row = bias_pair[:, width:].reshape(1, hidden)

    owners = lax.iota(jnp.int32, stack) // RANK
    own_id = jnp.where(core == 0, ids[0], ids[2])
    places = lax.iota(jnp.int32, total)[:, None]
    sel = (jnp.where(places < own_rows, own_id, ids[1]) == owners[None]).astype(F32)

    valid = jnp.arange(own_rows)[:, None]
    here, there = jnp.where(core == 0, cut, length - cut), jnp.where(core == 0, length - cut, cut)

    def mask_of(good):
        return jnp.broadcast_to(jnp.where(good, 0.0, -1e30), (own_rows, 2 * HD)).astype(BF16)

    mask_own = mask_of(valid < length)
    mask_shared = mask_of((valid < here) | ((valid >= tb) & (valid < tb + there)))

    gain1, bias1, gain2, bias2 = (t[None] for t in (ln1_gain, ln1_bias, ln2_gain, ln2_bias))

    rows_block = pl.BlockSpec((tb, width), lambda i: (i, 0))
    sel_block = pl.BlockSpec((tb, stack), lambda i: (i, 0))
    every = fixed((total, width))
    thin = fixed((total, stack))
    vec = fixed((1, width))
    pieces0 = [fixed((n_row // 2, deep, width))] * 4
    pieces1 = [fixed((n_row // 2, deep, half))] * 4
    pieces_out = [
        pl.BlockSpec(
            (n_row // 2, deep, half), lambda *_: (0, 0, 1), pipeline_mode=pl.Buffered(1)
        )
    ] * 4
    w_qkv_room = [pltpu.VMEM((3, n_row, deep, width), BF16)]
    w_out_room = [pltpu.VMEM((n_row, deep, width), BF16)]
    ad_out_spec = pl.BlockSpec(
        (n_col, stack, half), lambda *_: (0, 0, 3), pipeline_mode=pl.Buffered(1)
    )
    low_k = pl.BlockSpec((total, stack), lambda k: (0, k))
    own_k = pl.BlockSpec((1, own_rows, width), lambda k: (k, 0, 0))
    shared_k = pl.BlockSpec((1, tb, half), lambda k: (k, 0, 0))
    ad_k = pl.BlockSpec((n_col, stack, half), lambda k: (0, 0, k))
    shared_struct = struct((3, tb, half), BF16)
    half_rows = struct((tb, half), BF16)

    third_rows = pl.BlockSpec((tb, half), lambda i: (i, 0))
    low_block = pl.BlockSpec((tb, 3 * stack), lambda i: (i, 0))
    own_three = pl.BlockSpec((3, tb, width), lambda i: (0, jnp.minimum(i, 1), 0))
    all_three = pl.BlockSpec((3, tb, width), lambda i: (0, i, 0))
    shared_three = fixed((3, tb, half))
    x, z1, u_qkv, qkv, qkv_keep, qkv_send = call(
        functools.partial(qkv_body, scale),
        (3,),
        [
            SPOT, third_rows, third_rows, third_rows, vec, vec, *pieces0, *pieces1,
            fixed((width, 3 * stack)),
            pl.BlockSpec(
                (n_col, stack, 3 * half), lambda i: (0, 0, 0), pipeline_mode=pl.Buffered(1)
            ),
            fixed((3, 1, width)), sel_block,
        ],
        [rows_block, rows_block, low_block, all_three, shared_three, shared_three],
        [
            struct((total, width), BF16),
            struct((total, width), BF16),
            struct((total, 3 * stack), BF16),
            struct((3, total, width), BF16),
            shared_struct,
            shared_struct,
        ],
        scratch=w_qkv_room,
    )(place, *x_parts, gain1, bias1, *blocks0, *blocks1, a_qkv, ad_first, qv_rows, sel)

    qkv_mate = move(qkv_send, cores)
    adapt_part = part_of(adapt_second)
    qkv, g_near, g_far, adapt_part = tie(qkv, g_near, g_far, adapt_part)
    g_near, g_far = move(g_near, ring_in), move(g_far, cross)
    ad_near = move(adapt_part, cols_swap)

    head_specs = [pl.BlockSpec((1, own_rows, 2 * HD), lambda h, k=k: (k, 0, h)) for k in range(3)]
    head_rows = pl.BlockSpec((own_rows, 2 * HD), lambda h: (0, h))
    head_p = pl.BlockSpec((2, own_rows, own_rows), lambda h: (h, 0, 0))
    pair_k = pl.BlockSpec((3, tb, 2 * HD), lambda h: (0, 0, h))
    pair_rows = pl.BlockSpec((tb, 2 * HD), lambda h: (0, h))
    att_own, p_own = call(
        attend_body,
        (heads // 2,),
        head_specs + [fixed((own_rows, 2 * HD))],
        [head_rows, head_p],
        [struct((own_rows, width), BF16), struct((heads, own_rows, own_rows), BF16)],
    )(qkv, qkv, qkv, mask_own)
    qkv_mate, att_own = tie(qkv_mate, att_own)
    att_keep, att_send, p_sh = call(
        attend_shared_body,
        (heads // 4,),
        [pair_k, pair_k, fixed((own_rows, 2 * HD))],
        [pair_rows, pair_rows, head_p],
        [half_rows, half_rows, struct((heads // 2, own_rows, own_rows), BF16)],
    )(qkv_keep, qkv_mate, mask_shared)
    att_mate = move(att_send, cores)
    att_mate, ad_near, g_near, g_far = tie(att_mate, ad_near, g_near, g_far)
    g_parts = (g_own, g_near, g_far)
    ad_second = (adapt_second, ad_near, move(ad_near, cores))

    own_block = pl.BlockSpec((tb, width), lambda i: (jnp.minimum(i, 1), 0))
    shared_rows = fixed((tb, half))
    hid, z2, u_out, u_up = call(
        out_body,
        (3,),
        [
            SPOT, own_block, shared_rows, shared_rows, rows_block, *pieces_out,
            ad_out_spec, fixed((stack, width)), vec, vec, vec, fixed((width, stack)), sel_block,
        ],
        [rows_block, rows_block, sel_block, sel_block],
        [
            struct((total, width), F32),
            struct((total, width), BF16),
            struct((total, stack), BF16),
            struct((total, stack), BF16),
        ],
        scratch=w_out_room,
    )(
        place, att_own, att_keep, att_mate, x, *blocks1, ad_first, b_out, out_bias[None],
        gain2, bias2, a_up, sel,
    )

    chunk = half
    parts = hidden_half // chunk

    def w_spec(shift):
        return pl.BlockSpec(
            (n_row, 1, deep, chunk), lambda j: (0, j // parts, 0, j % parts + shift)
        )

    def ad_specs(shift):
        return [
            pl.BlockSpec((rows, chunk), lambda j: (0, j % parts + shift))
            for rows in (stack, part, part)
        ]

    early_half = fixed((2, part, 2 * hidden_half + 2 * half))
    early_struct = struct((2, part, 2 * hidden_half + 2 * half), BF16)
    y_own, y_near, y_far, g_h, ghb, early_keep, early_send = call(
        functools.partial(mlp_body, tb),
        (2 * parts,),
        [SPOT, every]
        + third_specs
        + [
            thin, thin, every, w_spec(0), w_spec(parts), *ad_specs(0), *ad_specs(parts),
            pl.BlockSpec((1, chunk), lambda j: (0, j)), fixed((stack, width)),
            fixed((width, stack)), vec, vec,
        ],
        third_specs + [every, every, early_half, early_half],
        thirds
        + [struct((total, width), F32), struct((total, width), BF16), early_struct, early_struct],
        scratch=[
            pltpu.VMEM((total, width), F32),
            pltpu.VMEM((total, width), F32),
            pltpu.VMEM((total, stack), F32),
            pltpu.VMEM((total, stack), F32),
            pltpu.VMEM((total, stack), BF16),
            pltpu.VMEM((stack, total), BF16),
            pltpu.VMEM((stack, total), BF16),
            pltpu.VMEM((total, chunk), BF16),
            pltpu.VMEM((total, chunk), BF16),
            pltpu.VMEM((total, width), BF16),
        ],
    )(
        place, z2, *g_parts, u_up, sel, hid, big_second, big_second, *ad_second, *ad_second, up_row,
        b_down, a_up, down_bias[None], gain2,
    )

    def added(kept, sent):
        return (kept.astype(F32) + sent.astype(F32)).astype(BF16)

    quarter = part // 2

    def quarter_of(values, index):
        return lax.dynamic_slice_in_dim(values, index * quarter, quarter, 1)

    def side_sent(values):
        return move(quarter_of(values, 1 - side), sides_swap)

    early_sum = added(early_keep, move(early_send, cores))
    early_sum, ghb = tie(early_sum, ghb)
    early_sent = side_sent(early_sum)
    out_half = fixed((2, part, width))
    d_att, d_keep, d_send, out_keep, out_send = call(
        out_back_body,
        (2,),
        [
            SPOT, every, pl.BlockSpec((own_rows, half), lambda i: (0, i)), shared_rows,
            shared_rows, *pieces_out,
            pl.BlockSpec((1, stack, half), lambda i: (i, 0, 3)), fixed((stack, width)), thin, thin,
        ],
        [
            pl.BlockSpec((own_rows, half), lambda i: (0, i)), shared_rows, shared_rows, out_half,
            out_half,
        ],
        [
            struct((own_rows, width), BF16),
            half_rows,
            half_rows,
            struct((2, part, width), BF16),
            struct((2, part, width), BF16),
        ],
        scratch=[
            pltpu.VMEM((2, n_row, deep, half), BF16),
            pltpu.VMEM((total, stack), BF16),
            pltpu.VMEM((stack, total), BF16),
        ],
    )(place, ghb, att_own, att_keep, att_mate, *blocks1, ad_first, b_out, sel, u_out)

    d_mate = move(d_send, cores)
    out_sum = added(out_keep, move(out_send, cores))
    d_mate, out_sum = tie(d_mate, out_sum)
    out_sent = side_sent(out_sum)

    g_keep, g_send = call(
        functools.partial(attend_back_shared_body, scale),
        (heads // 4,),
        [pair_k, pair_k, head_p, pair_rows, pair_rows, pair_rows, pair_rows],
        [pair_k, pair_k],
        [shared_struct, shared_struct],
    )(qkv_keep, qkv_mate, p_sh, att_keep, att_send, d_keep, d_mate)
    early_sum = jnp.concatenate(
        [
            added(quarter_of(early_sum, side), early_sent),
            added(quarter_of(out_sum, side), out_sent),
        ],
        axis=2,
    )
    d_att, g_send, y_near, y_far, early_sum = tie(d_att, g_send, y_near, y_far, early_sum)
    early_sent = move(pick(early_sum, 1 - col), cols_swap)
    g_mate = move(g_send, cores)
    y_near, y_far = move(y_near, ring_back), move(y_far, cross)
    d_own = call(
        functools.partial(attend_back_body, scale),
        (heads // 2,),
        head_specs + [head_p, head_rows, head_rows],
        pl.BlockSpec((3, own_rows, 2 * HD), lambda h: (0, 0, h)),
        struct((3, own_rows, width), BF16),
    )(qkv, qkv, qkv, p_own, att_own, d_att)

    grad_spec = pl.BlockSpec((2, 2, 1, part, half), lambda k: (0, 0, k, 0, 0))
    grad_struct = struct((2, 2, 3, part, half), BF16)
    early_sum = added(pick(early_sum, col), early_sent)
    d_own, early_sum = tie(d_own, early_sum)
    early_sent = move(early_sum, far_swaps[0])
    e_qkv, q_kept, q_sent = call(
        qkv_grads_body,
        (3,),
        [SPOT, own_k, shared_k, shared_k, ad_k, thin, low_k, every],
        [low_k, grad_spec, grad_spec],
        [struct((total, 3 * stack), BF16), grad_struct, grad_struct],
    )(place, d_own, g_keep, g_mate, ad_first, sel, u_qkv, z1)

    def side_of(values, index):
        return jnp.where(index == 0, values[:, 0], values[:, 1])

    sums = added(q_kept, move(q_sent, cores)).reshape(2, 2, 3 * part, half)
    early_sum = added(early_sum, early_sent)
    sums, d_own, e_qkv, early_sum = tie(sums, d_own, e_qkv, early_sum)
    early_sent = move(early_sum, far_swaps[-1])
    q_sent = move(side_of(sums, 1 - side), sides_swap)
    t_own, t_near, t_far = call(
        qkv_back_body,
        (3,),
        [
            SPOT, own_three, shared_three, shared_three, *pieces0, *pieces1,
            fixed((width, 3 * stack)), low_block, rows_block, rows_block, vec,
        ],
        [third_rows, third_rows, third_rows],
        thirds,
        scratch=w_qkv_room,
    )(place, d_own, g_keep, g_mate, *blocks0, *blocks1, a_qkv, e_qkv, x, g_h, gain1)
    sums = added(side_of(sums, side), q_sent)
    early_sum = added(early_sum, early_sent)
    sums, t_near, t_far, y_near, y_far, early_sum = tie(
        sums, t_near, t_far, y_near, y_far, early_sum
    )
    q_sent = move(pick(sums, 1 - col), cols_swap)
    t_near, t_far = move(t_near, ring_back), move(t_far, cross)
    layer_out = join(y_own, y_near, y_far, BF16)
    edge = 2 * hidden_half
    whole = edge + 4 * half
    split_lanes = [slice(edge, edge + 2 * half), slice(edge + 3 * half, whole)]
    rest = jnp.concatenate([early_sum[:, lanes] for lanes in split_lanes], axis=1)
    early_sum = jnp.concatenate([early_sum, move(rest, cols_swap)], axis=1)
    q_sent, layer_out, early_sum = tie(q_sent, layer_out, early_sum)
    early_sent = move(early_sum, sides_swap)
    sums = added(pick(sums, col), q_sent)
    for pairs in far_swaps[:-1]:
        sums = added(sums, move(sums, pairs))
    q_sent = move(sums, far_swaps[-1])
    early_sum = ordered(early_sum, early_sent, side, 0)
    q_sent, t_near, t_far, early_sum = tie(q_sent, t_near, t_far, early_sum)
    early_sent = move(early_sum, cores)
    sums = added(sums, q_sent)
    sums = ordered(sums[None], move(sums, sides_swap)[None], side, 0)
    a_sent = move(sums[1:], cols_swap)
    tokens_grad = join(t_own, t_near, t_far, F32)
    mine = ordered(early_sum, early_sent, core, 0).astype(F32)
    a_sent, tokens_grad, mine = tie(a_sent, tokens_grad, mine)
    every_sum = jnp.concatenate([sums[:1], ordered(sums[1:], a_sent, col, 0)])
    every_sum = every_sum.reshape(3, 3, part, half)
    every_sum = ordered(every_sum, move(every_sum, cores), core, 2).reshape(3, 3 * stack, half)
    b_sum = every_sum[0].reshape(3, stack, half).astype(F32)
    a_sum = jnp.concatenate([every_sum[1].T, every_sum[2].T]).astype(F32)

    own_starts = (edge, edge + half, edge + 3 * half)
    a_up_sum, b_down_sum, b_out_sum = (
        ordered(
            mine[:, start : start + half],
            mine[:, whole + i * half : whole + (i + 1) * half],
            col,
            1,
        )
        for i, start in enumerate(own_starts)
    )
    return (
        layer_out,
        tokens_grad,
        a_sum,
        b_sum,
        mine[:, edge + 2 * half : edge + 3 * half].T,
        b_out_sum,
        a_up_sum.T,
        mine[:, :hidden_half],
        mine[:, hidden_half:edge].T,
        b_down_sum,
    )


def solution(mesh):
    placed = (
        P("row", "col"),
        P("row", "col"),
        P(),
        P(),
        P(),
        P(),
        P(None, "row", "col"),
        P(None, "col"),
        P("col", "row"),
        P(),
        P("row", "col"),
        P("col"),
        P("col", "row"),
        P(),
        P("row"),
        P(),
        P(None, None, "col"),
        P("col", None),
        P(),
        P(),
        P(None, "col"),
        P("col", None),
        P(),
    )
    shape = (mesh.shape["row"], mesh.shape["col"])
    paired = shape[1] == 2 and shape[0] >= 16 and shape[0] & (shape[0] - 1) == 0
    return jax.shard_map(
        functools.partial(on_chip_pair, shape) if paired else on_device,
        mesh=mesh,
        in_specs=placed,
        out_specs=(
            P("row", "col"),
            P("row", "col"),
            P(),
            P(None, None, "col"),
            P("col", None),
            P(),
            P(),
            P(None, "col"),
            P("col", None),
            P(),
        ),
        check_vma=False,
    )
```

```python
import functools

import jax
import jax.numpy as jnp
from jax import lax
from jax.experimental import pallas as pl
from jax.experimental.pallas import tpu as pltpu
from jax.sharding import PartitionSpec as P

HD = 64
RANK = 16


EPS = 1e-05
GELU_SCALE = 1.702


def column_sums(first, second):
    return lax.psum((first, second), "col")


def gather_features(values):
    return lax.all_gather(values, "col", axis=1, tiled=True)


def sum_partials(terms):
    return lax.psum_scatter(
        terms.astype(jnp.bfloat16), "col", scatter_dimension=1, tiled=True
    ).astype(jnp.float32)


def norm_split(values, feature_width):
    first, second = column_sums(jnp.sum(values, axis=1), jnp.sum(values * values, axis=1))
    centre = first / feature_width
    inverse = lax.rsqrt(second / feature_width - centre * centre + EPS)
    return ((values - centre[:, None]) * inverse[:, None], inverse)


def norm_back(grad_normed, normal_rows, inverse, gain_part, feature_width):
    scaled = grad_normed * gain_part
    first, second = column_sums(jnp.sum(scaled, axis=1), jnp.sum(scaled * normal_rows, axis=1))
    return inverse[:, None] * (
        scaled - first[:, None] / feature_width - normal_rows * second[:, None] / feature_width
    )


def select_rows(low_rank, onehot, image_len):
    image_count, stack_width = onehot.shape
    shaped = low_rank.reshape(image_count, image_len, -1, stack_width)
    return (shaped * onehot[:, None, None, :]).reshape(low_rank.shape).astype(jnp.bfloat16)


def mult(form, first, second):
    return jnp.einsum(form, first, second, preferred_element_type=jnp.float32)


def on_device(
    tokens,
    cotangent,
    ln1_gain,
    ln1_bias,
    ln2_gain,
    ln2_bias,
    w_qkv,
    qv_bias,
    w_out,
    out_bias,
    w_up,
    up_bias,
    w_down,
    down_bias,
    adapter_ids,
    a_qkv,
    b_qkv,
    a_out,
    b_out,
    a_up,
    b_up,
    a_down,
    b_down,
):
    row_count, part_width = tokens.shape
    feature_width = a_qkv.shape[0]
    stack_width = a_qkv.shape[1] // 3
    image_count = adapter_ids.shape[0]
    image_len = row_count // image_count
    head_count = part_width // HD
    scale = HD ** (-0.5)
    offset = lax.axis_index("col") * part_width

    def own_part(values, axis):
        return lax.dynamic_slice_in_dim(values, offset, part_width, axis)

    owners = lax.iota(jnp.int32, stack_width) // RANK
    onehot = (adapter_ids[:, None] == owners[None, :]).astype(jnp.float32)
    wide_qkv, wide_out, wide_up, wide_down = (
        lax.all_gather(w_qkv, "row", axis=1, tiled=True),
        lax.all_gather(w_out, "row", axis=1, tiled=True),
        lax.all_gather(w_up, "row", axis=0, tiled=True),
        lax.all_gather(w_down, "row", axis=1, tiled=True),
    )
    inputs = tokens.astype(jnp.float32)
    normal_one, inverse_one = norm_split(inputs, feature_width)
    normed_part = (normal_one * own_part(ln1_gain, 0) + own_part(ln1_bias, 0)).astype(jnp.bfloat16)
    normed_one = gather_features(normed_part)
    projected = mult("td,kde->kte", normed_one, wide_qkv)
    kept_qkv = select_rows(mult("td,dj->tj", normed_one, a_qkv), onehot, image_len)
    projected = projected + mult("tkj,kje->kte", kept_qkv.reshape(row_count, 3, stack_width), b_qkv)
    bias_rows = jnp.stack([qv_bias[0], jnp.zeros_like(qv_bias[0]), qv_bias[1]])[:, None, :]
    qkv = (projected + bias_rows).astype(jnp.bfloat16)
    shaped = qkv.reshape(3, image_count, image_len, head_count, HD)
    queries, key_rows, value_rows = (shaped[0], shaped[1], shaped[2])
    scores = mult("bqhd,bkhd->bhqk", queries, key_rows) * scale
    highest = jnp.max(scores, axis=-1, keepdims=True)
    log_total = highest + jnp.log(jnp.sum(jnp.exp(scores - highest), axis=-1, keepdims=True))
    weights_low = jnp.exp(scores - log_total).astype(jnp.bfloat16)
    attended = mult("bhqk,bkhd->bqhd", weights_low, value_rows)
    attended = attended.reshape(row_count, part_width).astype(jnp.bfloat16)
    kept_out = select_rows(mult("tc,cj->tj", attended, a_out), onehot, image_len)
    out_terms = mult("tc,cd->td", attended, wide_out) + mult("tj,jd->td", kept_out, b_out)
    hidden = inputs + sum_partials(out_terms) + own_part(out_bias, 0)
    normal_two, inverse_two = norm_split(hidden, feature_width)
    normed_part_two = (normal_two * own_part(ln2_gain, 0) + own_part(ln2_bias, 0)).astype(
        jnp.bfloat16
    )
    normed_two = gather_features(normed_part_two)
    kept_up = select_rows(mult("td,dj->tj", normed_two, a_up), onehot, image_len)
    pre_up = mult("td,df->tf", normed_two, wide_up) + mult("tj,jf->tf", kept_up, b_up) + up_bias
    logistic = jax.nn.sigmoid(GELU_SCALE * pre_up)
    activated = (pre_up * logistic).astype(jnp.bfloat16)
    kept_down = select_rows(mult("tf,fj->tj", activated, a_down), onehot, image_len)
    down_terms = mult("tf,fd->td", activated, wide_down) + mult("tj,jd->td", kept_down, b_down)
    layer_out = (hidden + sum_partials(down_terms) + own_part(down_bias, 0)).astype(jnp.bfloat16)
    wide_qkv, wide_out, wide_up, wide_down = (
        lax.all_gather(w_qkv, "row", axis=1, tiled=True),
        lax.all_gather(w_out, "row", axis=1, tiled=True),
        lax.all_gather(w_up, "row", axis=0, tiled=True),
        lax.all_gather(w_down, "row", axis=1, tiled=True),
    )
    grad_layer = cotangent.astype(jnp.float32)
    grad_full = gather_features(cotangent)
    d_low_down = select_rows(mult("td,jd->tj", grad_full, b_down), onehot, image_len)
    d_activated = mult("td,fd->tf", grad_full, wide_down) + mult("tj,fj->tf", d_low_down, a_down)
    grad_b_down = mult("tj,td->jd", kept_down, grad_full)
    grad_a_down = mult("tf,tj->fj", activated, d_low_down)
    d_pre_up = (
        d_activated * (logistic + GELU_SCALE * pre_up * logistic * (1.0 - logistic))
    ).astype(jnp.bfloat16)
    d_low_up = select_rows(mult("tf,jf->tj", d_pre_up, b_up), onehot, image_len)
    grad_b_up = mult("tj,tf->jf", kept_up, d_pre_up)
    grad_a_up = mult("td,tj->dj", normed_two, d_low_up)
    normed_two_terms = mult("tf,df->td", d_pre_up, wide_up) + mult("tj,dj->td", d_low_up, a_up)
    d_normed_two = sum_partials(normed_two_terms)
    grad_hidden = grad_layer + norm_back(
        d_normed_two, normal_two, inverse_two, own_part(ln2_gain, 0), feature_width
    )
    hidden_full_grad = gather_features(grad_hidden.astype(jnp.bfloat16))
    d_low_out = select_rows(mult("td,jd->tj", hidden_full_grad, b_out), onehot, image_len)
    d_attended = mult("td,cd->tc", hidden_full_grad, wide_out) + mult("tj,cj->tc", d_low_out, a_out)
    grad_b_out = mult("tj,td->jd", kept_out, hidden_full_grad)
    grad_a_out = mult("tc,tj->cj", attended, d_low_out)
    d_heads = d_attended.astype(jnp.bfloat16).reshape(image_count, image_len, head_count, HD)
    scores_again = mult("bqhd,bkhd->bhqk", queries, key_rows) * scale
    weights_again = jnp.exp(scores_again - log_total)
    weights_again_low = weights_again.astype(jnp.bfloat16)
    d_weights = mult("bqhd,bkhd->bhqk", d_heads, value_rows)
    d_values = mult("bhqk,bqhd->bkhd", weights_again_low, d_heads)
    d_scores = weights_again * (
        d_weights - jnp.sum(weights_again * d_weights, axis=-1, keepdims=True)
    )
    d_scores = d_scores.astype(jnp.bfloat16)
    d_queries = scale * mult("bhqk,bkhd->bqhd", d_scores, key_rows)
    d_keys = scale * mult("bhqk,bqhd->bkhd", d_scores, queries)
    d_qkv = (
        jnp.stack([d_queries, d_keys, d_values])
        .reshape(3, row_count, part_width)
        .astype(jnp.bfloat16)
    )
    d_low_qkv = mult("kte,kje->tkj", d_qkv, b_qkv)
    d_low_qkv = select_rows(d_low_qkv.reshape(row_count, 3 * stack_width), onehot, image_len)
    grad_b_qkv = mult("tkj,kte->kje", kept_qkv.reshape(row_count, 3, stack_width), d_qkv)
    grad_a_qkv = mult("td,tj->dj", normed_one, d_low_qkv)
    normed_one_terms = mult("kte,kde->td", d_qkv, wide_qkv) + mult("tj,dj->td", d_low_qkv, a_qkv)
    d_normed_one = sum_partials(normed_one_terms)
    tokens_grad = grad_hidden + norm_back(
        d_normed_one, normal_one, inverse_one, own_part(ln1_gain, 0), feature_width
    )
    grad_a_qkv, grad_b_out, grad_a_up, grad_b_down = lax.psum(
        (grad_a_qkv, grad_b_out, grad_a_up, grad_b_down), ("row", "col")
    )
    grad_b_qkv, grad_a_out, grad_b_up, grad_a_down = (
        lax.psum(grad_b_qkv.astype(jnp.bfloat16), "row").astype(jnp.float32),
        lax.psum(grad_a_out.astype(jnp.bfloat16), "row").astype(jnp.float32),
        lax.psum(grad_b_up.astype(jnp.bfloat16), "row").astype(jnp.float32),
        lax.psum(grad_a_down.astype(jnp.bfloat16), "row").astype(jnp.float32),
    )
    return (
        layer_out,
        tokens_grad,
        grad_a_qkv,
        grad_b_qkv,
        grad_a_out,
        grad_b_out,
        grad_a_up,
        grad_b_up,
        grad_a_down,
        grad_b_down,
    )


NT = (((1,), (1,)), ((), ()))
NN = (((1,), (0,)), ((), ()))
F32 = jnp.float32
BF16 = jnp.bfloat16
VMEM_LIMIT = 60 * 1024 * 1024
SPOT = pl.BlockSpec(memory_space=pltpu.SMEM)


def dot(first, second, dims=NN):
    return lax.dot_general(first, second, dims, preferred_element_type=F32)


def dot_rows(first, second):
    return dot(first.T, second)


def call(body, grid, in_specs, out_specs, out_shape, scratch=()):
    return pl.pallas_call(
        body,
        grid=grid,
        in_specs=in_specs,
        out_specs=out_specs,
        out_shape=out_shape,
        scratch_shapes=list(scratch),
        compiler_params=pltpu.CompilerParams(
            dimension_semantics=("arbitrary",) * len(grid), vmem_limit_bytes=VMEM_LIMIT
        ),
    )


def fixed(shape):
    zeros = (0,) * len(shape)
    return pl.BlockSpec(shape, lambda *_: zeros, pipeline_mode=pl.Buffered(1))


def struct(shape, kind):
    return jax.ShapeDtypeStruct(shape, kind)


def norm_of(values):
    centred = values - jnp.mean(values, axis=1, keepdims=True)
    inverse = lax.rsqrt(jnp.mean(centred * centred, axis=1, keepdims=True) + EPS)
    return centred * inverse, inverse


def norm_pull(grad, normal, inverse, gain):
    scaled = grad * gain
    return inverse * (
        scaled
        - jnp.mean(scaled, axis=1, keepdims=True)
        - normal * jnp.mean(scaled * normal, axis=1, keepdims=True)
    )


def settle(place, pieces, side_first, store):
    depth = pieces[0].shape[0]
    n_far = depth // 2
    for group, piece in enumerate(pieces):
        for index in range(depth):
            other, outer, inner, back = (
                group // 2, group % 2, index // n_far, index % n_far
            )
            x_off, y_off = (outer, inner) if side_first else (inner, outer)
            far = lax.rem(place[0] + (n_far - back), n_far)
            x = place[1] if x_off == 0 else 1 - place[1]
            core = place[2] if other == 0 else 1 - place[2]
            y = place[3] if y_off == 0 else 1 - place[3]
            store(far * 4 + x * 2 + core, y, piece[index])


def settle_qkv(place, pieces0, pieces1, w_ref):
    half = pieces1[0].shape[2]

    def lanes(y):
        return pl.ds(pl.multiple_of(y * half, half), half)

    def first(row, y, block):
        w_ref[0, row, :, lanes(y)] = block[:, :half]
        w_ref[1, row, :, lanes(y)] = block[:, half:]

    def last(row, y, block):
        w_ref[2, row, :, lanes(y)] = block

    settle(place, pieces0, False, first)
    settle(place, pieces1, True, last)


def settle_out(place, pieces1, w_ref):
    half = pieces1[0].shape[2]

    def store(row, y, block):
        w_ref[row, :, pl.ds(pl.multiple_of(y * half, half), half)] = block

    settle(place, pieces1, True, store)


def chosen(index, first, second):
    return jnp.where(index == 0, first, second)


def both_halves(place, own, near, far):
    diagonal = place[2] == place[3]
    mine = jnp.where(diagonal, own, near)
    other = jnp.where(diagonal, near, far)
    return chosen(place[3], mine, other), chosen(place[3], other, mine)


def halves_out(place, values, rows, own_ref, near_ref, far_ref):
    half = values.shape[1] // 2
    left, right = values[:, :half], values[:, half:]
    mine, other = chosen(place[3], left, right), chosen(place[3], right, left)
    own_ref[rows, :] = mine
    near_ref[rows, :] = jnp.where(place[2] == place[3], other, mine)
    far_ref[rows, :] = other


def spread_body(length, cut, own_rows, tb, place, t_ref, own_ref, near_ref, far_ref, wide_ref):
    wide_ref[...] = t_ref[...].astype(F32)

    def put(ref, start, shared, shared_count):
        ref[:length, :] = wide_ref[start : start + length, :].astype(BF16)
        ref[own_rows : own_rows + shared_count, :] = wide_ref[
            shared : shared + shared_count, :
        ].astype(BF16)

    for ref, index in ((own_ref, place[2]), (near_ref, 1 - place[3]), (far_ref, 1 - place[2])):
        ref[...] = jnp.zeros_like(ref)

        @pl.when(index == 0)
        def _():
            put(ref, 0, length, cut)

        @pl.when(index == 1)
        def _():
            put(ref, 2 * length, length + cut, length - cut)


def join_body(length, cut, own_rows, pieces, place, *refs):
    *in_refs, out_ref, wide_ref = refs

    def whole(part):
        found = [ref[...] for ref in in_refs[part * pieces : (part + 1) * pieces]]
        return found[0] if pieces == 1 else jnp.concatenate(found)

    own, near, far = whole(0), whole(1), whole(2)
    diagonal = place[2] == place[3]
    mine = jnp.where(diagonal, own, near)
    mate = jnp.where(diagonal, near, far)
    first = chosen(place[2], mine, mate).astype(F32)
    second = chosen(place[2], mate, mine).astype(F32)
    wide_ref[:length, :] = first[:length]
    wide_ref[length : length + cut, :] = first[own_rows : own_rows + cut]
    wide_ref[length + cut : 2 * length, :] = second[own_rows : own_rows + length - cut]
    wide_ref[2 * length :, :] = second[:length]
    out_ref[...] = wide_ref[...].astype(out_ref.dtype)


def qkv_body(
    scale, place, own_ref, near_ref, far_ref, gain, bias, p0, p1, p2, p3, r0, r1, r2, r3, a_ref,
    b_ref, qv_ref, sel_ref, x_ref, z_ref, u_ref, out_ref, keep_out, send_out, w_ref,
):
    width = x_ref.shape[1]
    half = width // 2
    stack = sel_ref.shape[1]

    @pl.when(pl.program_id(0) == 0)
    def _():
        settle_qkv(place, (p0, p1, p2, p3), (r0, r1, r2, r3), w_ref)

    left, right = both_halves(place, own_ref[...], near_ref[...], far_ref[...])
    x = jnp.concatenate([left, right], axis=1)
    x_ref[...] = x
    normal, _ = norm_of(x.astype(F32))
    z = (normal * gain[...] + bias[...]).astype(BF16)
    z_ref[...] = z
    low = dot(z, a_ref[...])
    for k in range(3):
        kept = (low[:, k * stack : (k + 1) * stack] * sel_ref[...]).astype(BF16)
        u_ref[:, k * stack : (k + 1) * stack] = kept
        w = w_ref[k].reshape(width, width)
        parts = []
        for y in range(2):
            lanes = slice(y * half, (y + 1) * half)
            acc = dot(z, w[:, lanes]) + dot(kept, b_ref[y, :, k * half : (k + 1) * half])
            out = (acc + qv_ref[k, :, lanes]).astype(BF16)
            if k == 0:
                out = out * jnp.asarray(scale, BF16)
            out_ref[k, :, lanes] = out
            parts.append(out)
        keep_out[k] = chosen(place[2], parts[0], parts[1])
        send_out[k] = chosen(place[2], parts[1], parts[0])


def attend_pairs(pairs, mask, p_ref):
    lane = lax.broadcasted_iota(jnp.int32, mask.shape, 1)
    one, zero = jnp.ones_like(mask), jnp.zeros_like(mask)
    work = []
    for q, k, v in pairs:
        for spare, here in ((HD, lane < HD), (0, lane >= HD)):
            mine = jnp.where(here, q, jnp.where(lane == spare, one, zero))
            work.append((mine, jnp.where(lane == spare, mask, k), v))
    scores, parts = [dot(work[0][0], work[0][1], NT)], []
    for i, (_, _, v) in enumerate(work):
        if i + 1 < len(work):
            scores.append(dot(work[i + 1][0], work[i + 1][1], NT))
        s = scores[i]
        e = jnp.exp(s - jnp.max(s, axis=1, keepdims=True))
        p = (e * (1.0 / jnp.sum(e, axis=1, keepdims=True))).astype(BF16)
        p_ref[i] = p
        parts.append(dot(p, v))
    return [
        jnp.where(lane < HD, parts[i], parts[i + 1]).astype(BF16) for i in range(0, len(parts), 2)
    ]


def pair_lanes(ref):
    return [slice(i, i + 2 * HD) for i in range(0, ref.shape[-1], 2 * HD)]


def attend_body(q_ref, k_ref, v_ref, mask_ref, out_ref, p_ref):
    lanes = pair_lanes(out_ref)
    pairs = [(q_ref[0, :, at], k_ref[0, :, at], v_ref[0, :, at]) for at in lanes]
    for at, out in zip(lanes, attend_pairs(pairs, mask_ref[...], p_ref)):
        out_ref[:, at] = out


def attend_shared_body(mine_ref, mate_ref, mask_ref, keep_ref, send_ref, p_ref):
    lanes = pair_lanes(keep_ref)
    pairs = [
        [jnp.concatenate([mine_ref[i, :, at], mate_ref[i, :, at]]) for i in range(3)]
        for at in lanes
    ]
    count = keep_ref.shape[0]
    for at, out in zip(lanes, attend_pairs(pairs, mask_ref[...], p_ref)):
        keep_ref[:, at] = out[:count]
        send_ref[:, at] = out[count:]


def attend_back_one(scale, q, k, v, p_ref, att, do):
    low_lanes = lax.broadcasted_iota(jnp.int32, q.shape, 1) < HD
    zero = jnp.zeros_like(q)
    product = att.astype(F32) * do.astype(F32)
    dq = dk = dv = 0.0
    for head in range(2):
        here = low_lanes if head == 0 else ~low_lanes
        my_q, my_k, my_do = (jnp.where(here, t, zero) for t in (q, k, do))
        delta = jnp.sum(jnp.where(here, product, 0.0), axis=1, keepdims=True)
        p = p_ref[head]
        dp = dot(my_do, v, NT)
        ds = (p.astype(F32) * (dp - delta)).astype(BF16)
        dq = dq + dot(ds, my_k)
        dk = dk + dot(ds, my_q, (((0,), (0,)), ((), ())))
        dv = dv + dot(p, my_do, (((0,), (0,)), ((), ())))
    return (dq * scale).astype(BF16), dk.astype(BF16), dv.astype(BF16)


def attend_back_body(scale, q_ref, k_ref, v_ref, p_ref, att_ref, do_ref, out_ref):
    parts = attend_back_one(
        scale, q_ref[0], k_ref[0], v_ref[0], p_ref, att_ref[...], do_ref[...]
    )
    for i in range(3):
        out_ref[i] = parts[i]


def attend_back_shared_body(
    scale, mine_ref, mate_ref, p_ref, att_keep, att_send, do_keep, do_mate, keep_ref, send_ref
):
    q, k, v = (jnp.concatenate([mine_ref[i], mate_ref[i]]) for i in range(3))
    att = jnp.concatenate([att_keep[...], att_send[...]])
    do = jnp.concatenate([do_keep[...], do_mate[...]])
    parts = attend_back_one(scale, q, k, v, p_ref, att, do)
    count = keep_ref.shape[1]
    for i in range(3):
        keep_ref[i] = parts[i][:count]
        send_ref[i] = parts[i][count:]


def out_body(
    place, own_ref, keep_ref, mate_ref, x_ref, r0, r1, r2, r3, a_ref, b_ref, bias_ref, gain,
    lbias, aup_ref, sel_ref, hid_ref, z_ref, u_ref, uup_ref, w_ref,
):
    width = x_ref.shape[1]
    half = width // 2

    @pl.when(pl.program_id(0) == 0)
    def _():
        settle_out(place, (r0, r1, r2, r3), w_ref)

    keep, mate = keep_ref[...], mate_ref[...]
    shared = jnp.concatenate(
        [chosen(place[2], keep, mate), chosen(place[2], mate, keep)], axis=1
    )
    att = jnp.where(pl.program_id(0) < 2, own_ref[...], shared)
    sel = sel_ref[...]
    low = dot(att[:, :half], a_ref[0], NT) + dot(att[:, half:], a_ref[1], NT)
    kept = (low * sel).astype(BF16)
    u_ref[...] = kept
    acc = dot(att, w_ref[...].reshape(width, width), NT) + dot(kept, b_ref[...])
    hidden = x_ref[...].astype(F32) + acc + bias_ref[...]
    hid_ref[...] = hidden
    normal, _ = norm_of(hidden)
    z = (normal * gain[...] + lbias[...]).astype(BF16)
    z_ref[...] = z
    uup_ref[...] = (dot(z, aup_ref[...]) * sel).astype(BF16)


def mlp_body(
    rows, place, z_ref, gown_ref, gnear_ref, gfar_ref, uup_ref, sel_ref, hid_ref, wup_ref,
    wdn_ref, bup_own, bup_near, bup_far, adn_own, adn_near, adn_far, upb_ref, bdn_ref, aup_ref,
    dnb_ref, gain,
    own_ref, near_ref, far_ref, ghb_ref, ekeep_ref, esend_ref,
    down_acc, dz_acc, udn_acc, eup_acc, edn_ref, uup_t, edn_t, act_ref, dup_ref, gy_ref, hid_buf,
    hid_sem,
):
    total, width = z_ref.shape
    step = pl.program_id(0)
    blocks = [slice(i, i + rows) for i in range(0, total, rows)]

    fetch = pltpu.make_async_copy(hid_ref, hid_buf, hid_sem)

    @pl.when(step == 0)
    def _():
        fetch.start()
        for b in blocks:
            left, right = both_halves(place, gown_ref[b, :], gnear_ref[b, :], gfar_ref[b, :])
            gy = jnp.concatenate([left, right], axis=1)
            gy_ref[b, :] = gy
            edn_ref[b, :] = (dot(gy, bdn_ref[...], NT) * sel_ref[b, :]).astype(BF16)
        edn_t[...] = edn_ref[...].T
        uup_t[...] = uup_ref[...].T
        down_acc[...] = jnp.zeros_like(down_acc)
        dz_acc[...] = jnp.zeros_like(dz_acc)
        udn_acc[...] = jnp.zeros_like(udn_acc)
        eup_acc[...] = jnp.zeros_like(eup_acc)

    chunk = upb_ref.shape[1]
    wup = wup_ref[...].reshape(width, chunk)
    wdn = wdn_ref[...].reshape(width, chunk)
    parts = pl.num_programs(0) // 2
    y = step // parts

    def adapter(own_ref, near_ref, far_ref):
        near, far = near_ref[...], far_ref[...]
        other = jnp.concatenate([chosen(place[2], near, far), chosen(place[2], far, near)])
        return jnp.where(place[3] == y, own_ref[...], other)

    bup = adapter(bup_own, bup_near, bup_far)
    adn = adapter(adn_own, adn_near, adn_far)
    for b in blocks:
        pre = dot(z_ref[b, :], wup) + dot(uup_ref[b, :], bup) + upb_ref[...]
        q = 1.0 / (1.0 + jnp.exp(-GELU_SCALE * pre))
        act = (pre * q).astype(BF16)
        d_act = dot(gy_ref[b, :], wdn) + dot(edn_ref[b, :], adn)
        d_up = (d_act * (q + GELU_SCALE * pre * q * (1.0 - q))).astype(BF16)
        act_ref[b, :] = act
        dup_ref[b, :] = d_up
        down_acc[b, :] += dot(act, wdn, NT)
        dz_acc[b, :] += dot(d_up, wup, NT)
        udn_acc[b, :] += dot(act, adn, NT)
        eup_acc[b, :] += dot(d_up, bup, NT)
    hidden_half = parts * chunk
    for i, (low, high) in enumerate(((uup_t, dup_ref), (edn_t, act_ref))):
        rows = split_rows(place, dot(low[...], high[...]).astype(BF16))
        lanes = pl.ds(pl.multiple_of(i * hidden_half + step % parts * chunk, chunk), chunk)
        ekeep_ref[y, :, lanes], esend_ref[y, :, lanes] = rows

    @pl.when(step == pl.num_programs(0) - 1)
    def _():
        fetch.wait()
        gbdn = gaup = 0.0
        for b in blocks:
            sel = sel_ref[b, :]
            e_up = (eup_acc[b, :] * sel).astype(BF16)
            u_dn = (udn_acc[b, :] * sel).astype(BF16)
            hidden = hid_buf[b, :]
            y = hidden + down_acc[b, :] + dot(u_dn, bdn_ref[...]) + dnb_ref[...]
            halves_out(place, y.astype(BF16), b, own_ref, near_ref, far_ref)
            dz = dz_acc[b, :] + dot(e_up, aup_ref[...], NT)
            normal, inverse = norm_of(hidden)
            grad = gy_ref[b, :].astype(F32) + norm_pull(dz, normal, inverse, gain[...])
            ghb_ref[b, :] = grad.astype(BF16)
            gbdn = gbdn + dot_rows(u_dn, gy_ref[b, :])
            gaup = gaup + dot_rows(e_up, z_ref[b, :])
        half = width // 2
        for i, grad in enumerate((gaup, gbdn)):
            start = 2 * hidden_half + i * half
            for column in range(2):
                rows = split_rows(place, grad[:, column * half : (column + 1) * half].astype(BF16))
                lanes = slice(start, start + half)
                ekeep_ref[column, :, lanes], esend_ref[column, :, lanes] = rows


def split_rows(place, grad):
    part = grad.shape[0] // 2
    low, high = grad[:part], grad[part:]
    return chosen(place[2], low, high), chosen(place[2], high, low)


def out_back_body(
    place, g_ref, own_ref, keep_ref, mate_ref, r0, r1, r2, r3, a_ref, b_ref, sel_ref, u_ref,
    d_own, d_keep, d_send, g_keep, g_send, w_ref, e_ref, e_t,
):
    width = g_ref.shape[1]
    half = width // 2
    count = keep_ref.shape[0]
    y = pl.program_id(0)

    @pl.when(y == 0)
    def _():
        def store(row, column, block):
            w_ref[column, row] = block

        settle(place, (r0, r1, r2, r3), True, store)
        e = (dot(g_ref[...], b_ref[...], NT) * sel_ref[...]).astype(BF16)
        e_ref[...] = e
        e_t[...] = e.T
        gb = dot(u_ref[...].T, g_ref[...]).astype(BF16)
        for column in range(2):
            rows = split_rows(place, gb[:, column * half : (column + 1) * half])
            g_keep[column, :, half:], g_send[column, :, half:] = rows

    w = w_ref[y].reshape(width, half)
    d = (dot(g_ref[...], w) + dot(e_ref[...], a_ref[0])).astype(BF16)
    d_own[...] = d[: 2 * count]

    shared = jnp.where(place[2] == y, keep_ref[...], mate_ref[...])
    ga = dot(e_t[...], jnp.concatenate([own_ref[...], shared])).astype(BF16)
    g_keep[y, :, :half], g_send[y, :, :half] = split_rows(place, ga)

    @pl.when(place[2] == y)
    def _():
        d_keep[...] = d[2 * count :]

    @pl.when(place[2] != y)
    def _():
        d_send[...] = d[2 * count :]


def shared_halves(place, keep, mate):
    return chosen(place[2], keep, mate), chosen(place[2], mate, keep)


def qkv_grads_body(
    place, left_ref, right_ref, keep_ref, mate_ref, b_ref, sel_ref, u_ref, z_ref, e_ref,
    keep_out, send_out,
):
    half = left_ref.shape[2]
    part = sel_ref.shape[1] // 2
    shared = shared_halves(place, keep_ref[0], mate_ref[0])
    u_t = u_ref[...].T

    def put(grad, y, i):
        low, high = grad[:part], grad[part:]
        keep_out[y, i, 0] = chosen(place[2], low, high)
        send_out[y, i, 0] = chosen(place[2], high, low)

    low = 0.0
    for y, own_ref in enumerate((left_ref, right_ref)):
        d = jnp.concatenate([own_ref[0], shared[y]])
        low = low + dot(d, b_ref[y], NT)
        put(dot(u_t, d).astype(BF16), y, 0)
    e = (low * sel_ref[...]).astype(BF16)
    e_ref[...] = e
    ga = dot(e.T, z_ref[...]).astype(BF16)
    for y in range(2):
        put(ga[:, y * half : (y + 1) * half], y, 1)


def qkv_back_body(
    shared, place, left_ref, right_ref, p0, p1, p2, p3, r0, r1, r2, r3, a_ref, e_ref, x_ref,
    gh_ref, gain, own_out, near_out, far_out, w_ref,
):
    width = x_ref.shape[1]
    settle_qkv(place, (p0, p1, p2, p3), (r0, r1, r2, r3), w_ref)
    dz = dot(e_ref[...], a_ref[...], NT)
    for k in range(3):
        left, right = left_ref[k], right_ref[k]
        if shared:
            left, right = shared_halves(place, left, right)
        d = jnp.concatenate([left, right], axis=1)
        dz = dz + dot(d, w_ref[k].reshape(width, width), NT)
    normal, inverse = norm_of(x_ref[...].astype(F32))
    grad = gh_ref[...].astype(F32) + norm_pull(dz, normal, inverse, gain[...])
    halves_out(place, grad.astype(BF16), slice(None), own_out, near_out, far_out)


def on_chip_pair(
    mesh_shape, tokens, cotangent, ln1_gain, ln1_bias, ln2_gain, ln2_bias, w_qkv, qv_bias, w_out,
    out_bias, w_up, up_bias, w_down, down_bias, adapter_ids, a_qkv, b_qkv, a_out, b_out, a_up,
    b_up, a_down, b_down,
):
    n_row, n_col = mesh_shape
    count, half = tokens.shape
    width = half * 2
    stack = b_out.shape[0]
    part = stack // 2
    hidden_half = w_up.shape[1]
    hidden = hidden_half * 2
    length = count // adapter_ids.shape[0]
    cut = length // 2
    heads = width // HD
    tb = -(-(length + 1) // 32) * 16
    own_rows, total = 2 * tb, 3 * tb
    scale = HD ** (-0.5)
    both = ("row", "col")
    row, col = lax.axis_index("row"), lax.axis_index("col")
    core, side, n_far = row % 2, row // 2 % 2, n_row // 4
    place = jnp.stack([row // 4, side, core, col]).astype(jnp.int32)

    def device(r, c):
        return r * n_col + c

    far_swaps = [[] for _ in range(n_far.bit_length() - 1)]
    far_turns = [[] for _ in range(n_far - 1)]
    ring_in, ring_back, cross, cores, cols_swap, sides_swap = [], [], [], [], [], []
    for r in range(n_row):
        for c in range(n_col):
            k, mate = r % 2, r + 1 - 2 * (r % 2)
            cores.append((device(r, c), device(mate, c)))
            cols_swap.append((device(r, c), device(r, 1 - c)))
            sides_swap.append((device(r, c), device(r ^ 2, c)))
            for turn, pairs in enumerate(far_turns):
                pairs.append((device(r, c), device((r + 4 * (turn + 1)) % n_row, c)))
            for bit, pairs in enumerate(far_swaps):
                pairs.append((device(r, c), device(r ^ (4 << bit), c)))
            if k != c:
                ring_in.append((device(r, c), device(r, 1 - c)))
                ring_back.append((device(r, c), device(mate, c)))
                cross.append((device(r, c), device(mate, 1 - c)))
            else:
                ring_in.append((device(r, c), device(mate, c)))
                ring_back.append((device(r, c), device(r, 1 - c)))

    def move(values, pairs):
        return lax.ppermute(values, both, pairs)

    def pick(pair, index):
        return jnp.where(index == 0, pair[0], pair[1])

    def ordered(mine, other, index, axis):
        return jnp.where(
            index == 0,
            jnp.concatenate([mine, other], axis),
            jnp.concatenate([other, mine], axis),
        )

    def tie(*values):
        return lax.optimization_barrier(values)

    thirds = [struct((total, half), BF16)] * 3
    third_specs = [fixed((total, half))] * 3

    def spread(values):
        return call(
            functools.partial(spread_body, length, cut, own_rows, tb),
            (1,),
            [SPOT, fixed((count, half))],
            third_specs,
            thirds,
            scratch=[pltpu.VMEM((count, half), F32)],
        )(place, values)

    def join(own, near, far, kind):
        return call(
            functools.partial(join_body, length, cut, own_rows, len(own)),
            (1,),
            [SPOT] + [fixed(t.shape) for t in (*own, *near, *far)],
            fixed((count, half)),
            struct((count, half), kind),
            scratch=[pltpu.VMEM((count, half), F32)],
        )(place, *own, *near, *far)

    x_own, x_near, x_far = spread(tokens)
    x_near, x_far, w_qkv, w_out = tie(x_near, x_far, w_qkv, w_out)
    mine_first = jnp.concatenate(
        [jnp.swapaxes(w_qkv, 0, 1).reshape(-1, 3 * half), w_out.T], axis=1
    )
    mine_second = jnp.concatenate([w_up, w_down.T], axis=1)
    adapt_first = jnp.concatenate(
        [jnp.swapaxes(b_qkv, 0, 1).reshape(stack, 3 * half), a_out.T], axis=1
    )
    adapt_second = jnp.concatenate([b_up, a_down.T], axis=1)
    deep = width // n_row

    def turned(block):
        return jnp.stack([block] + [move(block, pairs) for pairs in far_turns])

    def doubled(found, pairs):
        return jnp.concatenate([found, move(found, pairs)])

    def part_of(values):
        return lax.dynamic_slice_in_dim(values, core * part, part, 0)

    def widened(values, near, far):
        return ordered(values[None], ordered(near, far, core, 0)[None], col, 0)

    x_near, x_far = move(x_near, ring_in), move(x_far, cross)
    near0, near1 = turned(mine_first[:, :width]), turned(mine_first[:, width:])
    near0, x_near, x_far, mine_second = tie(near0, x_near, x_far, mine_second)
    near0, near1 = tie(near0, near1)
    x_parts = (x_own, x_near, x_far)
    big_second = lax.all_gather(mine_second, both, axis=0, tiled=False)
    big_second = big_second.reshape(n_row, n_col, deep, 2 * hidden_half)
    near0, near1 = doubled(near0, sides_swap), doubled(near1, cols_swap)
    ad_near = move(part_of(adapt_first), cols_swap)
    biases = jnp.concatenate([qv_bias[0], qv_bias[1], up_bias])[None]
    bias_pair = ordered(biases, move(biases, cols_swap), col, 0)
    ids = jnp.where(core == col, adapter_ids, move(adapter_ids, cores))
    g_own, g_near, g_far = spread(cotangent)
    near0, near1, bias_pair, ids, ad_near = tie(near0, near1, bias_pair, ids, ad_near)
    ad_first = widened(adapt_first, ad_near, move(ad_near, cores))
    last0, last1 = move(near0, cols_swap), move(near1, sides_swap)
    far0, far1 = move(near0, cores), move(near1, cores)
    adapt_part = part_of(adapt_second)
    valid = jnp.arange(own_rows)[:, None]
    here, there = jnp.where(core == 0, cut, length - cut), jnp.where(core == 0, length - cut, cut)

    def mask_of(good):
        return jnp.broadcast_to(jnp.where(good, 0.0, -1e30), (own_rows, 2 * HD)).astype(BF16)

    mask_own = mask_of(valid < length)
    mask_shared = mask_of((valid < here) | ((valid >= tb) & (valid < tb + there)))
    last0, last1, far0, far1, ad_first, g_near, g_far = tie(
        last0, last1, far0, far1, ad_first, g_near, g_far
    )
    last0, adapt_part, adapt_second, mask_own, mask_shared = tie(
        last0, adapt_part, adapt_second, mask_own, mask_shared
    )
    ad_near = move(adapt_part, cols_swap)
    blocks0 = (near0, last0, far0, move(last0, cores))
    blocks1 = (near1, last1, far1, move(last1, cores))
    qv_rows = jnp.stack(
        [
            bias_pair[:, :half].reshape(1, width),
            jnp.zeros((1, width), F32),
            bias_pair[:, half:width].reshape(1, width),
        ]
    )
    up_row = bias_pair[:, width:].reshape(1, hidden)

    owners = lax.iota(jnp.int32, stack) // RANK
    own_id = jnp.where(core == 0, ids[0], ids[2])
    places = lax.iota(jnp.int32, total)[:, None]
    sel = (jnp.where(places < own_rows, own_id, ids[1]) == owners[None]).astype(F32)

    gain1, bias1, gain2, bias2 = (t[None] for t in (ln1_gain, ln1_bias, ln2_gain, ln2_bias))

    rows_block = pl.BlockSpec((tb, width), lambda i: (i, 0))
    sel_block = pl.BlockSpec((tb, stack), lambda i: (i, 0))
    every = fixed((total, width))
    thin = fixed((total, stack))
    vec = fixed((1, width))
    pieces0 = [fixed((n_row // 2, deep, width))] * 4
    pieces1 = [fixed((n_row // 2, deep, half))] * 4
    pieces_out = [
        pl.BlockSpec(
            (n_row // 2, deep, half), lambda *_: (0, 0, 1), pipeline_mode=pl.Buffered(1)
        )
    ] * 4
    w_qkv_room = [pltpu.VMEM((3, n_row, deep, width), BF16)]
    w_out_room = [pltpu.VMEM((n_row, deep, width), BF16)]
    ad_out_spec = pl.BlockSpec(
        (n_col, stack, half), lambda *_: (0, 0, 3), pipeline_mode=pl.Buffered(1)
    )
    low_k = pl.BlockSpec((total, stack), lambda k: (0, k))
    shared_k = pl.BlockSpec((1, tb, half), lambda k: (k, 0, 0))
    ad_k = pl.BlockSpec((n_col, stack, half), lambda k: (0, 0, k))
    shared_struct = struct((3, tb, half), BF16)
    half_rows = struct((tb, half), BF16)

    third_rows = pl.BlockSpec((tb, half), lambda i: (i, 0))
    low_block = pl.BlockSpec((tb, 3 * stack), lambda i: (i, 0))
    all_three = pl.BlockSpec((3, tb, width), lambda i: (0, i, 0))
    shared_three = fixed((3, tb, half))
    x, z1, u_qkv, qkv, qkv_keep, qkv_send = call(
        functools.partial(qkv_body, scale),
        (3,),
        [
            SPOT, third_rows, third_rows, third_rows, vec, vec, *pieces0, *pieces1,
            fixed((width, 3 * stack)),
            pl.BlockSpec(
                (n_col, stack, 3 * half), lambda i: (0, 0, 0), pipeline_mode=pl.Buffered(1)
            ),
            fixed((3, 1, width)), sel_block,
        ],
        [rows_block, rows_block, low_block, all_three, shared_three, shared_three],
        [
            struct((total, width), BF16),
            struct((total, width), BF16),
            struct((total, 3 * stack), BF16),
            struct((3, total, width), BF16),
            shared_struct,
            shared_struct,
        ],
        scratch=w_qkv_room,
    )(place, *x_parts, gain1, bias1, *blocks0, *blocks1, a_qkv, ad_first, qv_rows, sel)

    qkv_mate = move(qkv_send, cores)
    qkv, g_near, g_far = tie(qkv, g_near, g_far)
    g_near, g_far = move(g_near, ring_in), move(g_far, cross)

    head_p = pl.BlockSpec((2, own_rows, own_rows), lambda h: (h, 0, 0))
    pair_k = pl.BlockSpec((3, tb, 2 * HD), lambda h: (0, 0, h))
    pair_rows = pl.BlockSpec((tb, 2 * HD), lambda h: (0, h))
    wide = 4 * HD
    att_own, p_own = call(
        attend_body,
        (width // wide,),
        [pl.BlockSpec((1, own_rows, wide), lambda h, k=k: (k, 0, h)) for k in range(3)]
        + [fixed((own_rows, 2 * HD))],
        [
            pl.BlockSpec((own_rows, wide), lambda h: (0, h)),
            pl.BlockSpec((4, own_rows, own_rows), lambda h: (h, 0, 0)),
        ],
        [struct((own_rows, width), BF16), struct((heads, own_rows, own_rows), BF16)],
    )(qkv, qkv, qkv, mask_own)
    qkv_mate, att_own = tie(qkv_mate, att_own)
    wide_k = pl.BlockSpec((3, tb, wide), lambda h: (0, 0, h))
    wide_rows = pl.BlockSpec((tb, wide), lambda h: (0, h))
    att_keep, att_send, p_sh = call(
        attend_shared_body,
        (half // wide,),
        [wide_k, wide_k, fixed((own_rows, 2 * HD))],
        [wide_rows, wide_rows, pl.BlockSpec((4, own_rows, own_rows), lambda h: (h, 0, 0))],
        [half_rows, half_rows, struct((heads // 2, own_rows, own_rows), BF16)],
    )(qkv_keep, qkv_mate, mask_shared)
    att_send, ad_near = tie(att_send, ad_near)
    att_mate = move(att_send, cores)
    g_parts = (g_own, g_near, g_far)
    ad_second = (adapt_second, ad_near, move(ad_near, cores))

    own_block = pl.BlockSpec((tb, width), lambda i: (jnp.minimum(i, 1), 0))
    shared_rows = fixed((tb, half))
    hid, z2, u_out, u_up = call(
        out_body,
        (3,),
        [
            SPOT, own_block, shared_rows, shared_rows, rows_block, *pieces_out,
            ad_out_spec, fixed((stack, width)), vec, vec, vec, fixed((width, stack)), sel_block,
        ],
        [rows_block, rows_block, sel_block, sel_block],
        [
            struct((total, width), F32),
            struct((total, width), BF16),
            struct((total, stack), BF16),
            struct((total, stack), BF16),
        ],
        scratch=w_out_room,
    )(
        place, att_own, att_keep, att_mate, x, *blocks1, ad_first, b_out, out_bias[None],
        gain2, bias2, a_up, sel,
    )

    chunk = half
    parts = hidden_half // chunk

    def w_spec(shift):
        return pl.BlockSpec(
            (n_row, 1, deep, chunk), lambda j: (0, j // parts, 0, j % parts + shift)
        )

    def ad_specs(shift):
        return [
            pl.BlockSpec((rows, chunk), lambda j: (0, j % parts + shift))
            for rows in (stack, part, part)
        ]

    early_half = fixed((2, part, 2 * hidden_half + 2 * half))
    early_struct = struct((2, part, 2 * hidden_half + 2 * half), BF16)
    y_own, y_near, y_far, ghb, early_keep, early_send = call(
        functools.partial(mlp_body, tb),
        (2 * parts,),
        [SPOT, every]
        + third_specs
        + [
            thin, thin, pl.BlockSpec(memory_space=pl.ANY), w_spec(0), w_spec(parts), *ad_specs(0), *ad_specs(parts),
            pl.BlockSpec((1, chunk), lambda j: (0, j)), fixed((stack, width)),
            fixed((width, stack)), vec, vec,
        ],
        third_specs + [every, early_half, early_half],
        thirds
        + [struct((total, width), BF16), early_struct, early_struct],
        scratch=[
            pltpu.VMEM((total, width), F32),
            pltpu.VMEM((total, width), F32),
            pltpu.VMEM((total, stack), F32),
            pltpu.VMEM((total, stack), F32),
            pltpu.VMEM((total, stack), BF16),
            pltpu.VMEM((stack, total), BF16),
            pltpu.VMEM((stack, total), BF16),
            pltpu.VMEM((total, chunk), BF16),
            pltpu.VMEM((total, chunk), BF16),
            pltpu.VMEM((total, width), BF16),
            pltpu.VMEM((total, width), F32),
            pltpu.SemaphoreType.DMA,
        ],
    )(
        place, z2, *g_parts, u_up, sel, hid, big_second, big_second, *ad_second, *ad_second, up_row,
        b_down, a_up, down_bias[None], gain2,
    )

    def added(kept, sent):
        return (kept.astype(F32) + sent.astype(F32)).astype(BF16)

    quarter = part // 2

    def quarter_of(values, index):
        return lax.dynamic_slice_in_dim(values, index * quarter, quarter, 1)

    def side_sent(values):
        return move(quarter_of(values, 1 - side), sides_swap)

    early_sent = move(early_send, cores)
    y_near, y_far = move(y_near, ring_back), move(y_far, cross)
    out_half = fixed((2, part, width))
    d_att, d_keep, d_send, out_keep, out_send = call(
        out_back_body,
        (2,),
        [
            SPOT, every, pl.BlockSpec((own_rows, half), lambda i: (0, i)), shared_rows,
            shared_rows, *pieces_out,
            pl.BlockSpec((1, stack, half), lambda i: (i, 0, 3)), fixed((stack, width)), thin, thin,
        ],
        [
            pl.BlockSpec((own_rows, half), lambda i: (0, i)), shared_rows, shared_rows, out_half,
            out_half,
        ],
        [
            struct((own_rows, width), BF16),
            half_rows,
            half_rows,
            struct((2, part, width), BF16),
            struct((2, part, width), BF16),
        ],
        scratch=[
            pltpu.VMEM((2, n_row, deep, half), BF16),
            pltpu.VMEM((total, stack), BF16),
            pltpu.VMEM((stack, total), BF16),
        ],
    )(place, ghb, att_own, att_keep, att_mate, *blocks1, ad_first, b_out, sel, u_out)

    d_mate = move(d_send, cores)
    early_sum = jnp.concatenate(
        [added(early_keep, early_sent), added(out_keep, move(out_send, cores))], axis=2
    )
    d_mate, early_sum = tie(d_mate, early_sum)
    early_sent = side_sent(early_sum)

    g_keep, g_send = call(
        functools.partial(attend_back_shared_body, scale),
        (heads // 4,),
        [pair_k, pair_k, head_p, pair_rows, pair_rows, pair_rows, pair_rows],
        [pair_k, pair_k],
        [shared_struct, shared_struct],
    )(qkv_keep, qkv_mate, p_sh, att_keep, att_send, d_keep, d_mate)
    d_att, g_send = tie(d_att, g_send)
    g_mate = move(g_send, cores)
    quarters = heads // 4

    def own_back(shift, d_out):
        return call(
            functools.partial(attend_back_body, scale),
            (quarters,),
            [
                pl.BlockSpec((1, own_rows, 2 * HD), lambda h, k=k: (k, 0, h + shift))
                for k in range(3)
            ]
            + [
                pl.BlockSpec((2, own_rows, own_rows), lambda h: (h + shift, 0, 0)),
                pl.BlockSpec((own_rows, 2 * HD), lambda h: (0, h + shift)),
                pl.BlockSpec((own_rows, 2 * HD), lambda h: (0, h + shift)),
            ],
            pl.BlockSpec((3, own_rows, 2 * HD), lambda h: (0, 0, h)),
            struct((3, own_rows, half), BF16),
        )(qkv, qkv, qkv, p_own, att_own, d_out)

    d_left = own_back(0, d_att)
    early_sum = added(quarter_of(early_sum, side), early_sent)
    d_left, d_att, early_sum, y_near, y_far = tie(d_left, d_att, early_sum, y_near, y_far)
    early_sent = move(pick(early_sum, 1 - col), cols_swap)
    d_right = own_back(quarters, d_att)

    grad_spec = pl.BlockSpec((2, 2, 1, part, half), lambda k: (0, 0, k, 0, 0))
    grad_struct = struct((2, 2, 3, part, half), BF16)
    early_sum = added(pick(early_sum, col), early_sent)
    d_right, early_sum = tie(d_right, early_sum)
    early_sent = move(early_sum, far_swaps[0])
    half_k = pl.BlockSpec((1, own_rows, half), lambda k: (k, 0, 0))
    e_qkv, q_kept, q_sent = call(
        qkv_grads_body,
        (3,),
        [SPOT, half_k, half_k, shared_k, shared_k, ad_k, thin, low_k, every],
        [low_k, grad_spec, grad_spec],
        [struct((total, 3 * stack), BF16), grad_struct, grad_struct],
    )(place, d_left, d_right, g_keep, g_mate, ad_first, sel, u_qkv, z1)

    def side_of(values, index):
        return jnp.where(index == 0, values[:, 0], values[:, 1])

    sums = added(q_kept, move(q_sent, cores)).reshape(2, 2, 3 * part, half)
    early_sum = added(early_sum, early_sent)
    sums, e_qkv, early_sum = tie(sums, e_qkv, early_sum)
    early_sent = move(early_sum, far_swaps[-1])
    q_sent = move(side_of(sums, 1 - side), sides_swap)
    def token_rows(block, left, right):
        at = block % 2
        d_spec = pl.BlockSpec((3, tb, half), lambda i: (0, at, 0), pipeline_mode=pl.Buffered(1))
        rows = pl.BlockSpec((tb, width), lambda i: (block, 0), pipeline_mode=pl.Buffered(1))
        low = pl.BlockSpec((tb, 3 * stack), lambda i: (block, 0), pipeline_mode=pl.Buffered(1))
        return call(
            functools.partial(qkv_back_body, block == 2),
            (1,),
            [
                SPOT, d_spec, d_spec, *pieces0, *pieces1, fixed((width, 3 * stack)), low, rows,
                rows, vec,
            ],
            [shared_rows] * 3,
            [half_rows] * 3,
            scratch=w_qkv_room,
        )(place, left, right, *blocks0, *blocks1, a_qkv, e_qkv, x, ghb, gain1)

    t_own, t_near, t_far = [], [], []

    def sent_rows(own, near, far):
        t_own.append(own)
        t_near.append(move(near, ring_back))
        t_far.append(move(far, cross))

    rows_own, rows_near, rows_far = token_rows(0, d_left, d_right)
    q_sent, rows_near, rows_far = tie(q_sent, rows_near, rows_far)
    sums = added(side_of(sums, side), q_sent)
    sums, d_left, d_right = tie(sums, d_left, d_right)
    q_sent = move(pick(sums, 1 - col), cols_swap)
    sent_rows(rows_own, rows_near, rows_far)
    rows_own, rows_near, rows_far = token_rows(1, d_left, d_right)
    q_sent, rows_near, rows_far, early_sent = tie(q_sent, rows_near, rows_far, early_sent)
    early_sum = added(early_sum, early_sent)
    sums = added(pick(sums, col), q_sent)
    sums, g_keep, g_mate = tie(sums, g_keep, g_mate)
    q_sent = move(sums, far_swaps[0])
    sent_rows(rows_own, rows_near, rows_far)
    edge = 2 * hidden_half
    whole = edge + 4 * half
    split_lanes = [slice(edge, edge + 2 * half), slice(edge + 3 * half, whole)]
    rest = jnp.concatenate([early_sum[:, lanes] for lanes in split_lanes], axis=1)
    rest = move(rest, cols_swap)
    rows_own, rows_near, rows_far = token_rows(2, g_keep, g_mate)
    early_sum = jnp.concatenate([early_sum, rest], axis=1)
    q_sent, rows_near, rows_far, early_sum, y_own, t_near[0], t_far[0] = tie(
        q_sent, rows_near, rows_far, early_sum, y_own, t_near[0], t_far[0]
    )
    sums = added(sums, q_sent)
    q_sent = move(sums, far_swaps[1])
    sent_rows(rows_own, rows_near, rows_far)
    early_sent = move(early_sum, sides_swap)
    layer_out = join([y_own], [y_near], [y_far], BF16)
    early_sum = ordered(early_sum, early_sent, side, 0)
    q_sent, early_sum, layer_out, t_near[1], t_far[1] = tie(
        q_sent, early_sum, layer_out, t_near[1], t_far[1]
    )
    early_sent = move(early_sum, cores)
    sums = added(sums, q_sent)
    for pairs in far_swaps[2:]:
        sums = added(sums, move(sums, pairs))
    side_sums = move(sums, sides_swap)
    tokens_grad = join(t_own, t_near, t_far, F32)
    mine = ordered(early_sum, early_sent, core, 0)
    side_sums, tokens_grad, mine = tie(side_sums, tokens_grad, mine)
    mine = mine.astype(F32)
    sums = ordered(sums[None], side_sums[None], side, 0)
    a_sent = move(sums[1:], cols_swap)
    own_starts = (edge, edge + half, edge + 3 * half)
    a_up_sum, b_down_sum, b_out_sum = (
        ordered(
            mine[:, start : start + half],
            mine[:, whole + i * half : whole + (i + 1) * half],
            col,
            1,
        )
        for i, start in enumerate(own_starts)
    )
    a_out_sum, a_up_sum = mine[:, edge + 2 * half : edge + 3 * half].T, a_up_sum.T
    b_up_sum, a_down_sum = mine[:, :hidden_half], mine[:, hidden_half:edge].T
    a_sent, a_out_sum, a_up_sum, b_up_sum, a_down_sum, b_down_sum, b_out_sum = tie(
        a_sent, a_out_sum, a_up_sum, b_up_sum, a_down_sum, b_down_sum, b_out_sum
    )
    every_sum = jnp.concatenate([sums[:1], ordered(sums[1:], a_sent, col, 0)])
    every_sum = every_sum.reshape(3, 3, part, half)
    every_sum = ordered(every_sum, move(every_sum, cores), core, 2).reshape(3, 3 * stack, half)
    b_sum = every_sum[0].reshape(3, stack, half).astype(F32)
    a_sum = jnp.concatenate([every_sum[1].T, every_sum[2].T]).astype(F32)
    return (
        layer_out,
        tokens_grad,
        a_sum,
        b_sum,
        a_out_sum,
        b_out_sum,
        a_up_sum,
        b_up_sum,
        a_down_sum,
        b_down_sum,
    )


def solution(mesh):
    placed = (
        P("row", "col"),
        P("row", "col"),
        P(),
        P(),
        P(),
        P(),
        P(None, "row", "col"),
        P(None, "col"),
        P("col", "row"),
        P(),
        P("row", "col"),
        P("col"),
        P("col", "row"),
        P(),
        P("row"),
        P(),
        P(None, None, "col"),
        P("col", None),
        P(),
        P(),
        P(None, "col"),
        P("col", None),
        P(),
    )
    shape = (mesh.shape["row"], mesh.shape["col"])
    paired = shape[1] == 2 and shape[0] >= 16 and shape[0] & (shape[0] - 1) == 0
    return jax.shard_map(
        functools.partial(on_chip_pair, shape) if paired else on_device,
        mesh=mesh,
        in_specs=placed,
        out_specs=(
            P("row", "col"),
            P("row", "col"),
            P(),
            P(None, None, "col"),
            P("col", None),
            P(),
            P(),
            P(None, "col"),
            P("col", None),
            P(),
        ),
        check_vma=False,
    )
```

```python
import functools

import jax
import jax.numpy as jnp
from jax import lax
from jax.experimental import pallas as pl
from jax.experimental.pallas import tpu as pltpu
from jax.sharding import PartitionSpec as P

HD = 64
RANK = 16


EPS = 1e-05
GELU_SCALE = 1.702


def column_sums(first, second):
    return lax.psum((first, second), "col")


def gather_features(values):
    return lax.all_gather(values, "col", axis=1, tiled=True)


def sum_partials(terms):
    return lax.psum_scatter(
        terms.astype(jnp.bfloat16), "col", scatter_dimension=1, tiled=True
    ).astype(jnp.float32)


def norm_split(values, feature_width):
    first, second = column_sums(jnp.sum(values, axis=1), jnp.sum(values * values, axis=1))
    centre = first / feature_width
    inverse = lax.rsqrt(second / feature_width - centre * centre + EPS)
    return ((values - centre[:, None]) * inverse[:, None], inverse)


def norm_back(grad_normed, normal_rows, inverse, gain_part, feature_width):
    scaled = grad_normed * gain_part
    first, second = column_sums(jnp.sum(scaled, axis=1), jnp.sum(scaled * normal_rows, axis=1))
    return inverse[:, None] * (
        scaled - first[:, None] / feature_width - normal_rows * second[:, None] / feature_width
    )


def select_rows(low_rank, onehot, image_len):
    image_count, stack_width = onehot.shape
    shaped = low_rank.reshape(image_count, image_len, -1, stack_width)
    return (shaped * onehot[:, None, None, :]).reshape(low_rank.shape).astype(jnp.bfloat16)


def mult(form, first, second):
    return jnp.einsum(form, first, second, preferred_element_type=jnp.float32)


def on_device(
    tokens,
    cotangent,
    ln1_gain,
    ln1_bias,
    ln2_gain,
    ln2_bias,
    w_qkv,
    qv_bias,
    w_out,
    out_bias,
    w_up,
    up_bias,
    w_down,
    down_bias,
    adapter_ids,
    a_qkv,
    b_qkv,
    a_out,
    b_out,
    a_up,
    b_up,
    a_down,
    b_down,
):
    row_count, part_width = tokens.shape
    feature_width = a_qkv.shape[0]
    stack_width = a_qkv.shape[1] // 3
    image_count = adapter_ids.shape[0]
    image_len = row_count // image_count
    head_count = part_width // HD
    scale = HD ** (-0.5)
    offset = lax.axis_index("col") * part_width

    def own_part(values, axis):
        return lax.dynamic_slice_in_dim(values, offset, part_width, axis)

    owners = lax.iota(jnp.int32, stack_width) // RANK
    onehot = (adapter_ids[:, None] == owners[None, :]).astype(jnp.float32)
    wide_qkv, wide_out, wide_up, wide_down = (
        lax.all_gather(w_qkv, "row", axis=1, tiled=True),
        lax.all_gather(w_out, "row", axis=1, tiled=True),
        lax.all_gather(w_up, "row", axis=0, tiled=True),
        lax.all_gather(w_down, "row", axis=1, tiled=True),
    )
    inputs = tokens.astype(jnp.float32)
    normal_one, inverse_one = norm_split(inputs, feature_width)
    normed_part = (normal_one * own_part(ln1_gain, 0) + own_part(ln1_bias, 0)).astype(jnp.bfloat16)
    normed_one = gather_features(normed_part)
    projected = mult("td,kde->kte", normed_one, wide_qkv)
    kept_qkv = select_rows(mult("td,dj->tj", normed_one, a_qkv), onehot, image_len)
    projected = projected + mult("tkj,kje->kte", kept_qkv.reshape(row_count, 3, stack_width), b_qkv)
    bias_rows = jnp.stack([qv_bias[0], jnp.zeros_like(qv_bias[0]), qv_bias[1]])[:, None, :]
    qkv = (projected + bias_rows).astype(jnp.bfloat16)
    shaped = qkv.reshape(3, image_count, image_len, head_count, HD)
    queries, key_rows, value_rows = (shaped[0], shaped[1], shaped[2])
    scores = mult("bqhd,bkhd->bhqk", queries, key_rows) * scale
    highest = jnp.max(scores, axis=-1, keepdims=True)
    log_total = highest + jnp.log(jnp.sum(jnp.exp(scores - highest), axis=-1, keepdims=True))
    weights_low = jnp.exp(scores - log_total).astype(jnp.bfloat16)
    attended = mult("bhqk,bkhd->bqhd", weights_low, value_rows)
    attended = attended.reshape(row_count, part_width).astype(jnp.bfloat16)
    kept_out = select_rows(mult("tc,cj->tj", attended, a_out), onehot, image_len)
    out_terms = mult("tc,cd->td", attended, wide_out) + mult("tj,jd->td", kept_out, b_out)
    hidden = inputs + sum_partials(out_terms) + own_part(out_bias, 0)
    normal_two, inverse_two = norm_split(hidden, feature_width)
    normed_part_two = (normal_two * own_part(ln2_gain, 0) + own_part(ln2_bias, 0)).astype(
        jnp.bfloat16
    )
    normed_two = gather_features(normed_part_two)
    kept_up = select_rows(mult("td,dj->tj", normed_two, a_up), onehot, image_len)
    pre_up = mult("td,df->tf", normed_two, wide_up) + mult("tj,jf->tf", kept_up, b_up) + up_bias
    logistic = jax.nn.sigmoid(GELU_SCALE * pre_up)
    activated = (pre_up * logistic).astype(jnp.bfloat16)
    kept_down = select_rows(mult("tf,fj->tj", activated, a_down), onehot, image_len)
    down_terms = mult("tf,fd->td", activated, wide_down) + mult("tj,jd->td", kept_down, b_down)
    layer_out = (hidden + sum_partials(down_terms) + own_part(down_bias, 0)).astype(jnp.bfloat16)
    wide_qkv, wide_out, wide_up, wide_down = (
        lax.all_gather(w_qkv, "row", axis=1, tiled=True),
        lax.all_gather(w_out, "row", axis=1, tiled=True),
        lax.all_gather(w_up, "row", axis=0, tiled=True),
        lax.all_gather(w_down, "row", axis=1, tiled=True),
    )
    grad_layer = cotangent.astype(jnp.float32)
    grad_full = gather_features(cotangent)
    d_low_down = select_rows(mult("td,jd->tj", grad_full, b_down), onehot, image_len)
    d_activated = mult("td,fd->tf", grad_full, wide_down) + mult("tj,fj->tf", d_low_down, a_down)
    grad_b_down = mult("tj,td->jd", kept_down, grad_full)
    grad_a_down = mult("tf,tj->fj", activated, d_low_down)
    d_pre_up = (
        d_activated * (logistic + GELU_SCALE * pre_up * logistic * (1.0 - logistic))
    ).astype(jnp.bfloat16)
    d_low_up = select_rows(mult("tf,jf->tj", d_pre_up, b_up), onehot, image_len)
    grad_b_up = mult("tj,tf->jf", kept_up, d_pre_up)
    grad_a_up = mult("td,tj->dj", normed_two, d_low_up)
    normed_two_terms = mult("tf,df->td", d_pre_up, wide_up) + mult("tj,dj->td", d_low_up, a_up)
    d_normed_two = sum_partials(normed_two_terms)
    grad_hidden = grad_layer + norm_back(
        d_normed_two, normal_two, inverse_two, own_part(ln2_gain, 0), feature_width
    )
    hidden_full_grad = gather_features(grad_hidden.astype(jnp.bfloat16))
    d_low_out = select_rows(mult("td,jd->tj", hidden_full_grad, b_out), onehot, image_len)
    d_attended = mult("td,cd->tc", hidden_full_grad, wide_out) + mult("tj,cj->tc", d_low_out, a_out)
    grad_b_out = mult("tj,td->jd", kept_out, hidden_full_grad)
    grad_a_out = mult("tc,tj->cj", attended, d_low_out)
    d_heads = d_attended.astype(jnp.bfloat16).reshape(image_count, image_len, head_count, HD)
    scores_again = mult("bqhd,bkhd->bhqk", queries, key_rows) * scale
    weights_again = jnp.exp(scores_again - log_total)
    weights_again_low = weights_again.astype(jnp.bfloat16)
    d_weights = mult("bqhd,bkhd->bhqk", d_heads, value_rows)
    d_values = mult("bhqk,bqhd->bkhd", weights_again_low, d_heads)
    d_scores = weights_again * (
        d_weights - jnp.sum(weights_again * d_weights, axis=-1, keepdims=True)
    )
    d_scores = d_scores.astype(jnp.bfloat16)
    d_queries = scale * mult("bhqk,bkhd->bqhd", d_scores, key_rows)
    d_keys = scale * mult("bhqk,bqhd->bkhd", d_scores, queries)
    d_qkv = (
        jnp.stack([d_queries, d_keys, d_values])
        .reshape(3, row_count, part_width)
        .astype(jnp.bfloat16)
    )
    d_low_qkv = mult("kte,kje->tkj", d_qkv, b_qkv)
    d_low_qkv = select_rows(d_low_qkv.reshape(row_count, 3 * stack_width), onehot, image_len)
    grad_b_qkv = mult("tkj,kte->kje", kept_qkv.reshape(row_count, 3, stack_width), d_qkv)
    grad_a_qkv = mult("td,tj->dj", normed_one, d_low_qkv)
    normed_one_terms = mult("kte,kde->td", d_qkv, wide_qkv) + mult("tj,dj->td", d_low_qkv, a_qkv)
    d_normed_one = sum_partials(normed_one_terms)
    tokens_grad = grad_hidden + norm_back(
        d_normed_one, normal_one, inverse_one, own_part(ln1_gain, 0), feature_width
    )
    grad_a_qkv, grad_b_out, grad_a_up, grad_b_down = lax.psum(
        (grad_a_qkv, grad_b_out, grad_a_up, grad_b_down), ("row", "col")
    )
    grad_b_qkv, grad_a_out, grad_b_up, grad_a_down = (
        lax.psum(grad_b_qkv.astype(jnp.bfloat16), "row").astype(jnp.float32),
        lax.psum(grad_a_out.astype(jnp.bfloat16), "row").astype(jnp.float32),
        lax.psum(grad_b_up.astype(jnp.bfloat16), "row").astype(jnp.float32),
        lax.psum(grad_a_down.astype(jnp.bfloat16), "row").astype(jnp.float32),
    )
    return (
        layer_out,
        tokens_grad,
        grad_a_qkv,
        grad_b_qkv,
        grad_a_out,
        grad_b_out,
        grad_a_up,
        grad_b_up,
        grad_a_down,
        grad_b_down,
    )


NT = (((1,), (1,)), ((), ()))
NN = (((1,), (0,)), ((), ()))
F32 = jnp.float32
BF16 = jnp.bfloat16
VMEM_SMALL, VMEM_LARGE = 36 * 1024 * 1024, 60 * 1024 * 1024
SPOT = pl.BlockSpec(memory_space=pltpu.SMEM)


def dot(first, second, dims=NN):
    return lax.dot_general(first, second, dims, preferred_element_type=F32)


def dot_rows(first, second):
    return dot(first.T, second)


def call(body, grid, in_specs, out_specs, out_shape, scratch=(), us=None):
    return pl.pallas_call(
        body,
        grid=grid,
        in_specs=in_specs,
        out_specs=out_specs,
        out_shape=out_shape,
        scratch_shapes=list(scratch),
        compiler_params=pltpu.CompilerParams(
            dimension_semantics=("arbitrary",) * len(grid),
            vmem_limit_bytes=VMEM_LARGE if us is None else VMEM_SMALL,
        ),
        cost_estimate=None
        if us is None
        else pl.CostEstimate(
            flops=us * 900_000_000, bytes_accessed=1_000_000, transcendentals=0
        ),
    )


def fixed(shape):
    zeros = (0,) * len(shape)
    return pl.BlockSpec(shape, lambda *_: zeros, pipeline_mode=pl.Buffered(1))


def struct(shape, kind):
    return jax.ShapeDtypeStruct(shape, kind)


def norm_of(values):
    centred = values - jnp.mean(values, axis=1, keepdims=True)
    inverse = lax.rsqrt(jnp.mean(centred * centred, axis=1, keepdims=True) + EPS)
    return centred * inverse, inverse


def norm_pull(grad, normal, inverse, gain):
    scaled = grad * gain
    return inverse * (
        scaled
        - jnp.mean(scaled, axis=1, keepdims=True)
        - normal * jnp.mean(scaled * normal, axis=1, keepdims=True)
    )


def settle(place, pieces, side_first, store):
    depth = pieces[0].shape[0]
    n_far = depth // 2
    for group, piece in enumerate(pieces):
        for index in range(depth):
            other, outer, inner, back = (
                group // 2, group % 2, index // n_far, index % n_far
            )
            x_off, y_off = (outer, inner) if side_first else (inner, outer)
            far = lax.rem(place[0] + (n_far - back), n_far)
            x = place[1] if x_off == 0 else 1 - place[1]
            core = place[2] if other == 0 else 1 - place[2]
            y = place[3] if y_off == 0 else 1 - place[3]
            store(far * 4 + x * 2 + core, y, piece[index])


def settle_qkv(place, pieces0, pieces1, w_ref):
    half = pieces1[0].shape[2]

    def lanes(y):
        return pl.ds(pl.multiple_of(y * half, half), half)

    def first(row, y, block):
        w_ref[0, row, :, lanes(y)] = block[:, :half]
        w_ref[1, row, :, lanes(y)] = block[:, half:]

    def last(row, y, block):
        w_ref[2, row, :, lanes(y)] = block

    settle(place, pieces0, False, first)
    settle(place, pieces1, True, last)


def settle_out(place, pieces1, w_ref):
    half = pieces1[0].shape[2]

    def store(row, y, block):
        w_ref[row, :, pl.ds(pl.multiple_of(y * half, half), half)] = block

    settle(place, pieces1, True, store)


def chosen(index, first, second):
    return jnp.where(index == 0, first, second)


def both_halves(place, own, near, far):
    diagonal = place[2] == place[3]
    mine = jnp.where(diagonal, own, near)
    other = jnp.where(diagonal, near, far)
    return chosen(place[3], mine, other), chosen(place[3], other, mine)


def halves_out(place, values, rows, own_ref, near_ref, far_ref):
    half = values.shape[1] // 2
    left, right = values[:, :half], values[:, half:]
    mine, other = chosen(place[3], left, right), chosen(place[3], right, left)
    own_ref[rows, :] = mine
    near_ref[rows, :] = jnp.where(place[2] == place[3], other, mine)
    far_ref[rows, :] = other


def spread_body(length, cut, own_rows, tb, place, t_ref, own_ref, near_ref, far_ref, wide_ref):
    wide_ref[...] = t_ref[...].astype(F32)

    def put(ref, start, shared, shared_count):
        ref[:length, :] = wide_ref[start : start + length, :].astype(BF16)
        ref[own_rows : own_rows + shared_count, :] = wide_ref[
            shared : shared + shared_count, :
        ].astype(BF16)

    for ref, index in ((own_ref, place[2]), (near_ref, 1 - place[3]), (far_ref, 1 - place[2])):
        ref[...] = jnp.zeros_like(ref)

        @pl.when(index == 0)
        def _():
            put(ref, 0, length, cut)

        @pl.when(index == 1)
        def _():
            put(ref, 2 * length, length + cut, length - cut)


def join_body(length, cut, own_rows, pieces, place, *refs):
    *in_refs, out_ref, wide_ref = refs

    def whole(part):
        found = [ref[...] for ref in in_refs[part * pieces : (part + 1) * pieces]]
        return found[0] if pieces == 1 else jnp.concatenate(found)

    own, near, far = whole(0), whole(1), whole(2)
    diagonal = place[2] == place[3]
    mine = jnp.where(diagonal, own, near)
    mate = jnp.where(diagonal, near, far)
    first = chosen(place[2], mine, mate).astype(F32)
    second = chosen(place[2], mate, mine).astype(F32)
    wide_ref[:length, :] = first[:length]
    wide_ref[length : length + cut, :] = first[own_rows : own_rows + cut]
    wide_ref[length + cut : 2 * length, :] = second[own_rows : own_rows + length - cut]
    wide_ref[2 * length :, :] = second[:length]
    out_ref[...] = wide_ref[...].astype(out_ref.dtype)


def qkv_body(
    scale, place, own_ref, near_ref, far_ref, gain, bias, p0, p1, p2, p3, r0, r1, r2, r3, a_ref,
    b_ref, qv_ref, sel_ref, x_ref, z_ref, u_ref, out_ref, keep_out, send_out, w_ref,
):
    width = x_ref.shape[1]
    half = width // 2
    stack = sel_ref.shape[1]

    @pl.when(pl.program_id(0) == 0)
    def _():
        settle_qkv(place, (p0, p1, p2, p3), (r0, r1, r2, r3), w_ref)

    left, right = both_halves(place, own_ref[...], near_ref[...], far_ref[...])
    x = jnp.concatenate([left, right], axis=1)
    x_ref[...] = x
    normal, _ = norm_of(x.astype(F32))
    z = (normal * gain[...] + bias[...]).astype(BF16)
    z_ref[...] = z
    low = dot(z, a_ref[...])
    for k in range(3):
        kept = (low[:, k * stack : (k + 1) * stack] * sel_ref[...]).astype(BF16)
        u_ref[:, k * stack : (k + 1) * stack] = kept
        w = w_ref[k].reshape(width, width)
        parts = []
        for y in range(2):
            lanes = slice(y * half, (y + 1) * half)
            acc = dot(z, w[:, lanes]) + dot(kept, b_ref[y, :, k * half : (k + 1) * half])
            out = (acc + qv_ref[k, :, lanes]).astype(BF16)
            if k == 0:
                out = out * jnp.asarray(scale, BF16)
            out_ref[k, :, lanes] = out
            parts.append(out)
        keep_out[k] = chosen(place[2], parts[0], parts[1])
        send_out[k] = chosen(place[2], parts[1], parts[0])


def attend_pairs(pairs, mask, p_ref):
    lane = lax.broadcasted_iota(jnp.int32, mask.shape, 1)
    one, zero = jnp.ones_like(mask), jnp.zeros_like(mask)
    work = []
    for q, k, v in pairs:
        for spare, here in ((HD, lane < HD), (0, lane >= HD)):
            mine = jnp.where(here, q, jnp.where(lane == spare, one, zero))
            work.append((mine, jnp.where(lane == spare, mask, k), v))
    scores, parts = [dot(work[0][0], work[0][1], NT)], []
    for i, (_, _, v) in enumerate(work):
        if i + 1 < len(work):
            scores.append(dot(work[i + 1][0], work[i + 1][1], NT))
        s = scores[i]
        e = jnp.exp(s - jnp.max(s, axis=1, keepdims=True))
        p = (e * (1.0 / jnp.sum(e, axis=1, keepdims=True))).astype(BF16)
        p_ref[i] = p
        parts.append(dot(p, v))
    return [
        jnp.where(lane < HD, parts[i], parts[i + 1]).astype(BF16) for i in range(0, len(parts), 2)
    ]


def pair_lanes(ref):
    return [slice(i, i + 2 * HD) for i in range(0, ref.shape[-1], 2 * HD)]


def attend_body(q_ref, k_ref, v_ref, mask_ref, out_ref, p_ref):
    lanes = pair_lanes(out_ref)
    pairs = [(q_ref[0, :, at], k_ref[0, :, at], v_ref[0, :, at]) for at in lanes]
    for at, out in zip(lanes, attend_pairs(pairs, mask_ref[...], p_ref)):
        out_ref[:, at] = out


def attend_shared_body(mine_ref, mate_ref, mask_ref, keep_ref, send_ref, p_ref):
    lanes = pair_lanes(keep_ref)
    pairs = [
        [jnp.concatenate([mine_ref[i, :, at], mate_ref[i, :, at]]) for i in range(3)]
        for at in lanes
    ]
    count = keep_ref.shape[0]
    for at, out in zip(lanes, attend_pairs(pairs, mask_ref[...], p_ref)):
        keep_ref[:, at] = out[:count]
        send_ref[:, at] = out[count:]


def attend_back_one(scale, q, k, v, p_ref, att, do):
    low_lanes = lax.broadcasted_iota(jnp.int32, q.shape, 1) < HD
    zero = jnp.zeros_like(q)
    product = att.astype(F32) * do.astype(F32)
    do_t, q_t = do.T, q.T
    places = (low_lanes, ~low_lanes)
    dp = [dot(jnp.where(here, do, zero), v, NT) for here in places]
    dv = [dot(do_t[h * HD : (h + 1) * HD], p_ref[h]) for h in range(2)]
    ds = []
    for h, here in enumerate(places):
        delta = jnp.sum(jnp.where(here, product, 0.0), axis=1, keepdims=True)
        ds.append((p_ref[h].astype(F32) * (dp[h] - delta)).astype(BF16))
    dq = sum(dot(ds[h], jnp.where(here, k, zero)) for h, here in enumerate(places))
    dk = [dot(q_t[h * HD : (h + 1) * HD], ds[h]) for h in range(2)]
    dk, dv = (jnp.concatenate(t).astype(BF16).T for t in (dk, dv))
    return (dq * scale).astype(BF16), dk, dv


def attend_back_body(scale, q_ref, k_ref, v_ref, p_ref, att_ref, do_ref, out_ref):
    parts = attend_back_one(
        scale, q_ref[0], k_ref[0], v_ref[0], p_ref, att_ref[...], do_ref[...]
    )
    for i in range(3):
        out_ref[i] = parts[i]


def attend_back_shared_body(
    scale, mine_ref, mate_ref, p_ref, att_keep, att_send, do_keep, do_mate, keep_ref, send_ref
):
    q, k, v = (jnp.concatenate([mine_ref[i], mate_ref[i]]) for i in range(3))
    att = jnp.concatenate([att_keep[...], att_send[...]])
    do = jnp.concatenate([do_keep[...], do_mate[...]])
    parts = attend_back_one(scale, q, k, v, p_ref, att, do)
    count = keep_ref.shape[1]
    for i in range(3):
        keep_ref[i] = parts[i][:count]
        send_ref[i] = parts[i][count:]


def out_body(
    place, own_ref, keep_ref, mate_ref, x_ref, r0, r1, r2, r3, a_ref, b_ref, bias_ref, gain,
    lbias, aup_ref, sel_ref, hid_ref, z_ref, u_ref, uup_ref, w_ref,
):
    width = x_ref.shape[1]
    half = width // 2

    @pl.when(pl.program_id(0) == 0)
    def _():
        settle_out(place, (r0, r1, r2, r3), w_ref)

    keep, mate = keep_ref[...], mate_ref[...]
    shared = jnp.concatenate(
        [chosen(place[2], keep, mate), chosen(place[2], mate, keep)], axis=1
    )
    att = jnp.where(pl.program_id(0) < 2, own_ref[...], shared)
    sel = sel_ref[...]
    low = dot(att[:, :half], a_ref[0], NT) + dot(att[:, half:], a_ref[1], NT)
    kept = (low * sel).astype(BF16)
    u_ref[...] = kept
    acc = dot(att, w_ref[...].reshape(width, width), NT) + dot(kept, b_ref[...])
    hidden = x_ref[...].astype(F32) + acc + bias_ref[...]
    hid_ref[...] = hidden
    normal, _ = norm_of(hidden)
    z = (normal * gain[...] + lbias[...]).astype(BF16)
    z_ref[...] = z
    uup_ref[...] = (dot(z, aup_ref[...]) * sel).astype(BF16)


def mlp_body(
    rows, place, z_ref, gown_ref, gnear_ref, gfar_ref, uup_ref, sel_ref, hid_ref, wup_ref,
    wdn_ref, bup_own, bup_near, bup_far, adn_own, adn_near, adn_far, upb_ref, bdn_ref, aup_ref,
    dnb_ref, gain,
    own_ref, near_ref, far_ref, ghb_ref, ekeep_ref, esend_ref,
    down_acc, dz_acc, udn_acc, eup_acc, edn_ref, uup_t, edn_t, gy_ref, hid_buf, hid_sem,
):
    total, width = z_ref.shape
    step = pl.program_id(0)
    blocks = [slice(i, i + rows) for i in range(0, total, rows)]

    fetch = pltpu.make_async_copy(hid_ref, hid_buf, hid_sem)

    @pl.when(step == 0)
    def _():
        fetch.start()
        for b in blocks:
            left, right = both_halves(place, gown_ref[b, :], gnear_ref[b, :], gfar_ref[b, :])
            gy = jnp.concatenate([left, right], axis=1)
            gy_ref[b, :] = gy
            edn_ref[b, :] = (dot(gy, bdn_ref[...], NT) * sel_ref[b, :]).astype(BF16)
        edn_t[...] = edn_ref[...].T
        uup_t[...] = uup_ref[...].T
        down_acc[...] = jnp.zeros_like(down_acc)
        dz_acc[...] = jnp.zeros_like(dz_acc)
        udn_acc[...] = jnp.zeros_like(udn_acc)
        eup_acc[...] = jnp.zeros_like(eup_acc)

    chunk = upb_ref.shape[1]
    wup = wup_ref[...].reshape(width, chunk)
    wdn = wdn_ref[...].reshape(width, chunk)
    parts = pl.num_programs(0) // 2
    y = step // parts

    def adapter(own_ref, near_ref, far_ref):
        near, far = near_ref[...], far_ref[...]
        other = jnp.concatenate([chosen(place[2], near, far), chosen(place[2], far, near)])
        return jnp.where(place[3] == y, own_ref[...], other)

    bup = adapter(bup_own, bup_near, bup_far)
    adn = adapter(adn_own, adn_near, adn_far)
    pre = dot(z_ref[...], wup) + dot(uup_ref[...], bup) + upb_ref[...]
    d_act = dot(gy_ref[...], wdn) + dot(edn_ref[...], adn)
    bent = (0.5 * GELU_SCALE) * pre
    turn = jnp.tanh(bent)
    q = 0.5 + 0.5 * turn
    act = (pre * q).astype(BF16)
    d_up = (d_act * (q + q * (bent * (1.0 - turn)))).astype(BF16)
    down_acc[...] += dot(act, wdn, NT)
    dz_acc[...] += dot(d_up, wup, NT)
    udn_acc[...] += dot(act, adn, NT)
    eup_acc[...] += dot(d_up, bup, NT)
    hidden_half = parts * chunk
    for i, (low, high) in enumerate(((uup_t, d_up), (edn_t, act))):
        found = split_rows(place, dot(low[...], high).astype(BF16))
        lanes = pl.ds(pl.multiple_of(i * hidden_half + step % parts * chunk, chunk), chunk)
        ekeep_ref[y, :, lanes], esend_ref[y, :, lanes] = found

    @pl.when(step == pl.num_programs(0) - 1)
    def _():
        fetch.wait()
        gbdn = gaup = 0.0
        for b in blocks:
            sel = sel_ref[b, :]
            e_up = (eup_acc[b, :] * sel).astype(BF16)
            u_dn = (udn_acc[b, :] * sel).astype(BF16)
            hidden = hid_buf[b, :]
            y = hidden + down_acc[b, :] + dot(u_dn, bdn_ref[...]) + dnb_ref[...]
            halves_out(place, y.astype(BF16), b, own_ref, near_ref, far_ref)
            dz = dz_acc[b, :] + dot(e_up, aup_ref[...], NT)
            normal, inverse = norm_of(hidden)
            grad = gy_ref[b, :].astype(F32) + norm_pull(dz, normal, inverse, gain[...])
            ghb_ref[b, :] = grad.astype(BF16)
            gbdn = gbdn + dot_rows(u_dn, gy_ref[b, :])
            gaup = gaup + dot_rows(e_up, z_ref[b, :])
        half = width // 2
        for i, grad in enumerate((gaup, gbdn)):
            start = 2 * hidden_half + i * half
            for column in range(2):
                rows = split_rows(place, grad[:, column * half : (column + 1) * half].astype(BF16))
                lanes = slice(start, start + half)
                ekeep_ref[column, :, lanes], esend_ref[column, :, lanes] = rows


def split_rows(place, grad):
    part = grad.shape[0] // 2
    low, high = grad[:part], grad[part:]
    return chosen(place[2], low, high), chosen(place[2], high, low)


def out_back_body(
    place, g_ref, own_ref, keep_ref, mate_ref, r0, r1, r2, r3, a_ref, b_ref, sel_ref, u_ref,
    d_own, d_keep, d_send, g_keep, g_send, w_ref, e_ref, e_t,
):
    width = g_ref.shape[1]
    half = width // 2
    count = keep_ref.shape[0]
    y = pl.program_id(0)

    @pl.when(y == 0)
    def _():
        def store(row, column, block):
            w_ref[column, row] = block

        settle(place, (r0, r1, r2, r3), True, store)
        e = (dot(g_ref[...], b_ref[...], NT) * sel_ref[...]).astype(BF16)
        e_ref[...] = e
        e_t[...] = e.T
        gb = dot(u_ref[...].T, g_ref[...]).astype(BF16)
        for column in range(2):
            rows = split_rows(place, gb[:, column * half : (column + 1) * half])
            g_keep[column, :, half:], g_send[column, :, half:] = rows

    w = w_ref[y].reshape(width, half)
    d = (dot(g_ref[...], w) + dot(e_ref[...], a_ref[0])).astype(BF16)
    d_own[...] = d[: 2 * count]

    shared = jnp.where(place[2] == y, keep_ref[...], mate_ref[...])
    ga = dot(e_t[...], jnp.concatenate([own_ref[...], shared])).astype(BF16)
    g_keep[y, :, :half], g_send[y, :, :half] = split_rows(place, ga)

    @pl.when(place[2] == y)
    def _():
        d_keep[...] = d[2 * count :]

    @pl.when(place[2] != y)
    def _():
        d_send[...] = d[2 * count :]


def shared_halves(place, keep, mate):
    return chosen(place[2], keep, mate), chosen(place[2], mate, keep)


def qkv_grads_body(
    place, left_ref, right_ref, keep_ref, mate_ref, b_ref, sel_ref, u_ref, z_ref, e_ref,
    keep_out, send_out,
):
    half = left_ref.shape[2]
    part = sel_ref.shape[1] // 2
    shared = shared_halves(place, keep_ref[0], mate_ref[0])
    u_t = u_ref[...].T

    def put(grad, y, i):
        low, high = grad[:part], grad[part:]
        keep_out[y, i, 0] = chosen(place[2], low, high)
        send_out[y, i, 0] = chosen(place[2], high, low)

    low = 0.0
    for y, own_ref in enumerate((left_ref, right_ref)):
        d = jnp.concatenate([own_ref[0], shared[y]])
        low = low + dot(d, b_ref[y], NT)
        put(dot(u_t, d).astype(BF16), y, 0)
    e = (low * sel_ref[...]).astype(BF16)
    e_ref[...] = e
    ga = dot(e.T, z_ref[...]).astype(BF16)
    for y in range(2):
        put(ga[:, y * half : (y + 1) * half], y, 1)


def qkv_back_body(
    shared, place, left_ref, right_ref, p0, p1, p2, p3, r0, r1, r2, r3, a_ref, e_ref, x_ref,
    gh_ref, gain, own_out, near_out, far_out, w_ref,
):
    width = x_ref.shape[1]
    settle_qkv(place, (p0, p1, p2, p3), (r0, r1, r2, r3), w_ref)
    dz = dot(e_ref[...], a_ref[...], NT)
    for k in range(3):
        left, right = left_ref[k], right_ref[k]
        if shared:
            left, right = shared_halves(place, left, right)
        d = jnp.concatenate([left, right], axis=1)
        dz = dz + dot(d, w_ref[k].reshape(width, width), NT)
    normal, inverse = norm_of(x_ref[...].astype(F32))
    grad = gh_ref[...].astype(F32) + norm_pull(dz, normal, inverse, gain[...])
    halves_out(place, grad.astype(BF16), slice(None), own_out, near_out, far_out)


def on_chip_pair(
    mesh_shape, tokens, cotangent, ln1_gain, ln1_bias, ln2_gain, ln2_bias, w_qkv, qv_bias, w_out,
    out_bias, w_up, up_bias, w_down, down_bias, adapter_ids, a_qkv, b_qkv, a_out, b_out, a_up,
    b_up, a_down, b_down,
):
    n_row, n_col = mesh_shape
    count, half = tokens.shape
    width = half * 2
    stack = b_out.shape[0]
    part = stack // 2
    hidden_half = w_up.shape[1]
    hidden = hidden_half * 2
    length = count // adapter_ids.shape[0]
    cut = length // 2
    heads = width // HD
    tb = -(-(length + 1) // 32) * 16
    own_rows, total = 2 * tb, 3 * tb
    scale = HD ** (-0.5)
    both = ("row", "col")
    row, col = lax.axis_index("row"), lax.axis_index("col")
    core, side, n_far = row % 2, row // 2 % 2, n_row // 4
    place = jnp.stack([row // 4, side, core, col]).astype(jnp.int32)

    def device(r, c):
        return r * n_col + c

    far_swaps = [[] for _ in range(n_far.bit_length() - 1)]
    far_turns = [[] for _ in range(n_far - 1)]
    ring_in, ring_back, cross, cores, cols_swap, sides_swap = [], [], [], [], [], []
    for r in range(n_row):
        for c in range(n_col):
            k, mate = r % 2, r + 1 - 2 * (r % 2)
            cores.append((device(r, c), device(mate, c)))
            cols_swap.append((device(r, c), device(r, 1 - c)))
            sides_swap.append((device(r, c), device(r ^ 2, c)))
            for turn, pairs in enumerate(far_turns):
                pairs.append((device(r, c), device((r + 4 * (turn + 1)) % n_row, c)))
            for bit, pairs in enumerate(far_swaps):
                pairs.append((device(r, c), device(r ^ (4 << bit), c)))
            if k != c:
                ring_in.append((device(r, c), device(r, 1 - c)))
                ring_back.append((device(r, c), device(mate, c)))
                cross.append((device(r, c), device(mate, 1 - c)))
            else:
                ring_in.append((device(r, c), device(mate, c)))
                ring_back.append((device(r, c), device(r, 1 - c)))

    def move(values, pairs):
        return lax.ppermute(values, both, pairs)

    def pick(pair, index):
        return jnp.where(index == 0, pair[0], pair[1])

    def ordered(mine, other, index, axis):
        return jnp.where(
            index == 0,
            jnp.concatenate([mine, other], axis),
            jnp.concatenate([other, mine], axis),
        )

    def tie(*values):
        return lax.optimization_barrier(values)

    thirds = [struct((total, half), BF16)] * 3
    third_specs = [fixed((total, half))] * 3

    def spread(values):
        return call(
            functools.partial(spread_body, length, cut, own_rows, tb),
            (1,),
            [SPOT, fixed((count, half))],
            third_specs,
            thirds,
            scratch=[pltpu.VMEM((count, half), F32)],
        )(place, values)

    def join(own, near, far, kind):
        return call(
            functools.partial(join_body, length, cut, own_rows, len(own)),
            (1,),
            [SPOT] + [fixed(t.shape) for t in (*own, *near, *far)],
            fixed((count, half)),
            struct((count, half), kind),
            scratch=[pltpu.VMEM((count, half), F32)],
        )(place, *own, *near, *far)

    x_own, x_near, x_far = spread(tokens)
    x_near, x_far, w_qkv, w_out = tie(x_near, x_far, w_qkv, w_out)
    mine_first = jnp.concatenate(
        [jnp.swapaxes(w_qkv, 0, 1).reshape(-1, 3 * half), w_out.T], axis=1
    )
    mine_second = jnp.concatenate([w_up, w_down.T], axis=1)
    adapt_first = jnp.concatenate(
        [jnp.swapaxes(b_qkv, 0, 1).reshape(stack, 3 * half), a_out.T], axis=1
    )
    adapt_second = jnp.concatenate([b_up, a_down.T], axis=1)
    deep = width // n_row

    def turned(block):
        return jnp.stack([block] + [move(block, pairs) for pairs in far_turns])

    def doubled(found, pairs):
        return jnp.concatenate([found, move(found, pairs)])

    def part_of(values):
        return lax.dynamic_slice_in_dim(values, core * part, part, 0)

    def widened(values, near, far):
        return ordered(values[None], ordered(near, far, core, 0)[None], col, 0)

    x_near, x_far = move(x_near, ring_in), move(x_far, cross)
    near0, near1 = turned(mine_first[:, :width]), turned(mine_first[:, width:])
    near0, x_near, x_far, mine_second = tie(near0, x_near, x_far, mine_second)
    near0, near1 = tie(near0, near1)
    x_parts = (x_own, x_near, x_far)
    big_second = lax.all_gather(mine_second, both, axis=0, tiled=False)
    big_second = big_second.reshape(n_row, n_col, deep, 2 * hidden_half)
    near0, near1 = doubled(near0, sides_swap), doubled(near1, cols_swap)
    ad_near = move(part_of(adapt_first), cols_swap)
    biases = jnp.concatenate([qv_bias[0], qv_bias[1], up_bias])[None]
    bias_pair = ordered(biases, move(biases, cols_swap), col, 0)
    ids = jnp.where(core == col, adapter_ids, move(adapter_ids, cores))
    g_own, g_near, g_far = spread(cotangent)
    near0, near1, bias_pair, ids, ad_near = tie(near0, near1, bias_pair, ids, ad_near)
    ad_first = widened(adapt_first, ad_near, move(ad_near, cores))
    last0, last1 = move(near0, cols_swap), move(near1, sides_swap)
    far0, far1 = move(near0, cores), move(near1, cores)
    adapt_part = part_of(adapt_second)
    valid = jnp.arange(own_rows)[:, None]
    here, there = jnp.where(core == 0, cut, length - cut), jnp.where(core == 0, length - cut, cut)

    def mask_of(good):
        return jnp.broadcast_to(jnp.where(good, 0.0, -1e30), (own_rows, 2 * HD)).astype(BF16)

    mask_own = mask_of(valid < length)
    mask_shared = mask_of((valid < here) | ((valid >= tb) & (valid < tb + there)))
    last0, last1, far0, far1, ad_first, g_near, g_far = tie(
        last0, last1, far0, far1, ad_first, g_near, g_far
    )
    last0, adapt_part, adapt_second, mask_own, mask_shared = tie(
        last0, adapt_part, adapt_second, mask_own, mask_shared
    )
    ad_near = move(adapt_part, cols_swap)
    blocks0 = (near0, last0, far0, move(last0, cores))
    blocks1 = (near1, last1, far1, move(last1, cores))
    qv_rows = jnp.stack(
        [
            bias_pair[:, :half].reshape(1, width),
            jnp.zeros((1, width), F32),
            bias_pair[:, half:width].reshape(1, width),
        ]
    )
    up_row = bias_pair[:, width:].reshape(1, hidden)

    owners = lax.iota(jnp.int32, stack) // RANK
    own_id = jnp.where(core == 0, ids[0], ids[2])
    places = lax.iota(jnp.int32, total)[:, None]
    sel = (jnp.where(places < own_rows, own_id, ids[1]) == owners[None]).astype(F32)

    gain1, bias1, gain2, bias2 = (t[None] for t in (ln1_gain, ln1_bias, ln2_gain, ln2_bias))

    rows_block = pl.BlockSpec((tb, width), lambda i: (i, 0))
    sel_block = pl.BlockSpec((tb, stack), lambda i: (i, 0))
    every = fixed((total, width))
    thin = fixed((total, stack))
    vec = fixed((1, width))
    pieces0 = [fixed((n_row // 2, deep, width))] * 4
    pieces1 = [fixed((n_row // 2, deep, half))] * 4
    pieces_out = [
        pl.BlockSpec(
            (n_row // 2, deep, half), lambda *_: (0, 0, 1), pipeline_mode=pl.Buffered(1)
        )
    ] * 4
    w_qkv_room = [pltpu.VMEM((3, n_row, deep, width), BF16)]
    w_out_room = [pltpu.VMEM((n_row, deep, width), BF16)]
    ad_out_spec = pl.BlockSpec(
        (n_col, stack, half), lambda *_: (0, 0, 3), pipeline_mode=pl.Buffered(1)
    )
    low_k = pl.BlockSpec((total, stack), lambda k: (0, k))
    shared_k = pl.BlockSpec((1, tb, half), lambda k: (k, 0, 0))
    ad_k = pl.BlockSpec((n_col, stack, half), lambda k: (0, 0, k))
    shared_struct = struct((3, tb, half), BF16)
    half_rows = struct((tb, half), BF16)

    third_rows = pl.BlockSpec((tb, half), lambda i: (i, 0))
    low_block = pl.BlockSpec((tb, 3 * stack), lambda i: (i, 0))
    all_three = pl.BlockSpec((3, tb, width), lambda i: (0, i, 0))
    shared_three = fixed((3, tb, half))
    x, z1, u_qkv, qkv, qkv_keep, qkv_send = call(
        functools.partial(qkv_body, scale),
        (3,),
        [
            SPOT, third_rows, third_rows, third_rows, vec, vec, *pieces0, *pieces1,
            fixed((width, 3 * stack)),
            pl.BlockSpec(
                (n_col, stack, 3 * half), lambda i: (0, 0, 0), pipeline_mode=pl.Buffered(1)
            ),
            fixed((3, 1, width)), sel_block,
        ],
        [rows_block, rows_block, low_block, all_three, shared_three, shared_three],
        [
            struct((total, width), BF16),
            struct((total, width), BF16),
            struct((total, 3 * stack), BF16),
            struct((3, total, width), BF16),
            shared_struct,
            shared_struct,
        ],
        scratch=w_qkv_room,
    )(place, *x_parts, gain1, bias1, *blocks0, *blocks1, a_qkv, ad_first, qv_rows, sel)

    qkv_mate = move(qkv_send, cores)
    qkv, g_near, g_far = tie(qkv, g_near, g_far)
    g_near, g_far = move(g_near, ring_in), move(g_far, cross)

    head_p = pl.BlockSpec((2, own_rows, own_rows), lambda h: (h, 0, 0))
    pair_k = pl.BlockSpec((3, tb, 2 * HD), lambda h: (0, 0, h))
    pair_rows = pl.BlockSpec((tb, 2 * HD), lambda h: (0, h))
    wide = 4 * HD
    att_own, p_own = call(
        attend_body,
        (width // wide,),
        [pl.BlockSpec((1, own_rows, wide), lambda h, k=k: (k, 0, h)) for k in range(3)]
        + [fixed((own_rows, 2 * HD))],
        [
            pl.BlockSpec((own_rows, wide), lambda h: (0, h)),
            pl.BlockSpec((4, own_rows, own_rows), lambda h: (h, 0, 0)),
        ],
        [struct((own_rows, width), BF16), struct((heads, own_rows, own_rows), BF16)],
    )(qkv, qkv, qkv, mask_own)
    qkv_mate, att_own = tie(qkv_mate, att_own)
    wide_k = pl.BlockSpec((3, tb, wide), lambda h: (0, 0, h))
    wide_rows = pl.BlockSpec((tb, wide), lambda h: (0, h))
    att_keep, att_send, p_sh = call(
        attend_shared_body,
        (half // wide,),
        [wide_k, wide_k, fixed((own_rows, 2 * HD))],
        [wide_rows, wide_rows, pl.BlockSpec((4, own_rows, own_rows), lambda h: (h, 0, 0))],
        [half_rows, half_rows, struct((heads // 2, own_rows, own_rows), BF16)],
    )(qkv_keep, qkv_mate, mask_shared)
    att_send, ad_near = tie(att_send, ad_near)
    att_mate = move(att_send, cores)
    g_parts = (g_own, g_near, g_far)
    ad_second = (adapt_second, ad_near, move(ad_near, cores))

    own_block = pl.BlockSpec((tb, width), lambda i: (jnp.minimum(i, 1), 0))
    shared_rows = fixed((tb, half))
    hid, z2, u_out, u_up = call(
        out_body,
        (3,),
        [
            SPOT, own_block, shared_rows, shared_rows, rows_block, *pieces_out,
            ad_out_spec, fixed((stack, width)), vec, vec, vec, fixed((width, stack)), sel_block,
        ],
        [rows_block, rows_block, sel_block, sel_block],
        [
            struct((total, width), F32),
            struct((total, width), BF16),
            struct((total, stack), BF16),
            struct((total, stack), BF16),
        ],
        scratch=w_out_room,
    )(
        place, att_own, att_keep, att_mate, x, *blocks1, ad_first, b_out, out_bias[None],
        gain2, bias2, a_up, sel,
    )

    chunk = half
    parts = hidden_half // chunk

    def w_spec(shift):
        return pl.BlockSpec(
            (n_row, 1, deep, chunk), lambda j: (0, j // parts, 0, j % parts + shift)
        )

    def ad_specs(shift):
        return [
            pl.BlockSpec((rows, chunk), lambda j: (0, j % parts + shift))
            for rows in (stack, part, part)
        ]

    early_half = fixed((2, part, 2 * hidden_half + 2 * half))
    early_struct = struct((2, part, 2 * hidden_half + 2 * half), BF16)
    y_own, y_near, y_far, ghb, early_keep, early_send = call(
        functools.partial(mlp_body, tb),
        (2 * parts,),
        [SPOT, every]
        + third_specs
        + [
            thin, thin, pl.BlockSpec(memory_space=pl.ANY), w_spec(0), w_spec(parts), *ad_specs(0), *ad_specs(parts),
            pl.BlockSpec((1, chunk), lambda j: (0, j)), fixed((stack, width)),
            fixed((width, stack)), vec, vec,
        ],
        third_specs + [every, early_half, early_half],
        thirds
        + [struct((total, width), BF16), early_struct, early_struct],
        scratch=[
            pltpu.VMEM((total, width), F32),
            pltpu.VMEM((total, width), F32),
            pltpu.VMEM((total, stack), F32),
            pltpu.VMEM((total, stack), F32),
            pltpu.VMEM((total, stack), BF16),
            pltpu.VMEM((stack, total), BF16),
            pltpu.VMEM((stack, total), BF16),
            pltpu.VMEM((total, width), BF16),
            pltpu.VMEM((total, width), F32),
            pltpu.SemaphoreType.DMA,
        ],
    )(
        place, z2, *g_parts, u_up, sel, hid, big_second, big_second, *ad_second, *ad_second, up_row,
        b_down, a_up, down_bias[None], gain2,
    )

    def added(kept, sent):
        return (kept.astype(F32) + sent.astype(F32)).astype(BF16)

    quarter = part // 2

    def quarter_of(values, index):
        return lax.dynamic_slice_in_dim(values, index * quarter, quarter, 1)

    def side_sent(values):
        return move(quarter_of(values, 1 - side), sides_swap)

    early_sent = move(early_send, cores)
    y_near, y_far = move(y_near, ring_back), move(y_far, cross)
    out_half = fixed((2, part, width))
    d_att, d_keep, d_send, out_keep, out_send = call(
        out_back_body,
        (2,),
        [
            SPOT, every, pl.BlockSpec((own_rows, half), lambda i: (0, i)), shared_rows,
            shared_rows, *pieces_out,
            pl.BlockSpec((1, stack, half), lambda i: (i, 0, 3)), fixed((stack, width)), thin, thin,
        ],
        [
            pl.BlockSpec((own_rows, half), lambda i: (0, i)), shared_rows, shared_rows, out_half,
            out_half,
        ],
        [
            struct((own_rows, width), BF16),
            half_rows,
            half_rows,
            struct((2, part, width), BF16),
            struct((2, part, width), BF16),
        ],
        scratch=[
            pltpu.VMEM((2, n_row, deep, half), BF16),
            pltpu.VMEM((total, stack), BF16),
            pltpu.VMEM((stack, total), BF16),
        ],
    )(place, ghb, att_own, att_keep, att_mate, *blocks1, ad_first, b_out, sel, u_out)

    d_mate = move(d_send, cores)
    early_sum = jnp.concatenate(
        [added(early_keep, early_sent), added(out_keep, move(out_send, cores))], axis=2
    )
    d_mate, early_sum = tie(d_mate, early_sum)
    early_sent = side_sent(early_sum)

    g_keep, g_send = call(
        functools.partial(attend_back_shared_body, scale),
        (heads // 4,),
        [pair_k, pair_k, head_p, pair_rows, pair_rows, pair_rows, pair_rows],
        [pair_k, pair_k],
        [shared_struct, shared_struct],
        us=8,
    )(qkv_keep, qkv_mate, p_sh, att_keep, att_send, d_keep, d_mate)
    d_att, g_send = tie(d_att, g_send)
    g_mate = move(g_send, cores)
    quarters = heads // 4

    def own_back(shift, d_out):
        return call(
            functools.partial(attend_back_body, scale),
            (quarters,),
            [
                pl.BlockSpec((1, own_rows, 2 * HD), lambda h, k=k: (k, 0, h + shift))
                for k in range(3)
            ]
            + [
                pl.BlockSpec((2, own_rows, own_rows), lambda h: (h + shift, 0, 0)),
                pl.BlockSpec((own_rows, 2 * HD), lambda h: (0, h + shift)),
                pl.BlockSpec((own_rows, 2 * HD), lambda h: (0, h + shift)),
            ],
            pl.BlockSpec((3, own_rows, 2 * HD), lambda h: (0, 0, h)),
            struct((3, own_rows, half), BF16),
            us=9,
        )(qkv, qkv, qkv, p_own, att_own, d_out)

    d_left = own_back(0, d_att)
    early_sum = added(quarter_of(early_sum, side), early_sent)
    d_left, d_att, early_sum, y_near, y_far = tie(d_left, d_att, early_sum, y_near, y_far)
    early_sent = move(pick(early_sum, 1 - col), cols_swap)
    d_right = own_back(quarters, d_att)

    grad_spec = pl.BlockSpec((2, 2, 1, part, half), lambda k: (0, 0, k, 0, 0))
    grad_struct = struct((2, 2, 3, part, half), BF16)
    early_sum = added(pick(early_sum, col), early_sent)
    d_right, early_sum = tie(d_right, early_sum)
    early_sent = move(early_sum, far_swaps[0])
    half_k = pl.BlockSpec((1, own_rows, half), lambda k: (k, 0, 0))
    e_qkv, q_kept, q_sent = call(
        qkv_grads_body,
        (3,),
        [SPOT, half_k, half_k, shared_k, shared_k, ad_k, thin, low_k, every],
        [low_k, grad_spec, grad_spec],
        [struct((total, 3 * stack), BF16), grad_struct, grad_struct],
        us=7,
    )(place, d_left, d_right, g_keep, g_mate, ad_first, sel, u_qkv, z1)

    def side_of(values, index):
        return jnp.where(index == 0, values[:, 0], values[:, 1])

    sums = added(q_kept, move(q_sent, cores)).reshape(2, 2, 3 * part, half)
    early_sum = added(early_sum, early_sent)
    sums, e_qkv, early_sum = tie(sums, e_qkv, early_sum)
    early_sent = move(early_sum, far_swaps[-1])
    q_sent = move(side_of(sums, 1 - side), sides_swap)

    def token_rows(block, left, right):
        at = block % 2
        d_spec = pl.BlockSpec((3, tb, half), lambda i: (0, at, 0), pipeline_mode=pl.Buffered(1))
        rows = pl.BlockSpec((tb, width), lambda i: (block, 0), pipeline_mode=pl.Buffered(1))
        low = pl.BlockSpec((tb, 3 * stack), lambda i: (block, 0), pipeline_mode=pl.Buffered(1))
        return call(
            functools.partial(qkv_back_body, block == 2),
            (1,),
            [
                SPOT, d_spec, d_spec, *pieces0, *pieces1, fixed((width, 3 * stack)), low, rows,
                rows, vec,
            ],
            [shared_rows] * 3,
            [half_rows] * 3,
            scratch=w_qkv_room,
            us=6,
        )(place, left, right, *blocks0, *blocks1, a_qkv, e_qkv, x, ghb, gain1)

    t_own, t_near, t_far = [], [], []

    def sent_rows(own, near, far):
        t_own.append(own)
        t_near.append(move(near, ring_back))
        t_far.append(move(far, cross))

    rows_own, rows_near, rows_far = token_rows(0, d_left, d_right)
    q_sent, rows_near, rows_far = tie(q_sent, rows_near, rows_far)
    sums = added(side_of(sums, side), q_sent)
    sums, d_left, d_right = tie(sums, d_left, d_right)
    q_sent = move(pick(sums, 1 - col), cols_swap)
    sent_rows(rows_own, rows_near, rows_far)
    rows_own, rows_near, rows_far = token_rows(1, d_left, d_right)
    q_sent, rows_near, rows_far, early_sent = tie(q_sent, rows_near, rows_far, early_sent)
    early_sum = added(early_sum, early_sent)
    sums = added(pick(sums, col), q_sent)
    sums, g_keep, g_mate = tie(sums, g_keep, g_mate)
    q_sent = move(sums, far_swaps[1])
    sent_rows(rows_own, rows_near, rows_far)
    edge = 2 * hidden_half
    whole = edge + 4 * half
    split_lanes = [slice(edge, edge + 2 * half), slice(edge + 3 * half, whole)]
    rest = jnp.concatenate([early_sum[:, lanes] for lanes in split_lanes], axis=1)
    rest = move(rest, cols_swap)
    rows_own, rows_near, rows_far = token_rows(2, g_keep, g_mate)
    early_sum = jnp.concatenate([early_sum, rest], axis=1)
    q_sent, rows_near, rows_far, early_sum, y_own, t_near[0], t_far[0] = tie(
        q_sent, rows_near, rows_far, early_sum, y_own, t_near[0], t_far[0]
    )
    sums = added(sums, q_sent)
    q_sent = move(sums, far_swaps[0])
    sent_rows(rows_own, rows_near, rows_far)
    early_sent = move(early_sum, sides_swap)
    layer_out = join([y_own], [y_near], [y_far], BF16)
    early_sum = ordered(early_sum, early_sent, side, 0)
    q_sent, early_sum, layer_out, t_near[1], t_far[1] = tie(
        q_sent, early_sum, layer_out, t_near[1], t_far[1]
    )
    early_sent = move(early_sum, cores)
    sums = added(sums, q_sent)
    for pairs in far_swaps[2:]:
        sums = added(sums, move(sums, pairs))
    side_sums = move(sums, sides_swap)
    mine = ordered(early_sum, early_sent, core, 0)
    side_sums, t_near[2], t_far[2], mine = tie(side_sums, t_near[2], t_far[2], mine)
    tokens_grad = join(t_own, t_near, t_far, F32)
    mine = mine.astype(F32)
    sums = ordered(sums[None], side_sums[None], side, 0)
    a_sent = move(sums[1:], cols_swap)
    own_starts = (edge, edge + half, edge + 3 * half)
    a_up_sum, b_down_sum, b_out_sum = (
        ordered(
            mine[:, start : start + half],
            mine[:, whole + i * half : whole + (i + 1) * half],
            col,
            1,
        )
        for i, start in enumerate(own_starts)
    )
    a_out_sum, a_up_sum = mine[:, edge + 2 * half : edge + 3 * half].T, a_up_sum.T
    b_up_sum, a_down_sum = mine[:, :hidden_half], mine[:, hidden_half:edge].T
    a_sent, tokens_grad, a_out_sum, a_up_sum, b_up_sum, a_down_sum, b_down_sum, b_out_sum = tie(
        a_sent, tokens_grad, a_out_sum, a_up_sum, b_up_sum, a_down_sum, b_down_sum, b_out_sum
    )
    every_sum = jnp.concatenate([sums[:1], ordered(sums[1:], a_sent, col, 0)])
    every_sum = every_sum.reshape(3, 3, part, half)
    every_sum = ordered(every_sum, move(every_sum, cores), core, 2).reshape(3, 3 * stack, half)
    b_sum = every_sum[0].reshape(3, stack, half).astype(F32)
    a_sum = jnp.concatenate([every_sum[1].T, every_sum[2].T]).astype(F32)
    return (
        layer_out,
        tokens_grad,
        a_sum,
        b_sum,
        a_out_sum,
        b_out_sum,
        a_up_sum,
        b_up_sum,
        a_down_sum,
        b_down_sum,
    )


def solution(mesh):
    placed = (
        P("row", "col"),
        P("row", "col"),
        P(),
        P(),
        P(),
        P(),
        P(None, "row", "col"),
        P(None, "col"),
        P("col", "row"),
        P(),
        P("row", "col"),
        P("col"),
        P("col", "row"),
        P(),
        P("row"),
        P(),
        P(None, None, "col"),
        P("col", None),
        P(),
        P(),
        P(None, "col"),
        P("col", None),
        P(),
    )
    shape = (mesh.shape["row"], mesh.shape["col"])
    paired = shape[1] == 2 and shape[0] >= 16 and shape[0] & (shape[0] - 1) == 0
    return jax.shard_map(
        functools.partial(on_chip_pair, shape) if paired else on_device,
        mesh=mesh,
        in_specs=placed,
        out_specs=(
            P("row", "col"),
            P("row", "col"),
            P(),
            P(None, None, "col"),
            P("col", None),
            P(),
            P(),
            P(None, "col"),
            P("col", None),
            P(),
        ),
        check_vma=False,
    )
```

```python
import functools

import jax
import jax.numpy as jnp
from jax import lax
from jax.experimental import pallas as pl
from jax.experimental.pallas import tpu as pltpu
from jax.sharding import PartitionSpec as P

HD = 64
RANK = 16


EPS = 1e-05
GELU_SCALE = 1.702


def column_sums(first, second):
    return lax.psum((first, second), "col")


def gather_features(values):
    return lax.all_gather(values, "col", axis=1, tiled=True)


def sum_partials(terms):
    return lax.psum_scatter(
        terms.astype(jnp.bfloat16), "col", scatter_dimension=1, tiled=True
    ).astype(jnp.float32)


def norm_split(values, feature_width):
    first, second = column_sums(jnp.sum(values, axis=1), jnp.sum(values * values, axis=1))
    centre = first / feature_width
    inverse = lax.rsqrt(second / feature_width - centre * centre + EPS)
    return ((values - centre[:, None]) * inverse[:, None], inverse)


def norm_back(grad_normed, normal_rows, inverse, gain_part, feature_width):
    scaled = grad_normed * gain_part
    first, second = column_sums(jnp.sum(scaled, axis=1), jnp.sum(scaled * normal_rows, axis=1))
    return inverse[:, None] * (
        scaled - first[:, None] / feature_width - normal_rows * second[:, None] / feature_width
    )


def select_rows(low_rank, onehot, image_len):
    image_count, stack_width = onehot.shape
    shaped = low_rank.reshape(image_count, image_len, -1, stack_width)
    return (shaped * onehot[:, None, None, :]).reshape(low_rank.shape).astype(jnp.bfloat16)


def mult(form, first, second):
    return jnp.einsum(form, first, second, preferred_element_type=jnp.float32)


def on_device(
    tokens,
    cotangent,
    ln1_gain,
    ln1_bias,
    ln2_gain,
    ln2_bias,
    w_qkv,
    qv_bias,
    w_out,
    out_bias,
    w_up,
    up_bias,
    w_down,
    down_bias,
    adapter_ids,
    a_qkv,
    b_qkv,
    a_out,
    b_out,
    a_up,
    b_up,
    a_down,
    b_down,
):
    row_count, part_width = tokens.shape
    feature_width = a_qkv.shape[0]
    stack_width = a_qkv.shape[1] // 3
    image_count = adapter_ids.shape[0]
    image_len = row_count // image_count
    head_count = part_width // HD
    scale = HD ** (-0.5)
    offset = lax.axis_index("col") * part_width

    def own_part(values, axis):
        return lax.dynamic_slice_in_dim(values, offset, part_width, axis)

    owners = lax.iota(jnp.int32, stack_width) // RANK
    onehot = (adapter_ids[:, None] == owners[None, :]).astype(jnp.float32)
    wide_qkv, wide_out, wide_up, wide_down = (
        lax.all_gather(w_qkv, "row", axis=1, tiled=True),
        lax.all_gather(w_out, "row", axis=1, tiled=True),
        lax.all_gather(w_up, "row", axis=0, tiled=True),
        lax.all_gather(w_down, "row", axis=1, tiled=True),
    )
    inputs = tokens.astype(jnp.float32)
    normal_one, inverse_one = norm_split(inputs, feature_width)
    normed_part = (normal_one * own_part(ln1_gain, 0) + own_part(ln1_bias, 0)).astype(jnp.bfloat16)
    normed_one = gather_features(normed_part)
    projected = mult("td,kde->kte", normed_one, wide_qkv)
    kept_qkv = select_rows(mult("td,dj->tj", normed_one, a_qkv), onehot, image_len)
    projected = projected + mult("tkj,kje->kte", kept_qkv.reshape(row_count, 3, stack_width), b_qkv)
    bias_rows = jnp.stack([qv_bias[0], jnp.zeros_like(qv_bias[0]), qv_bias[1]])[:, None, :]
    qkv = (projected + bias_rows).astype(jnp.bfloat16)
    shaped = qkv.reshape(3, image_count, image_len, head_count, HD)
    queries, key_rows, value_rows = (shaped[0], shaped[1], shaped[2])
    scores = mult("bqhd,bkhd->bhqk", queries, key_rows) * scale
    highest = jnp.max(scores, axis=-1, keepdims=True)
    log_total = highest + jnp.log(jnp.sum(jnp.exp(scores - highest), axis=-1, keepdims=True))
    weights_low = jnp.exp(scores - log_total).astype(jnp.bfloat16)
    attended = mult("bhqk,bkhd->bqhd", weights_low, value_rows)
    attended = attended.reshape(row_count, part_width).astype(jnp.bfloat16)
    kept_out = select_rows(mult("tc,cj->tj", attended, a_out), onehot, image_len)
    out_terms = mult("tc,cd->td", attended, wide_out) + mult("tj,jd->td", kept_out, b_out)
    hidden = inputs + sum_partials(out_terms) + own_part(out_bias, 0)
    normal_two, inverse_two = norm_split(hidden, feature_width)
    normed_part_two = (normal_two * own_part(ln2_gain, 0) + own_part(ln2_bias, 0)).astype(
        jnp.bfloat16
    )
    normed_two = gather_features(normed_part_two)
    kept_up = select_rows(mult("td,dj->tj", normed_two, a_up), onehot, image_len)
    pre_up = mult("td,df->tf", normed_two, wide_up) + mult("tj,jf->tf", kept_up, b_up) + up_bias
    logistic = jax.nn.sigmoid(GELU_SCALE * pre_up)
    activated = (pre_up * logistic).astype(jnp.bfloat16)
    kept_down = select_rows(mult("tf,fj->tj", activated, a_down), onehot, image_len)
    down_terms = mult("tf,fd->td", activated, wide_down) + mult("tj,jd->td", kept_down, b_down)
    layer_out = (hidden + sum_partials(down_terms) + own_part(down_bias, 0)).astype(jnp.bfloat16)
    wide_qkv, wide_out, wide_up, wide_down = (
        lax.all_gather(w_qkv, "row", axis=1, tiled=True),
        lax.all_gather(w_out, "row", axis=1, tiled=True),
        lax.all_gather(w_up, "row", axis=0, tiled=True),
        lax.all_gather(w_down, "row", axis=1, tiled=True),
    )
    grad_layer = cotangent.astype(jnp.float32)
    grad_full = gather_features(cotangent)
    d_low_down = select_rows(mult("td,jd->tj", grad_full, b_down), onehot, image_len)
    d_activated = mult("td,fd->tf", grad_full, wide_down) + mult("tj,fj->tf", d_low_down, a_down)
    grad_b_down = mult("tj,td->jd", kept_down, grad_full)
    grad_a_down = mult("tf,tj->fj", activated, d_low_down)
    d_pre_up = (
        d_activated * (logistic + GELU_SCALE * pre_up * logistic * (1.0 - logistic))
    ).astype(jnp.bfloat16)
    d_low_up = select_rows(mult("tf,jf->tj", d_pre_up, b_up), onehot, image_len)
    grad_b_up = mult("tj,tf->jf", kept_up, d_pre_up)
    grad_a_up = mult("td,tj->dj", normed_two, d_low_up)
    normed_two_terms = mult("tf,df->td", d_pre_up, wide_up) + mult("tj,dj->td", d_low_up, a_up)
    d_normed_two = sum_partials(normed_two_terms)
    grad_hidden = grad_layer + norm_back(
        d_normed_two, normal_two, inverse_two, own_part(ln2_gain, 0), feature_width
    )
    hidden_full_grad = gather_features(grad_hidden.astype(jnp.bfloat16))
    d_low_out = select_rows(mult("td,jd->tj", hidden_full_grad, b_out), onehot, image_len)
    d_attended = mult("td,cd->tc", hidden_full_grad, wide_out) + mult("tj,cj->tc", d_low_out, a_out)
    grad_b_out = mult("tj,td->jd", kept_out, hidden_full_grad)
    grad_a_out = mult("tc,tj->cj", attended, d_low_out)
    d_heads = d_attended.astype(jnp.bfloat16).reshape(image_count, image_len, head_count, HD)
    scores_again = mult("bqhd,bkhd->bhqk", queries, key_rows) * scale
    weights_again = jnp.exp(scores_again - log_total)
    weights_again_low = weights_again.astype(jnp.bfloat16)
    d_weights = mult("bqhd,bkhd->bhqk", d_heads, value_rows)
    d_values = mult("bhqk,bqhd->bkhd", weights_again_low, d_heads)
    d_scores = weights_again * (
        d_weights - jnp.sum(weights_again * d_weights, axis=-1, keepdims=True)
    )
    d_scores = d_scores.astype(jnp.bfloat16)
    d_queries = scale * mult("bhqk,bkhd->bqhd", d_scores, key_rows)
    d_keys = scale * mult("bhqk,bqhd->bkhd", d_scores, queries)
    d_qkv = (
        jnp.stack([d_queries, d_keys, d_values])
        .reshape(3, row_count, part_width)
        .astype(jnp.bfloat16)
    )
    d_low_qkv = mult("kte,kje->tkj", d_qkv, b_qkv)
    d_low_qkv = select_rows(d_low_qkv.reshape(row_count, 3 * stack_width), onehot, image_len)
    grad_b_qkv = mult("tkj,kte->kje", kept_qkv.reshape(row_count, 3, stack_width), d_qkv)
    grad_a_qkv = mult("td,tj->dj", normed_one, d_low_qkv)
    normed_one_terms = mult("kte,kde->td", d_qkv, wide_qkv) + mult("tj,dj->td", d_low_qkv, a_qkv)
    d_normed_one = sum_partials(normed_one_terms)
    tokens_grad = grad_hidden + norm_back(
        d_normed_one, normal_one, inverse_one, own_part(ln1_gain, 0), feature_width
    )
    grad_a_qkv, grad_b_out, grad_a_up, grad_b_down = lax.psum(
        (grad_a_qkv, grad_b_out, grad_a_up, grad_b_down), ("row", "col")
    )
    grad_b_qkv, grad_a_out, grad_b_up, grad_a_down = (
        lax.psum(grad_b_qkv.astype(jnp.bfloat16), "row").astype(jnp.float32),
        lax.psum(grad_a_out.astype(jnp.bfloat16), "row").astype(jnp.float32),
        lax.psum(grad_b_up.astype(jnp.bfloat16), "row").astype(jnp.float32),
        lax.psum(grad_a_down.astype(jnp.bfloat16), "row").astype(jnp.float32),
    )
    return (
        layer_out,
        tokens_grad,
        grad_a_qkv,
        grad_b_qkv,
        grad_a_out,
        grad_b_out,
        grad_a_up,
        grad_b_up,
        grad_a_down,
        grad_b_down,
    )


NT = (((1,), (1,)), ((), ()))
NN = (((1,), (0,)), ((), ()))
F32 = jnp.float32
BF16 = jnp.bfloat16
VMEM_SMALL, VMEM_LARGE = 36 * 1024 * 1024, 60 * 1024 * 1024
SPOT = pl.BlockSpec(memory_space=pltpu.SMEM)


def dot(first, second, dims=NN):
    return lax.dot_general(first, second, dims, preferred_element_type=F32)


def dot_rows(first, second):
    return dot(first.T, second)


def call(body, grid, in_specs, out_specs, out_shape, scratch=(), us=None):
    return pl.pallas_call(
        body,
        grid=grid,
        in_specs=in_specs,
        out_specs=out_specs,
        out_shape=out_shape,
        scratch_shapes=list(scratch),
        compiler_params=pltpu.CompilerParams(
            dimension_semantics=("arbitrary",) * len(grid),
            vmem_limit_bytes=VMEM_LARGE if us is None else VMEM_SMALL,
        ),
        cost_estimate=None
        if us is None
        else pl.CostEstimate(
            flops=us * 900_000_000, bytes_accessed=1_000_000, transcendentals=0
        ),
    )


def fixed(shape):
    zeros = (0,) * len(shape)
    return pl.BlockSpec(shape, lambda *_: zeros, pipeline_mode=pl.Buffered(1))


def struct(shape, kind):
    return jax.ShapeDtypeStruct(shape, kind)


def norm_of(values):
    centred = values - jnp.mean(values, axis=1, keepdims=True)
    inverse = lax.rsqrt(jnp.mean(centred * centred, axis=1, keepdims=True) + EPS)
    return centred * inverse, inverse


def norm_pull(grad, normal, inverse, gain):
    scaled = grad * gain
    return inverse * (
        scaled
        - jnp.mean(scaled, axis=1, keepdims=True)
        - normal * jnp.mean(scaled * normal, axis=1, keepdims=True)
    )


def settle(place, pieces, side_first, store):
    depth = pieces[0].shape[0]
    n_far = depth // 2
    for group, piece in enumerate(pieces):
        for index in range(depth):
            other, outer, inner, back = (
                group // 2, group % 2, index // n_far, index % n_far
            )
            x_off, y_off = (outer, inner) if side_first else (inner, outer)
            far = lax.rem(place[0] + (n_far - back), n_far)
            x = place[1] if x_off == 0 else 1 - place[1]
            core = place[2] if other == 0 else 1 - place[2]
            y = place[3] if y_off == 0 else 1 - place[3]
            store(far * 4 + x * 2 + core, y, piece[index])


def settle_qkv(place, pieces0, pieces1, w_ref):
    half = pieces1[0].shape[2]

    def lanes(y):
        return pl.ds(pl.multiple_of(y * half, half), half)

    def first(row, y, block):
        w_ref[0, row, :, lanes(y)] = block[:, :half]
        w_ref[1, row, :, lanes(y)] = block[:, half:]

    def last(row, y, block):
        w_ref[2, row, :, lanes(y)] = block

    settle(place, pieces0, False, first)
    settle(place, pieces1, True, last)


def settle_out(place, pieces1, w_ref):
    half = pieces1[0].shape[2]

    def store(row, y, block):
        w_ref[row, :, pl.ds(pl.multiple_of(y * half, half), half)] = block

    settle(place, pieces1, True, store)


def chosen(index, first, second):
    return jnp.where(index == 0, first, second)


def both_halves(place, own, near, far):
    diagonal = place[2] == place[3]
    mine = jnp.where(diagonal, own, near)
    other = jnp.where(diagonal, near, far)
    return chosen(place[3], mine, other), chosen(place[3], other, mine)


def halves_out(place, values, rows, own_ref, near_ref, far_ref):
    half = values.shape[1] // 2
    left, right = values[:, :half], values[:, half:]
    mine, other = chosen(place[3], left, right), chosen(place[3], right, left)
    own_ref[rows, :] = mine
    near_ref[rows, :] = jnp.where(place[2] == place[3], other, mine)
    far_ref[rows, :] = other


def spread_body(length, cut, own_rows, tb, place, t_ref, own_ref, near_ref, far_ref, wide_ref):
    wide_ref[...] = t_ref[...].astype(F32)

    def put(ref, start, shared, shared_count):
        ref[:length, :] = wide_ref[start : start + length, :].astype(BF16)
        ref[own_rows : own_rows + shared_count, :] = wide_ref[
            shared : shared + shared_count, :
        ].astype(BF16)

    for ref, index in ((own_ref, place[2]), (near_ref, 1 - place[3]), (far_ref, 1 - place[2])):
        ref[...] = jnp.zeros_like(ref)

        @pl.when(index == 0)
        def _():
            put(ref, 0, length, cut)

        @pl.when(index == 1)
        def _():
            put(ref, 2 * length, length + cut, length - cut)


def join_body(length, cut, own_rows, pieces, place, *refs):
    *in_refs, out_ref, wide_ref = refs

    def whole(part):
        found = [ref[...] for ref in in_refs[part * pieces : (part + 1) * pieces]]
        return found[0] if pieces == 1 else jnp.concatenate(found)

    own, near, far = whole(0), whole(1), whole(2)
    diagonal = place[2] == place[3]
    mine = jnp.where(diagonal, own, near)
    mate = jnp.where(diagonal, near, far)
    first = chosen(place[2], mine, mate).astype(F32)
    second = chosen(place[2], mate, mine).astype(F32)
    wide_ref[:length, :] = first[:length]
    wide_ref[length : length + cut, :] = first[own_rows : own_rows + cut]
    wide_ref[length + cut : 2 * length, :] = second[own_rows : own_rows + length - cut]
    wide_ref[2 * length :, :] = second[:length]
    out_ref[...] = wide_ref[...].astype(out_ref.dtype)


def qkv_body(
    scale, place, own_ref, near_ref, far_ref, gain, bias, p0, p1, p2, p3, r0, r1, r2, r3, a_ref,
    b_ref, qv_ref, sel_ref, x_ref, z_ref, u_ref, out_ref, keep_out, send_out, w_ref,
):
    width = x_ref.shape[1]
    half = width // 2
    stack = sel_ref.shape[1]

    @pl.when(pl.program_id(0) == 0)
    def _():
        settle_qkv(place, (p0, p1, p2, p3), (r0, r1, r2, r3), w_ref)

    left, right = both_halves(place, own_ref[...], near_ref[...], far_ref[...])
    x = jnp.concatenate([left, right], axis=1)
    x_ref[...] = x
    normal, _ = norm_of(x.astype(F32))
    z = (normal * gain[...] + bias[...]).astype(BF16)
    z_ref[...] = z
    low = dot(z, a_ref[...])
    for k in range(3):
        kept = (low[:, k * stack : (k + 1) * stack] * sel_ref[...]).astype(BF16)
        u_ref[:, k * stack : (k + 1) * stack] = kept
        w = w_ref[k].reshape(width, width)
        parts = []
        for y in range(2):
            lanes = slice(y * half, (y + 1) * half)
            acc = dot(z, w[:, lanes]) + dot(kept, b_ref[y, :, k * half : (k + 1) * half])
            out = (acc + qv_ref[k, :, lanes]).astype(BF16)
            if k == 0:
                out = out * jnp.asarray(scale, BF16)
            out_ref[k, :, lanes] = out
            parts.append(out)
        keep_out[k] = chosen(place[2], parts[0], parts[1])
        send_out[k] = chosen(place[2], parts[1], parts[0])


def attend_pairs(pairs, mask, p_ref):
    lane = lax.broadcasted_iota(jnp.int32, mask.shape, 1)
    one, zero = jnp.ones_like(mask), jnp.zeros_like(mask)
    work = []
    for q, k, v in pairs:
        for spare, here in ((HD, lane < HD), (0, lane >= HD)):
            mine = jnp.where(here, q, jnp.where(lane == spare, one, zero))
            work.append((mine, jnp.where(lane == spare, mask, k), v))
    scores, parts = [dot(work[0][0], work[0][1], NT)], []
    for i, (_, _, v) in enumerate(work):
        if i + 1 < len(work):
            scores.append(dot(work[i + 1][0], work[i + 1][1], NT))
        s = scores[i]
        e = jnp.exp(s - jnp.max(s, axis=1, keepdims=True))
        p = (e * (1.0 / jnp.sum(e, axis=1, keepdims=True))).astype(BF16)
        p_ref[i] = p
        parts.append(dot(p, v))
    return [
        jnp.where(lane < HD, parts[i], parts[i + 1]).astype(BF16) for i in range(0, len(parts), 2)
    ]


def pair_lanes(ref):
    return [slice(i, i + 2 * HD) for i in range(0, ref.shape[-1], 2 * HD)]


def attend_body(q_ref, k_ref, v_ref, mask_ref, out_ref, p_ref):
    lanes = pair_lanes(out_ref)
    pairs = [(q_ref[0, :, at], k_ref[0, :, at], v_ref[0, :, at]) for at in lanes]
    for at, out in zip(lanes, attend_pairs(pairs, mask_ref[...], p_ref)):
        out_ref[:, at] = out


def attend_shared_body(mine_ref, mate_ref, mask_ref, keep_ref, send_ref, p_ref):
    lanes = pair_lanes(keep_ref)
    pairs = [
        [jnp.concatenate([mine_ref[i, :, at], mate_ref[i, :, at]]) for i in range(3)]
        for at in lanes
    ]
    count = keep_ref.shape[0]
    for at, out in zip(lanes, attend_pairs(pairs, mask_ref[...], p_ref)):
        keep_ref[:, at] = out[:count]
        send_ref[:, at] = out[count:]


def attend_back_one(scale, q, k, v, p_ref, att, do):
    low_lanes = lax.broadcasted_iota(jnp.int32, q.shape, 1) < HD
    zero = jnp.zeros_like(q)
    product = att.astype(F32) * do.astype(F32)
    do_t, q_t = do.T, q.T
    places = (low_lanes, ~low_lanes)
    dp = [dot(jnp.where(here, do, zero), v, NT) for here in places]
    dv = [dot(do_t[h * HD : (h + 1) * HD], p_ref[h]) for h in range(2)]
    ds = []
    for h, here in enumerate(places):
        delta = jnp.sum(jnp.where(here, product, 0.0), axis=1, keepdims=True)
        ds.append((p_ref[h].astype(F32) * (dp[h] - delta)).astype(BF16))
    dq = sum(dot(ds[h], jnp.where(here, k, zero)) for h, here in enumerate(places))
    dk = [dot(q_t[h * HD : (h + 1) * HD], ds[h]) for h in range(2)]
    dk, dv = (jnp.concatenate(t).astype(BF16).T for t in (dk, dv))
    return (dq * scale).astype(BF16), dk, dv


def attend_back_body(scale, q_ref, k_ref, v_ref, p_ref, att_ref, do_ref, out_ref):
    parts = attend_back_one(
        scale, q_ref[0], k_ref[0], v_ref[0], p_ref, att_ref[...], do_ref[...]
    )
    for i in range(3):
        out_ref[i] = parts[i]


def attend_back_shared_body(
    scale, mine_ref, mate_ref, p_ref, att_keep, att_send, do_keep, do_mate, keep_ref, send_ref
):
    q, k, v = (jnp.concatenate([mine_ref[i], mate_ref[i]]) for i in range(3))
    att = jnp.concatenate([att_keep[...], att_send[...]])
    do = jnp.concatenate([do_keep[...], do_mate[...]])
    parts = attend_back_one(scale, q, k, v, p_ref, att, do)
    count = keep_ref.shape[1]
    for i in range(3):
        keep_ref[i] = parts[i][:count]
        send_ref[i] = parts[i][count:]


def out_body(
    place, own_ref, keep_ref, mate_ref, x_ref, r0, r1, r2, r3, a_ref, b_ref, bias_ref, gain,
    lbias, aup_ref, sel_ref, hid_ref, z_ref, u_ref, uup_ref, w_ref,
):
    width = x_ref.shape[1]
    half = width // 2

    @pl.when(pl.program_id(0) == 0)
    def _():
        settle_out(place, (r0, r1, r2, r3), w_ref)

    keep, mate = keep_ref[...], mate_ref[...]
    shared = jnp.concatenate(
        [chosen(place[2], keep, mate), chosen(place[2], mate, keep)], axis=1
    )
    att = jnp.where(pl.program_id(0) < 2, own_ref[...], shared)
    sel = sel_ref[...]
    low = dot(att[:, :half], a_ref[0], NT) + dot(att[:, half:], a_ref[1], NT)
    kept = (low * sel).astype(BF16)
    u_ref[...] = kept
    acc = dot(att, w_ref[...].reshape(width, width), NT) + dot(kept, b_ref[...])
    hidden = x_ref[...].astype(F32) + acc + bias_ref[...]
    hid_ref[...] = hidden
    normal, _ = norm_of(hidden)
    z = (normal * gain[...] + lbias[...]).astype(BF16)
    z_ref[...] = z
    uup_ref[...] = (dot(z, aup_ref[...]) * sel).astype(BF16)


def mlp_body(
    rows, place, z_ref, gown_ref, gnear_ref, gfar_ref, uup_ref, sel_ref, hid_ref, wup_ref,
    wdn_ref, bup_own, bup_near, bup_far, adn_own, adn_near, adn_far, upb_ref, bdn_ref, aup_ref,
    dnb_ref, gain,
    own_ref, near_ref, far_ref, ghb_ref, ekeep_ref, esend_ref,
    down_acc, dz_acc, udn_acc, eup_acc, edn_ref, uup_t, edn_t, gy_ref, hid_buf, hid_sem,
):
    total, width = z_ref.shape
    step = pl.program_id(0)
    blocks = [slice(i, i + rows) for i in range(0, total, rows)]

    fetch = pltpu.make_async_copy(hid_ref, hid_buf, hid_sem)

    @pl.when(step == 0)
    def _():
        fetch.start()
        for b in blocks:
            left, right = both_halves(place, gown_ref[b, :], gnear_ref[b, :], gfar_ref[b, :])
            gy = jnp.concatenate([left, right], axis=1)
            gy_ref[b, :] = gy
            edn_ref[b, :] = (dot(gy, bdn_ref[...], NT) * sel_ref[b, :]).astype(BF16)
        edn_t[...] = edn_ref[...].T
        uup_t[...] = uup_ref[...].T
        down_acc[...] = jnp.zeros_like(down_acc)
        dz_acc[...] = jnp.zeros_like(dz_acc)
        udn_acc[...] = jnp.zeros_like(udn_acc)
        eup_acc[...] = jnp.zeros_like(eup_acc)

    chunk = upb_ref.shape[1]
    wup = wup_ref[...].reshape(width, chunk)
    wdn = wdn_ref[...].reshape(width, chunk)
    parts = pl.num_programs(0) // 2
    y = step // parts

    def adapter(own_ref, near_ref, far_ref):
        near, far = near_ref[...], far_ref[...]
        other = jnp.concatenate([chosen(place[2], near, far), chosen(place[2], far, near)])
        return jnp.where(place[3] == y, own_ref[...], other)

    bup = adapter(bup_own, bup_near, bup_far)
    adn = adapter(adn_own, adn_near, adn_far)
    pre = dot(z_ref[...], wup) + dot(uup_ref[...], bup) + upb_ref[...]
    d_act = dot(gy_ref[...], wdn) + dot(edn_ref[...], adn)
    bent = (0.5 * GELU_SCALE) * pre
    turn = jnp.tanh(bent)
    q = 0.5 + 0.5 * turn
    act = (pre * q).astype(BF16)
    d_up = (d_act * (q + q * (bent * (1.0 - turn)))).astype(BF16)
    down_acc[...] += dot(act, wdn, NT)
    dz_acc[...] += dot(d_up, wup, NT)
    udn_acc[...] += dot(act, adn, NT)
    eup_acc[...] += dot(d_up, bup, NT)
    hidden_half = parts * chunk
    for i, (low, high) in enumerate(((uup_t, d_up), (edn_t, act))):
        found = split_rows(place, dot(low[...], high).astype(BF16))
        lanes = pl.ds(pl.multiple_of(i * hidden_half + step % parts * chunk, chunk), chunk)
        ekeep_ref[y, :, lanes], esend_ref[y, :, lanes] = found

    @pl.when(step == pl.num_programs(0) - 1)
    def _():
        fetch.wait()
        gbdn = gaup = 0.0
        for b in blocks:
            sel = sel_ref[b, :]
            e_up = (eup_acc[b, :] * sel).astype(BF16)
            u_dn = (udn_acc[b, :] * sel).astype(BF16)
            hidden = hid_buf[b, :]
            y = hidden + down_acc[b, :] + dot(u_dn, bdn_ref[...]) + dnb_ref[...]
            halves_out(place, y.astype(BF16), b, own_ref, near_ref, far_ref)
            dz = dz_acc[b, :] + dot(e_up, aup_ref[...], NT)
            normal, inverse = norm_of(hidden)
            grad = gy_ref[b, :].astype(F32) + norm_pull(dz, normal, inverse, gain[...])
            ghb_ref[b, :] = grad.astype(BF16)
            gbdn = gbdn + dot_rows(u_dn, gy_ref[b, :])
            gaup = gaup + dot_rows(e_up, z_ref[b, :])
        half = width // 2
        for i, grad in enumerate((gaup, gbdn)):
            start = 2 * hidden_half + i * half
            for column in range(2):
                rows = split_rows(place, grad[:, column * half : (column + 1) * half].astype(BF16))
                lanes = slice(start, start + half)
                ekeep_ref[column, :, lanes], esend_ref[column, :, lanes] = rows


def split_rows(place, grad):
    part = grad.shape[0] // 2
    low, high = grad[:part], grad[part:]
    return chosen(place[2], low, high), chosen(place[2], high, low)


def out_back_body(
    place, g_ref, own_ref, keep_ref, mate_ref, r0, r1, r2, r3, a_ref, b_ref, sel_ref, u_ref,
    d_own, d_keep, d_send, g_keep, g_send, w_ref, e_ref, e_t,
):
    width = g_ref.shape[1]
    half = width // 2
    count = keep_ref.shape[0]
    y = pl.program_id(0)

    @pl.when(y == 0)
    def _():
        def store(row, column, block):
            w_ref[column, row] = block

        settle(place, (r0, r1, r2, r3), True, store)
        e = (dot(g_ref[...], b_ref[...], NT) * sel_ref[...]).astype(BF16)
        e_ref[...] = e
        e_t[...] = e.T
        gb = dot(u_ref[...].T, g_ref[...]).astype(BF16)
        for column in range(2):
            rows = split_rows(place, gb[:, column * half : (column + 1) * half])
            g_keep[column, :, half:], g_send[column, :, half:] = rows

    w = w_ref[y].reshape(width, half)
    d = (dot(g_ref[...], w) + dot(e_ref[...], a_ref[0])).astype(BF16)
    d_own[...] = d[: 2 * count]

    shared = jnp.where(place[2] == y, keep_ref[...], mate_ref[...])
    ga = dot(e_t[...], jnp.concatenate([own_ref[...], shared])).astype(BF16)
    g_keep[y, :, :half], g_send[y, :, :half] = split_rows(place, ga)

    @pl.when(place[2] == y)
    def _():
        d_keep[...] = d[2 * count :]

    @pl.when(place[2] != y)
    def _():
        d_send[...] = d[2 * count :]


def shared_halves(place, keep, mate):
    return chosen(place[2], keep, mate), chosen(place[2], mate, keep)


def qkv_grads_body(
    place, left_ref, right_ref, keep_ref, mate_ref, b_ref, sel_ref, u_ref, z_ref, e_ref,
    keep_out, send_out,
):
    half = left_ref.shape[2]
    part = sel_ref.shape[1] // 2
    shared = shared_halves(place, keep_ref[0], mate_ref[0])
    u_t = u_ref[...].T

    def put(grad, y, i):
        low, high = grad[:part], grad[part:]
        keep_out[y, i, 0] = chosen(place[2], low, high)
        send_out[y, i, 0] = chosen(place[2], high, low)

    low = 0.0
    for y, own_ref in enumerate((left_ref, right_ref)):
        d = jnp.concatenate([own_ref[0], shared[y]])
        low = low + dot(d, b_ref[y], NT)
        put(dot(u_t, d).astype(BF16), y, 0)
    e = (low * sel_ref[...]).astype(BF16)
    e_ref[...] = e
    ga = dot(e.T, z_ref[...]).astype(BF16)
    for y in range(2):
        put(ga[:, y * half : (y + 1) * half], y, 1)


def qkv_back_body(
    shared, place, left_ref, right_ref, p0, p1, p2, p3, r0, r1, r2, r3, a_ref, e_ref, x_ref,
    gh_ref, gain, own_out, near_out, far_out, w_ref,
):
    width = x_ref.shape[1]
    settle_qkv(place, (p0, p1, p2, p3), (r0, r1, r2, r3), w_ref)
    dz = dot(e_ref[...], a_ref[...], NT)
    for k in range(3):
        left, right = left_ref[k], right_ref[k]
        if shared:
            left, right = shared_halves(place, left, right)
        d = jnp.concatenate([left, right], axis=1)
        dz = dz + dot(d, w_ref[k].reshape(width, width), NT)
    normal, inverse = norm_of(x_ref[...].astype(F32))
    grad = gh_ref[...].astype(F32) + norm_pull(dz, normal, inverse, gain[...])
    halves_out(place, grad.astype(BF16), slice(None), own_out, near_out, far_out)


def on_chip_pair(
    mesh_shape, tokens, cotangent, ln1_gain, ln1_bias, ln2_gain, ln2_bias, w_qkv, qv_bias, w_out,
    out_bias, w_up, up_bias, w_down, down_bias, adapter_ids, a_qkv, b_qkv, a_out, b_out, a_up,
    b_up, a_down, b_down,
):
    n_row, n_col = mesh_shape
    count, half = tokens.shape
    width = half * 2
    stack = b_out.shape[0]
    part = stack // 2
    hidden_half = w_up.shape[1]
    hidden = hidden_half * 2
    length = count // adapter_ids.shape[0]
    cut = length // 2
    heads = width // HD
    tb = -(-(length + 1) // 32) * 16
    own_rows, total = 2 * tb, 3 * tb
    scale = HD ** (-0.5)
    both = ("row", "col")
    row, col = lax.axis_index("row"), lax.axis_index("col")
    core, side, n_far = row % 2, row // 2 % 2, n_row // 4
    place = jnp.stack([row // 4, side, core, col]).astype(jnp.int32)

    def device(r, c):
        return r * n_col + c

    far_swaps = [[] for _ in range(n_far.bit_length() - 1)]
    far_turns = [[] for _ in range(n_far - 1)]
    ring_in, ring_back, cross, cores, cols_swap, sides_swap = [], [], [], [], [], []
    for r in range(n_row):
        for c in range(n_col):
            k, mate = r % 2, r + 1 - 2 * (r % 2)
            cores.append((device(r, c), device(mate, c)))
            cols_swap.append((device(r, c), device(r, 1 - c)))
            sides_swap.append((device(r, c), device(r ^ 2, c)))
            for turn, pairs in enumerate(far_turns):
                pairs.append((device(r, c), device((r + 4 * (turn + 1)) % n_row, c)))
            for bit, pairs in enumerate(far_swaps):
                pairs.append((device(r, c), device(r ^ (4 << bit), c)))
            if k != c:
                ring_in.append((device(r, c), device(r, 1 - c)))
                ring_back.append((device(r, c), device(mate, c)))
                cross.append((device(r, c), device(mate, 1 - c)))
            else:
                ring_in.append((device(r, c), device(mate, c)))
                ring_back.append((device(r, c), device(r, 1 - c)))

    def move(values, pairs):
        return lax.ppermute(values, both, pairs)

    def pick(pair, index):
        return jnp.where(index == 0, pair[0], pair[1])

    def ordered(mine, other, index, axis):
        return jnp.where(
            index == 0,
            jnp.concatenate([mine, other], axis),
            jnp.concatenate([other, mine], axis),
        )

    def tie(*values):
        return lax.optimization_barrier(values)

    thirds = [struct((total, half), BF16)] * 3
    third_specs = [fixed((total, half))] * 3

    def spread(values):
        return call(
            functools.partial(spread_body, length, cut, own_rows, tb),
            (1,),
            [SPOT, fixed((count, half))],
            third_specs,
            thirds,
            scratch=[pltpu.VMEM((count, half), F32)],
        )(place, values)

    def join(own, near, far, kind):
        return call(
            functools.partial(join_body, length, cut, own_rows, len(own)),
            (1,),
            [SPOT] + [fixed(t.shape) for t in (*own, *near, *far)],
            fixed((count, half)),
            struct((count, half), kind),
            scratch=[pltpu.VMEM((count, half), F32)],
        )(place, *own, *near, *far)

    x_own, x_near, x_far = spread(tokens)
    x_near, x_far, w_qkv, w_out = tie(x_near, x_far, w_qkv, w_out)
    mine_first = jnp.concatenate(
        [jnp.swapaxes(w_qkv, 0, 1).reshape(-1, 3 * half), w_out.T], axis=1
    )
    mine_second = jnp.concatenate([w_up, w_down.T], axis=1)
    adapt_first = jnp.concatenate(
        [jnp.swapaxes(b_qkv, 0, 1).reshape(stack, 3 * half), a_out.T], axis=1
    )
    adapt_second = jnp.concatenate([b_up, a_down.T], axis=1)
    deep = width // n_row

    def turned(block):
        return jnp.stack([block] + [move(block, pairs) for pairs in far_turns])

    def doubled(found, pairs):
        return jnp.concatenate([found, move(found, pairs)])

    def part_of(values):
        return lax.dynamic_slice_in_dim(values, core * part, part, 0)

    def widened(values, near, far):
        return ordered(values[None], ordered(near, far, core, 0)[None], col, 0)

    x_near, x_far = move(x_near, ring_in), move(x_far, cross)
    near0, near1 = turned(mine_first[:, :width]), turned(mine_first[:, width:])
    near0, x_near, x_far, mine_second = tie(near0, x_near, x_far, mine_second)
    near0, near1 = tie(near0, near1)
    x_parts = (x_own, x_near, x_far)
    big_second = lax.all_gather(mine_second, both, axis=0, tiled=False)
    big_second = big_second.reshape(n_row, n_col, deep, 2 * hidden_half)
    near0, near1 = doubled(near0, sides_swap), doubled(near1, cols_swap)
    ad_near = move(part_of(adapt_first), cols_swap)
    biases = jnp.concatenate([qv_bias[0], qv_bias[1], up_bias])[None]
    bias_pair = ordered(biases, move(biases, cols_swap), col, 0)
    ids = jnp.where(core == col, adapter_ids, move(adapter_ids, cores))
    g_own, g_near, g_far = spread(cotangent)
    near0, near1, bias_pair, ids, ad_near = tie(near0, near1, bias_pair, ids, ad_near)
    ad_first = widened(adapt_first, ad_near, move(ad_near, cores))
    last0, last1 = move(near0, cols_swap), move(near1, sides_swap)
    far0, far1 = move(near0, cores), move(near1, cores)
    adapt_part = part_of(adapt_second)
    valid = jnp.arange(own_rows)[:, None]
    here, there = jnp.where(core == 0, cut, length - cut), jnp.where(core == 0, length - cut, cut)

    def mask_of(good):
        return jnp.broadcast_to(jnp.where(good, 0.0, -1e30), (own_rows, 2 * HD)).astype(BF16)

    mask_own = mask_of(valid < length)
    mask_shared = mask_of((valid < here) | ((valid >= tb) & (valid < tb + there)))
    last0, last1, far0, far1, ad_first, g_near, g_far = tie(
        last0, last1, far0, far1, ad_first, g_near, g_far
    )
    last0, adapt_part, adapt_second, mask_own, mask_shared = tie(
        last0, adapt_part, adapt_second, mask_own, mask_shared
    )
    ad_near = move(adapt_part, cols_swap)
    blocks0 = (near0, last0, far0, move(last0, cores))
    blocks1 = (near1, last1, far1, move(last1, cores))
    qv_rows = jnp.stack(
        [
            bias_pair[:, :half].reshape(1, width),
            jnp.zeros((1, width), F32),
            bias_pair[:, half:width].reshape(1, width),
        ]
    )
    up_row = bias_pair[:, width:].reshape(1, hidden)

    owners = lax.iota(jnp.int32, stack) // RANK
    own_id = jnp.where(core == 0, ids[0], ids[2])
    places = lax.iota(jnp.int32, total)[:, None]
    sel = (jnp.where(places < own_rows, own_id, ids[1]) == owners[None]).astype(F32)

    gain1, bias1, gain2, bias2 = (t[None] for t in (ln1_gain, ln1_bias, ln2_gain, ln2_bias))

    rows_block = pl.BlockSpec((tb, width), lambda i: (i, 0))
    sel_block = pl.BlockSpec((tb, stack), lambda i: (i, 0))
    every = fixed((total, width))
    thin = fixed((total, stack))
    vec = fixed((1, width))
    pieces0 = [fixed((n_row // 2, deep, width))] * 4
    pieces1 = [fixed((n_row // 2, deep, half))] * 4
    pieces_out = [
        pl.BlockSpec(
            (n_row // 2, deep, half), lambda *_: (0, 0, 1), pipeline_mode=pl.Buffered(1)
        )
    ] * 4
    w_qkv_room = [pltpu.VMEM((3, n_row, deep, width), BF16)]
    w_out_room = [pltpu.VMEM((n_row, deep, width), BF16)]
    ad_out_spec = pl.BlockSpec(
        (n_col, stack, half), lambda *_: (0, 0, 3), pipeline_mode=pl.Buffered(1)
    )
    low_k = pl.BlockSpec((total, stack), lambda k: (0, k))
    shared_k = pl.BlockSpec((1, tb, half), lambda k: (k, 0, 0))
    ad_k = pl.BlockSpec((n_col, stack, half), lambda k: (0, 0, k))
    shared_struct = struct((3, tb, half), BF16)
    half_rows = struct((tb, half), BF16)

    third_rows = pl.BlockSpec((tb, half), lambda i: (i, 0))
    low_block = pl.BlockSpec((tb, 3 * stack), lambda i: (i, 0))
    all_three = pl.BlockSpec((3, tb, width), lambda i: (0, i, 0))
    shared_three = fixed((3, tb, half))
    x, z1, u_qkv, qkv, qkv_keep, qkv_send = call(
        functools.partial(qkv_body, scale),
        (3,),
        [
            SPOT, third_rows, third_rows, third_rows, vec, vec, *pieces0, *pieces1,
            fixed((width, 3 * stack)),
            pl.BlockSpec(
                (n_col, stack, 3 * half), lambda i: (0, 0, 0), pipeline_mode=pl.Buffered(1)
            ),
            fixed((3, 1, width)), sel_block,
        ],
        [rows_block, rows_block, low_block, all_three, shared_three, shared_three],
        [
            struct((total, width), BF16),
            struct((total, width), BF16),
            struct((total, 3 * stack), BF16),
            struct((3, total, width), BF16),
            shared_struct,
            shared_struct,
        ],
        scratch=w_qkv_room,
    )(place, *x_parts, gain1, bias1, *blocks0, *blocks1, a_qkv, ad_first, qv_rows, sel)

    qkv_mate = move(qkv_send, cores)
    qkv, g_near, g_far = tie(qkv, g_near, g_far)
    g_near, g_far = move(g_near, ring_in), move(g_far, cross)

    head_p = pl.BlockSpec((2, own_rows, own_rows), lambda h: (h, 0, 0))
    pair_k = pl.BlockSpec((3, tb, 2 * HD), lambda h: (0, 0, h))
    pair_rows = pl.BlockSpec((tb, 2 * HD), lambda h: (0, h))
    wide = 4 * HD
    att_own, p_own = call(
        attend_body,
        (width // wide,),
        [pl.BlockSpec((1, own_rows, wide), lambda h, k=k: (k, 0, h)) for k in range(3)]
        + [fixed((own_rows, 2 * HD))],
        [
            pl.BlockSpec((own_rows, wide), lambda h: (0, h)),
            pl.BlockSpec((4, own_rows, own_rows), lambda h: (h, 0, 0)),
        ],
        [struct((own_rows, width), BF16), struct((heads, own_rows, own_rows), BF16)],
    )(qkv, qkv, qkv, mask_own)
    qkv_mate, att_own = tie(qkv_mate, att_own)
    wide_k = pl.BlockSpec((3, tb, wide), lambda h: (0, 0, h))
    wide_rows = pl.BlockSpec((tb, wide), lambda h: (0, h))
    att_keep, att_send, p_sh = call(
        attend_shared_body,
        (half // wide,),
        [wide_k, wide_k, fixed((own_rows, 2 * HD))],
        [wide_rows, wide_rows, pl.BlockSpec((4, own_rows, own_rows), lambda h: (h, 0, 0))],
        [half_rows, half_rows, struct((heads // 2, own_rows, own_rows), BF16)],
    )(qkv_keep, qkv_mate, mask_shared)
    att_send, ad_near = tie(att_send, ad_near)
    att_mate = move(att_send, cores)
    g_parts = (g_own, g_near, g_far)
    ad_second = (adapt_second, ad_near, move(ad_near, cores))

    own_block = pl.BlockSpec((tb, width), lambda i: (jnp.minimum(i, 1), 0))
    shared_rows = fixed((tb, half))
    hid, z2, u_out, u_up = call(
        out_body,
        (3,),
        [
            SPOT, own_block, shared_rows, shared_rows, rows_block, *pieces_out,
            ad_out_spec, fixed((stack, width)), vec, vec, vec, fixed((width, stack)), sel_block,
        ],
        [rows_block, rows_block, sel_block, sel_block],
        [
            struct((total, width), F32),
            struct((total, width), BF16),
            struct((total, stack), BF16),
            struct((total, stack), BF16),
        ],
        scratch=w_out_room,
    )(
        place, att_own, att_keep, att_mate, x, *blocks1, ad_first, b_out, out_bias[None],
        gain2, bias2, a_up, sel,
    )

    chunk = half
    parts = hidden_half // chunk

    def w_spec(shift):
        return pl.BlockSpec(
            (n_row, 1, deep, chunk), lambda j: (0, j // parts, 0, j % parts + shift)
        )

    def ad_specs(shift):
        return [
            pl.BlockSpec((rows, chunk), lambda j: (0, j % parts + shift))
            for rows in (stack, part, part)
        ]

    early_half = fixed((2, part, 2 * hidden_half + 2 * half))
    early_struct = struct((2, part, 2 * hidden_half + 2 * half), BF16)
    y_own, y_near, y_far, ghb, early_keep, early_send = call(
        functools.partial(mlp_body, tb),
        (2 * parts,),
        [SPOT, every]
        + third_specs
        + [
            thin, thin, pl.BlockSpec(memory_space=pl.ANY), w_spec(0), w_spec(parts), *ad_specs(0), *ad_specs(parts),
            pl.BlockSpec((1, chunk), lambda j: (0, j)), fixed((stack, width)),
            fixed((width, stack)), vec, vec,
        ],
        third_specs + [every, early_half, early_half],
        thirds
        + [struct((total, width), BF16), early_struct, early_struct],
        scratch=[
            pltpu.VMEM((total, width), F32),
            pltpu.VMEM((total, width), F32),
            pltpu.VMEM((total, stack), F32),
            pltpu.VMEM((total, stack), F32),
            pltpu.VMEM((total, stack), BF16),
            pltpu.VMEM((stack, total), BF16),
            pltpu.VMEM((stack, total), BF16),
            pltpu.VMEM((total, width), BF16),
            pltpu.VMEM((total, width), F32),
            pltpu.SemaphoreType.DMA,
        ],
    )(
        place, z2, *g_parts, u_up, sel, hid, big_second, big_second, *ad_second, *ad_second, up_row,
        b_down, a_up, down_bias[None], gain2,
    )

    def added(kept, sent):
        return (kept.astype(F32) + sent.astype(F32)).astype(BF16)

    quarter = part // 2

    def quarter_of(values, index):
        return lax.dynamic_slice_in_dim(values, index * quarter, quarter, 1)

    def side_sent(values):
        return move(quarter_of(values, 1 - side), sides_swap)

    early_sent = move(early_send, cores)
    y_near, y_far = move(y_near, ring_back), move(y_far, cross)
    out_half = fixed((2, part, width))
    d_att, d_keep, d_send, out_keep, out_send = call(
        out_back_body,
        (2,),
        [
            SPOT, every, pl.BlockSpec((own_rows, half), lambda i: (0, i)), shared_rows,
            shared_rows, *pieces_out,
            pl.BlockSpec((1, stack, half), lambda i: (i, 0, 3)), fixed((stack, width)), thin, thin,
        ],
        [
            pl.BlockSpec((own_rows, half), lambda i: (0, i)), shared_rows, shared_rows, out_half,
            out_half,
        ],
        [
            struct((own_rows, width), BF16),
            half_rows,
            half_rows,
            struct((2, part, width), BF16),
            struct((2, part, width), BF16),
        ],
        scratch=[
            pltpu.VMEM((2, n_row, deep, half), BF16),
            pltpu.VMEM((total, stack), BF16),
            pltpu.VMEM((stack, total), BF16),
        ],
    )(place, ghb, att_own, att_keep, att_mate, *blocks1, ad_first, b_out, sel, u_out)

    d_mate = move(d_send, cores)
    early_sum = jnp.concatenate(
        [added(early_keep, early_sent), added(out_keep, move(out_send, cores))], axis=2
    )
    d_mate, early_sum = tie(d_mate, early_sum)
    early_sent = side_sent(early_sum)

    g_keep, g_send = call(
        functools.partial(attend_back_shared_body, scale),
        (heads // 4,),
        [pair_k, pair_k, head_p, pair_rows, pair_rows, pair_rows, pair_rows],
        [pair_k, pair_k],
        [shared_struct, shared_struct],
        us=8,
    )(qkv_keep, qkv_mate, p_sh, att_keep, att_send, d_keep, d_mate)
    d_att, g_send = tie(d_att, g_send)
    g_mate = move(g_send, cores)
    quarters = heads // 4

    def own_back(shift, d_out):
        return call(
            functools.partial(attend_back_body, scale),
            (quarters,),
            [
                pl.BlockSpec((1, own_rows, 2 * HD), lambda h, k=k: (k, 0, h + shift))
                for k in range(3)
            ]
            + [
                pl.BlockSpec((2, own_rows, own_rows), lambda h: (h + shift, 0, 0)),
                pl.BlockSpec((own_rows, 2 * HD), lambda h: (0, h + shift)),
                pl.BlockSpec((own_rows, 2 * HD), lambda h: (0, h + shift)),
            ],
            pl.BlockSpec((3, own_rows, 2 * HD), lambda h: (0, 0, h)),
            struct((3, own_rows, half), BF16),
            us=9,
        )(qkv, qkv, qkv, p_own, att_own, d_out)

    d_left = own_back(0, d_att)
    early_sum = added(quarter_of(early_sum, side), early_sent)
    d_left, d_att, early_sum, y_near, y_far = tie(d_left, d_att, early_sum, y_near, y_far)
    early_sent = move(pick(early_sum, 1 - col), cols_swap)
    d_right = own_back(quarters, d_att)

    grad_spec = pl.BlockSpec((2, 2, 1, part, half), lambda k: (0, 0, k, 0, 0))
    grad_struct = struct((2, 2, 3, part, half), BF16)
    early_sum = added(pick(early_sum, col), early_sent)
    d_right, early_sum = tie(d_right, early_sum)
    early_sent = move(early_sum, far_swaps[0])
    half_k = pl.BlockSpec((1, own_rows, half), lambda k: (k, 0, 0))
    e_qkv, q_kept, q_sent = call(
        qkv_grads_body,
        (3,),
        [SPOT, half_k, half_k, shared_k, shared_k, ad_k, thin, low_k, every],
        [low_k, grad_spec, grad_spec],
        [struct((total, 3 * stack), BF16), grad_struct, grad_struct],
        us=7,
    )(place, d_left, d_right, g_keep, g_mate, ad_first, sel, u_qkv, z1)

    def side_of(values, index):
        return jnp.where(index == 0, values[:, 0], values[:, 1])

    sums = added(q_kept, move(q_sent, cores)).reshape(2, 2, 3 * part, half)
    early_sum = added(early_sum, early_sent)
    sums, e_qkv, early_sum = tie(sums, e_qkv, early_sum)
    early_sent = move(early_sum, far_swaps[-1])
    q_sent = move(side_of(sums, 1 - side), sides_swap)

    def token_rows(block, left, right):
        at = block % 2
        d_spec = pl.BlockSpec((3, tb, half), lambda i: (0, at, 0), pipeline_mode=pl.Buffered(1))
        rows = pl.BlockSpec((tb, width), lambda i: (block, 0), pipeline_mode=pl.Buffered(1))
        low = pl.BlockSpec((tb, 3 * stack), lambda i: (block, 0), pipeline_mode=pl.Buffered(1))
        return call(
            functools.partial(qkv_back_body, block == 2),
            (1,),
            [
                SPOT, d_spec, d_spec, *pieces0, *pieces1, fixed((width, 3 * stack)), low, rows,
                rows, vec,
            ],
            [shared_rows] * 3,
            [half_rows] * 3,
            scratch=w_qkv_room,
            us=6,
        )(place, left, right, *blocks0, *blocks1, a_qkv, e_qkv, x, ghb, gain1)

    t_own, t_near, t_far = [], [], []

    def sent_rows(own, near, far):
        t_own.append(own)
        t_near.append(move(near, ring_back))
        t_far.append(move(far, cross))

    rows_own, rows_near, rows_far = token_rows(0, d_left, d_right)
    q_sent, rows_near, rows_far = tie(q_sent, rows_near, rows_far)
    sums = added(side_of(sums, side), q_sent)
    sums, d_left, d_right = tie(sums, d_left, d_right)
    q_sent = move(pick(sums, 1 - col), cols_swap)
    sent_rows(rows_own, rows_near, rows_far)
    rows_own, rows_near, rows_far = token_rows(1, d_left, d_right)
    q_sent, rows_near, rows_far, early_sent = tie(q_sent, rows_near, rows_far, early_sent)
    early_sum = added(early_sum, early_sent)
    sums = added(pick(sums, col), q_sent)
    sums, g_keep, g_mate = tie(sums, g_keep, g_mate)
    q_sent = move(sums, far_swaps[1])
    sent_rows(rows_own, rows_near, rows_far)
    edge = 2 * hidden_half
    whole = edge + 4 * half
    split_lanes = [slice(edge, edge + 2 * half), slice(edge + 3 * half, whole)]
    rest = jnp.concatenate([early_sum[:, lanes] for lanes in split_lanes], axis=1)
    rest = move(rest, cols_swap)
    rows_own, rows_near, rows_far = token_rows(2, g_keep, g_mate)
    early_sum = jnp.concatenate([early_sum, rest], axis=1)
    q_sent, rows_near, rows_far, early_sum, y_own, t_near[0], t_far[0] = tie(
        q_sent, rows_near, rows_far, early_sum, y_own, t_near[0], t_far[0]
    )
    sums = added(sums, q_sent)
    q_sent = move(sums, far_swaps[0])
    sent_rows(rows_own, rows_near, rows_far)
    early_sent = move(early_sum, sides_swap)
    layer_out = join([y_own], [y_near], [y_far], BF16)
    q_sent, layer_out, t_near[1], t_far[1] = tie(q_sent, layer_out, t_near[1], t_far[1])
    sums = added(sums, q_sent)
    for pairs in far_swaps[2:]:
        sums = added(sums, move(sums, pairs))
    side_sums = move(sums, sides_swap)
    early_sum = ordered(early_sum, early_sent, side, 0)
    side_sums, t_near[2], t_far[2], early_sum = tie(
        side_sums, t_near[2], t_far[2], early_sum
    )
    early_sent = move(early_sum, cores)
    tokens_grad = join(t_own, t_near, t_far, F32)
    mine = ordered(early_sum, early_sent, core, 0).astype(F32)
    sums = ordered(sums[None], side_sums[None], side, 0)
    a_sent = move(sums[1:], cols_swap)
    own_starts = (edge, edge + half, edge + 3 * half)
    a_up_sum, b_down_sum, b_out_sum = (
        ordered(
            mine[:, start : start + half],
            mine[:, whole + i * half : whole + (i + 1) * half],
            col,
            1,
        )
        for i, start in enumerate(own_starts)
    )
    a_out_sum, a_up_sum = mine[:, edge + 2 * half : edge + 3 * half].T, a_up_sum.T
    b_up_sum, a_down_sum = mine[:, :hidden_half], mine[:, hidden_half:edge].T
    a_sent, tokens_grad, a_out_sum, a_up_sum, b_up_sum, a_down_sum, b_down_sum, b_out_sum = tie(
        a_sent, tokens_grad, a_out_sum, a_up_sum, b_up_sum, a_down_sum, b_down_sum, b_out_sum
    )
    every_sum = jnp.concatenate([sums[:1], ordered(sums[1:], a_sent, col, 0)])
    every_sum = every_sum.reshape(3, 3, part, half)
    every_sum = ordered(every_sum, move(every_sum, cores), core, 2).reshape(3, 3 * stack, half)
    b_sum = every_sum[0].reshape(3, stack, half).astype(F32)
    a_sum = jnp.concatenate([every_sum[1].T, every_sum[2].T]).astype(F32)
    return (
        layer_out,
        tokens_grad,
        a_sum,
        b_sum,
        a_out_sum,
        b_out_sum,
        a_up_sum,
        b_up_sum,
        a_down_sum,
        b_down_sum,
    )


def solution(mesh):
    placed = (
        P("row", "col"),
        P("row", "col"),
        P(),
        P(),
        P(),
        P(),
        P(None, "row", "col"),
        P(None, "col"),
        P("col", "row"),
        P(),
        P("row", "col"),
        P("col"),
        P("col", "row"),
        P(),
        P("row"),
        P(),
        P(None, None, "col"),
        P("col", None),
        P(),
        P(),
        P(None, "col"),
        P("col", None),
        P(),
    )
    shape = (mesh.shape["row"], mesh.shape["col"])
    paired = shape[1] == 2 and shape[0] >= 16 and shape[0] & (shape[0] - 1) == 0
    return jax.shard_map(
        functools.partial(on_chip_pair, shape) if paired else on_device,
        mesh=mesh,
        in_specs=placed,
        out_specs=(
            P("row", "col"),
            P("row", "col"),
            P(),
            P(None, None, "col"),
            P("col", None),
            P(),
            P(),
            P(None, "col"),
            P("col", None),
            P(),
        ),
        check_vma=False,
    )
```

```python
import functools

import jax
import jax.numpy as jnp
from jax import lax
from jax.experimental import pallas as pl
from jax.experimental.pallas import tpu as pltpu
from jax.sharding import PartitionSpec as P

HD = 64
RANK = 16


EPS = 1e-05
GELU_SCALE = 1.702


def column_sums(first, second):
    return lax.psum((first, second), "col")


def gather_features(values):
    return lax.all_gather(values, "col", axis=1, tiled=True)


def sum_partials(terms):
    return lax.psum_scatter(
        terms.astype(jnp.bfloat16), "col", scatter_dimension=1, tiled=True
    ).astype(jnp.float32)


def norm_split(values, feature_width):
    first, second = column_sums(jnp.sum(values, axis=1), jnp.sum(values * values, axis=1))
    centre = first / feature_width
    inverse = lax.rsqrt(second / feature_width - centre * centre + EPS)
    return ((values - centre[:, None]) * inverse[:, None], inverse)


def norm_back(grad_normed, normal_rows, inverse, gain_part, feature_width):
    scaled = grad_normed * gain_part
    first, second = column_sums(jnp.sum(scaled, axis=1), jnp.sum(scaled * normal_rows, axis=1))
    return inverse[:, None] * (
        scaled - first[:, None] / feature_width - normal_rows * second[:, None] / feature_width
    )


def select_rows(low_rank, onehot, image_len):
    image_count, stack_width = onehot.shape
    shaped = low_rank.reshape(image_count, image_len, -1, stack_width)
    return (shaped * onehot[:, None, None, :]).reshape(low_rank.shape).astype(jnp.bfloat16)


def mult(form, first, second):
    return jnp.einsum(form, first, second, preferred_element_type=jnp.float32)


def on_device(
    tokens,
    cotangent,
    ln1_gain,
    ln1_bias,
    ln2_gain,
    ln2_bias,
    w_qkv,
    qv_bias,
    w_out,
    out_bias,
    w_up,
    up_bias,
    w_down,
    down_bias,
    adapter_ids,
    a_qkv,
    b_qkv,
    a_out,
    b_out,
    a_up,
    b_up,
    a_down,
    b_down,
):
    row_count, part_width = tokens.shape
    feature_width = a_qkv.shape[0]
    stack_width = a_qkv.shape[1] // 3
    image_count = adapter_ids.shape[0]
    image_len = row_count // image_count
    head_count = part_width // HD
    scale = HD ** (-0.5)
    offset = lax.axis_index("col") * part_width

    def own_part(values, axis):
        return lax.dynamic_slice_in_dim(values, offset, part_width, axis)

    owners = lax.iota(jnp.int32, stack_width) // RANK
    onehot = (adapter_ids[:, None] == owners[None, :]).astype(jnp.float32)
    wide_qkv, wide_out, wide_up, wide_down = (
        lax.all_gather(w_qkv, "row", axis=1, tiled=True),
        lax.all_gather(w_out, "row", axis=1, tiled=True),
        lax.all_gather(w_up, "row", axis=0, tiled=True),
        lax.all_gather(w_down, "row", axis=1, tiled=True),
    )
    inputs = tokens.astype(jnp.float32)
    normal_one, inverse_one = norm_split(inputs, feature_width)
    normed_part = (normal_one * own_part(ln1_gain, 0) + own_part(ln1_bias, 0)).astype(jnp.bfloat16)
    normed_one = gather_features(normed_part)
    projected = mult("td,kde->kte", normed_one, wide_qkv)
    kept_qkv = select_rows(mult("td,dj->tj", normed_one, a_qkv), onehot, image_len)
    projected = projected + mult("tkj,kje->kte", kept_qkv.reshape(row_count, 3, stack_width), b_qkv)
    bias_rows = jnp.stack([qv_bias[0], jnp.zeros_like(qv_bias[0]), qv_bias[1]])[:, None, :]
    qkv = (projected + bias_rows).astype(jnp.bfloat16)
    shaped = qkv.reshape(3, image_count, image_len, head_count, HD)
    queries, key_rows, value_rows = (shaped[0], shaped[1], shaped[2])
    scores = mult("bqhd,bkhd->bhqk", queries, key_rows) * scale
    highest = jnp.max(scores, axis=-1, keepdims=True)
    log_total = highest + jnp.log(jnp.sum(jnp.exp(scores - highest), axis=-1, keepdims=True))
    weights_low = jnp.exp(scores - log_total).astype(jnp.bfloat16)
    attended = mult("bhqk,bkhd->bqhd", weights_low, value_rows)
    attended = attended.reshape(row_count, part_width).astype(jnp.bfloat16)
    kept_out = select_rows(mult("tc,cj->tj", attended, a_out), onehot, image_len)
    out_terms = mult("tc,cd->td", attended, wide_out) + mult("tj,jd->td", kept_out, b_out)
    hidden = inputs + sum_partials(out_terms) + own_part(out_bias, 0)
    normal_two, inverse_two = norm_split(hidden, feature_width)
    normed_part_two = (normal_two * own_part(ln2_gain, 0) + own_part(ln2_bias, 0)).astype(
        jnp.bfloat16
    )
    normed_two = gather_features(normed_part_two)
    kept_up = select_rows(mult("td,dj->tj", normed_two, a_up), onehot, image_len)
    pre_up = mult("td,df->tf", normed_two, wide_up) + mult("tj,jf->tf", kept_up, b_up) + up_bias
    logistic = jax.nn.sigmoid(GELU_SCALE * pre_up)
    activated = (pre_up * logistic).astype(jnp.bfloat16)
    kept_down = select_rows(mult("tf,fj->tj", activated, a_down), onehot, image_len)
    down_terms = mult("tf,fd->td", activated, wide_down) + mult("tj,jd->td", kept_down, b_down)
    layer_out = (hidden + sum_partials(down_terms) + own_part(down_bias, 0)).astype(jnp.bfloat16)
    wide_qkv, wide_out, wide_up, wide_down = (
        lax.all_gather(w_qkv, "row", axis=1, tiled=True),
        lax.all_gather(w_out, "row", axis=1, tiled=True),
        lax.all_gather(w_up, "row", axis=0, tiled=True),
        lax.all_gather(w_down, "row", axis=1, tiled=True),
    )
    grad_layer = cotangent.astype(jnp.float32)
    grad_full = gather_features(cotangent)
    d_low_down = select_rows(mult("td,jd->tj", grad_full, b_down), onehot, image_len)
    d_activated = mult("td,fd->tf", grad_full, wide_down) + mult("tj,fj->tf", d_low_down, a_down)
    grad_b_down = mult("tj,td->jd", kept_down, grad_full)
    grad_a_down = mult("tf,tj->fj", activated, d_low_down)
    d_pre_up = (
        d_activated * (logistic + GELU_SCALE * pre_up * logistic * (1.0 - logistic))
    ).astype(jnp.bfloat16)
    d_low_up = select_rows(mult("tf,jf->tj", d_pre_up, b_up), onehot, image_len)
    grad_b_up = mult("tj,tf->jf", kept_up, d_pre_up)
    grad_a_up = mult("td,tj->dj", normed_two, d_low_up)
    normed_two_terms = mult("tf,df->td", d_pre_up, wide_up) + mult("tj,dj->td", d_low_up, a_up)
    d_normed_two = sum_partials(normed_two_terms)
    grad_hidden = grad_layer + norm_back(
        d_normed_two, normal_two, inverse_two, own_part(ln2_gain, 0), feature_width
    )
    hidden_full_grad = gather_features(grad_hidden.astype(jnp.bfloat16))
    d_low_out = select_rows(mult("td,jd->tj", hidden_full_grad, b_out), onehot, image_len)
    d_attended = mult("td,cd->tc", hidden_full_grad, wide_out) + mult("tj,cj->tc", d_low_out, a_out)
    grad_b_out = mult("tj,td->jd", kept_out, hidden_full_grad)
    grad_a_out = mult("tc,tj->cj", attended, d_low_out)
    d_heads = d_attended.astype(jnp.bfloat16).reshape(image_count, image_len, head_count, HD)
    scores_again = mult("bqhd,bkhd->bhqk", queries, key_rows) * scale
    weights_again = jnp.exp(scores_again - log_total)
    weights_again_low = weights_again.astype(jnp.bfloat16)
    d_weights = mult("bqhd,bkhd->bhqk", d_heads, value_rows)
    d_values = mult("bhqk,bqhd->bkhd", weights_again_low, d_heads)
    d_scores = weights_again * (
        d_weights - jnp.sum(weights_again * d_weights, axis=-1, keepdims=True)
    )
    d_scores = d_scores.astype(jnp.bfloat16)
    d_queries = scale * mult("bhqk,bkhd->bqhd", d_scores, key_rows)
    d_keys = scale * mult("bhqk,bqhd->bkhd", d_scores, queries)
    d_qkv = (
        jnp.stack([d_queries, d_keys, d_values])
        .reshape(3, row_count, part_width)
        .astype(jnp.bfloat16)
    )
    d_low_qkv = mult("kte,kje->tkj", d_qkv, b_qkv)
    d_low_qkv = select_rows(d_low_qkv.reshape(row_count, 3 * stack_width), onehot, image_len)
    grad_b_qkv = mult("tkj,kte->kje", kept_qkv.reshape(row_count, 3, stack_width), d_qkv)
    grad_a_qkv = mult("td,tj->dj", normed_one, d_low_qkv)
    normed_one_terms = mult("kte,kde->td", d_qkv, wide_qkv) + mult("tj,dj->td", d_low_qkv, a_qkv)
    d_normed_one = sum_partials(normed_one_terms)
    tokens_grad = grad_hidden + norm_back(
        d_normed_one, normal_one, inverse_one, own_part(ln1_gain, 0), feature_width
    )
    grad_a_qkv, grad_b_out, grad_a_up, grad_b_down = lax.psum(
        (grad_a_qkv, grad_b_out, grad_a_up, grad_b_down), ("row", "col")
    )
    grad_b_qkv, grad_a_out, grad_b_up, grad_a_down = (
        lax.psum(grad_b_qkv.astype(jnp.bfloat16), "row").astype(jnp.float32),
        lax.psum(grad_a_out.astype(jnp.bfloat16), "row").astype(jnp.float32),
        lax.psum(grad_b_up.astype(jnp.bfloat16), "row").astype(jnp.float32),
        lax.psum(grad_a_down.astype(jnp.bfloat16), "row").astype(jnp.float32),
    )
    return (
        layer_out,
        tokens_grad,
        grad_a_qkv,
        grad_b_qkv,
        grad_a_out,
        grad_b_out,
        grad_a_up,
        grad_b_up,
        grad_a_down,
        grad_b_down,
    )


NT = (((1,), (1,)), ((), ()))
NN = (((1,), (0,)), ((), ()))
F32 = jnp.float32
BF16 = jnp.bfloat16
VMEM_SMALL, VMEM_LARGE = 36 * 1024 * 1024, 60 * 1024 * 1024
SPOT = pl.BlockSpec(memory_space=pltpu.SMEM)


def dot(first, second, dims=NN):
    return lax.dot_general(first, second, dims, preferred_element_type=F32)


def dot_rows(first, second):
    return dot(first.T, second)


def call(body, grid, in_specs, out_specs, out_shape, scratch=(), us=None):
    return pl.pallas_call(
        body,
        grid=grid,
        in_specs=in_specs,
        out_specs=out_specs,
        out_shape=out_shape,
        scratch_shapes=list(scratch),
        compiler_params=pltpu.CompilerParams(
            dimension_semantics=("arbitrary",) * len(grid),
            vmem_limit_bytes=VMEM_LARGE if us is None else VMEM_SMALL,
        ),
        cost_estimate=None
        if us is None
        else pl.CostEstimate(
            flops=us * 900_000_000, bytes_accessed=1_000_000, transcendentals=0
        ),
    )


def fixed(shape):
    zeros = (0,) * len(shape)
    return pl.BlockSpec(shape, lambda *_: zeros, pipeline_mode=pl.Buffered(1))


def struct(shape, kind):
    return jax.ShapeDtypeStruct(shape, kind)


def norm_of(values):
    centred = values - jnp.mean(values, axis=1, keepdims=True)
    inverse = lax.rsqrt(jnp.mean(centred * centred, axis=1, keepdims=True) + EPS)
    return centred * inverse, inverse


def norm_pull(grad, normal, inverse, gain):
    scaled = grad * gain
    return inverse * (
        scaled
        - jnp.mean(scaled, axis=1, keepdims=True)
        - normal * jnp.mean(scaled * normal, axis=1, keepdims=True)
    )


def settle(place, pieces, side_first, store):
    depth = pieces[0].shape[0]
    n_far = depth // 2
    for group, piece in enumerate(pieces):
        for index in range(depth):
            other, outer, inner, back = (
                group // 2, group % 2, index // n_far, index % n_far
            )
            x_off, y_off = (outer, inner) if side_first else (inner, outer)
            far = lax.rem(place[0] + (n_far - back), n_far)
            x = place[1] if x_off == 0 else 1 - place[1]
            core = place[2] if other == 0 else 1 - place[2]
            y = place[3] if y_off == 0 else 1 - place[3]
            store(far * 4 + x * 2 + core, y, piece[index])


def settle_qkv(place, pieces0, pieces1, w_ref):
    half = pieces1[0].shape[2]

    def lanes(y):
        return pl.ds(pl.multiple_of(y * half, half), half)

    def first(row, y, block):
        w_ref[0, row, :, lanes(y)] = block[:, :half]
        w_ref[1, row, :, lanes(y)] = block[:, half:]

    def last(row, y, block):
        w_ref[2, row, :, lanes(y)] = block

    settle(place, pieces0, False, first)
    settle(place, pieces1, True, last)


def settle_out(place, pieces1, w_ref):
    half = pieces1[0].shape[2]

    def store(row, y, block):
        w_ref[row, :, pl.ds(pl.multiple_of(y * half, half), half)] = block

    settle(place, pieces1, True, store)


def chosen(index, first, second):
    return jnp.where(index == 0, first, second)


def both_halves(place, own, near, far):
    diagonal = place[2] == place[3]
    mine = jnp.where(diagonal, own, near)
    other = jnp.where(diagonal, near, far)
    return chosen(place[3], mine, other), chosen(place[3], other, mine)


def halves_out(place, values, rows, own_ref, near_ref, far_ref):
    half = values.shape[1] // 2
    left, right = values[:, :half], values[:, half:]
    mine, other = chosen(place[3], left, right), chosen(place[3], right, left)
    own_ref[rows, :] = mine
    near_ref[rows, :] = jnp.where(place[2] == place[3], other, mine)
    far_ref[rows, :] = other


def spread_body(length, cut, own_rows, tb, place, t_ref, own_ref, near_ref, far_ref, wide_ref):
    wide_ref[...] = t_ref[...].astype(F32)

    def put(ref, start, shared, shared_count):
        ref[:length, :] = wide_ref[start : start + length, :].astype(BF16)
        ref[own_rows : own_rows + shared_count, :] = wide_ref[
            shared : shared + shared_count, :
        ].astype(BF16)

    for ref, index in ((own_ref, place[2]), (near_ref, 1 - place[3]), (far_ref, 1 - place[2])):
        ref[...] = jnp.zeros_like(ref)

        @pl.when(index == 0)
        def _():
            put(ref, 0, length, cut)

        @pl.when(index == 1)
        def _():
            put(ref, 2 * length, length + cut, length - cut)


def join_body(length, cut, own_rows, pieces, place, *refs):
    *in_refs, out_ref, wide_ref = refs

    def whole(part):
        found = [ref[...] for ref in in_refs[part * pieces : (part + 1) * pieces]]
        return found[0] if pieces == 1 else jnp.concatenate(found)

    own, near, far = whole(0), whole(1), whole(2)
    diagonal = place[2] == place[3]
    mine = jnp.where(diagonal, own, near)
    mate = jnp.where(diagonal, near, far)
    first = chosen(place[2], mine, mate).astype(F32)
    second = chosen(place[2], mate, mine).astype(F32)
    wide_ref[:length, :] = first[:length]
    wide_ref[length : length + cut, :] = first[own_rows : own_rows + cut]
    wide_ref[length + cut : 2 * length, :] = second[own_rows : own_rows + length - cut]
    wide_ref[2 * length :, :] = second[:length]
    out_ref[...] = wide_ref[...].astype(out_ref.dtype)


def qkv_body(
    scale, place, own_ref, near_ref, far_ref, gain, bias, p0, p1, p2, p3, r0, r1, r2, r3, a_ref,
    b_ref, qv_ref, sel_ref, x_ref, z_ref, u_ref, out_ref, keep_out, send_out, w_ref,
):
    width = x_ref.shape[1]
    half = width // 2
    stack = sel_ref.shape[1]

    @pl.when(pl.program_id(0) == 0)
    def _():
        settle_qkv(place, (p0, p1, p2, p3), (r0, r1, r2, r3), w_ref)

    left, right = both_halves(place, own_ref[...], near_ref[...], far_ref[...])
    x = jnp.concatenate([left, right], axis=1)
    x_ref[...] = x
    normal, _ = norm_of(x.astype(F32))
    z = (normal * gain[...] + bias[...]).astype(BF16)
    z_ref[...] = z
    low = dot(z, a_ref[...])
    for k in range(3):
        kept = (low[:, k * stack : (k + 1) * stack] * sel_ref[...]).astype(BF16)
        u_ref[:, k * stack : (k + 1) * stack] = kept
        w = w_ref[k].reshape(width, width)
        parts = []
        for y in range(2):
            lanes = slice(y * half, (y + 1) * half)
            acc = dot(z, w[:, lanes]) + dot(kept, b_ref[y, :, k * half : (k + 1) * half])
            out = (acc + qv_ref[k, :, lanes]).astype(BF16)
            if k == 0:
                out = out * jnp.asarray(scale, BF16)
            out_ref[k, :, lanes] = out
            parts.append(out)
        keep_out[k] = chosen(place[2], parts[0], parts[1])
        send_out[k] = chosen(place[2], parts[1], parts[0])


def attend_pairs(pairs, mask, p_ref):
    lane = lax.broadcasted_iota(jnp.int32, mask.shape, 1)
    one, zero = jnp.ones_like(mask), jnp.zeros_like(mask)
    work = []
    for q, k, v in pairs:
        for spare, here in ((HD, lane < HD), (0, lane >= HD)):
            mine = jnp.where(here, q, jnp.where(lane == spare, one, zero))
            work.append((mine, jnp.where(lane == spare, mask, k), v))
    scores, parts = [dot(work[0][0], work[0][1], NT)], []
    for i, (_, _, v) in enumerate(work):
        if i + 1 < len(work):
            scores.append(dot(work[i + 1][0], work[i + 1][1], NT))
        s = scores[i]
        e = jnp.exp(s - jnp.max(s, axis=1, keepdims=True))
        p = (e * (1.0 / jnp.sum(e, axis=1, keepdims=True))).astype(BF16)
        p_ref[i] = p
        parts.append(dot(p, v))
    return [
        jnp.where(lane < HD, parts[i], parts[i + 1]).astype(BF16) for i in range(0, len(parts), 2)
    ]


def pair_lanes(ref):
    return [slice(i, i + 2 * HD) for i in range(0, ref.shape[-1], 2 * HD)]


def attend_body(q_ref, k_ref, v_ref, mask_ref, out_ref, p_ref):
    lanes = pair_lanes(out_ref)
    pairs = [(q_ref[0, :, at], k_ref[0, :, at], v_ref[0, :, at]) for at in lanes]
    for at, out in zip(lanes, attend_pairs(pairs, mask_ref[...], p_ref)):
        out_ref[:, at] = out


def attend_shared_body(mine_ref, mate_ref, mask_ref, keep_ref, send_ref, p_ref):
    lanes = pair_lanes(keep_ref)
    pairs = [
        [jnp.concatenate([mine_ref[i, :, at], mate_ref[i, :, at]]) for i in range(3)]
        for at in lanes
    ]
    count = keep_ref.shape[0]
    for at, out in zip(lanes, attend_pairs(pairs, mask_ref[...], p_ref)):
        keep_ref[:, at] = out[:count]
        send_ref[:, at] = out[count:]


def attend_back_one(scale, q, k, v, p_ref, att, do):
    low_lanes = lax.broadcasted_iota(jnp.int32, q.shape, 1) < HD
    zero = jnp.zeros_like(q)
    product = att.astype(F32) * do.astype(F32)
    do_t, q_t = do.T, q.T
    places = (low_lanes, ~low_lanes)
    dp = [dot(jnp.where(here, do, zero), v, NT) for here in places]
    dv = [dot(do_t[h * HD : (h + 1) * HD], p_ref[h]) for h in range(2)]
    ds = []
    for h, here in enumerate(places):
        delta = jnp.sum(jnp.where(here, product, 0.0), axis=1, keepdims=True)
        ds.append((p_ref[h].astype(F32) * (dp[h] - delta)).astype(BF16))
    dq = sum(dot(ds[h], jnp.where(here, k, zero)) for h, here in enumerate(places))
    dk = [dot(q_t[h * HD : (h + 1) * HD], ds[h]) for h in range(2)]
    dk, dv = (jnp.concatenate(t).astype(BF16).T for t in (dk, dv))
    return (dq * scale).astype(BF16), dk, dv


def attend_back_body(scale, q_ref, k_ref, v_ref, p_ref, att_ref, do_ref, out_ref):
    parts = attend_back_one(
        scale, q_ref[0], k_ref[0], v_ref[0], p_ref, att_ref[...], do_ref[...]
    )
    for i in range(3):
        out_ref[i] = parts[i]


def attend_back_shared_body(
    scale, mine_ref, mate_ref, p_ref, att_keep, att_send, do_keep, do_mate, keep_ref, send_ref
):
    q, k, v = (jnp.concatenate([mine_ref[i], mate_ref[i]]) for i in range(3))
    att = jnp.concatenate([att_keep[...], att_send[...]])
    do = jnp.concatenate([do_keep[...], do_mate[...]])
    parts = attend_back_one(scale, q, k, v, p_ref, att, do)
    count = keep_ref.shape[1]
    for i in range(3):
        keep_ref[i] = parts[i][:count]
        send_ref[i] = parts[i][count:]


def out_body(
    place, own_ref, keep_ref, mate_ref, x_ref, r0, r1, r2, r3, a_ref, b_ref, bias_ref, gain,
    lbias, aup_ref, sel_ref, hid_ref, z_ref, u_ref, uup_ref, w_ref,
):
    width = x_ref.shape[1]
    half = width // 2

    @pl.when(pl.program_id(0) == 0)
    def _():
        settle_out(place, (r0, r1, r2, r3), w_ref)

    keep, mate = keep_ref[...], mate_ref[...]
    shared = jnp.concatenate(
        [chosen(place[2], keep, mate), chosen(place[2], mate, keep)], axis=1
    )
    att = jnp.where(pl.program_id(0) < 2, own_ref[...], shared)
    sel = sel_ref[...]
    low = dot(att[:, :half], a_ref[0], NT) + dot(att[:, half:], a_ref[1], NT)
    kept = (low * sel).astype(BF16)
    u_ref[...] = kept
    acc = dot(att, w_ref[...].reshape(width, width), NT) + dot(kept, b_ref[...])
    hidden = x_ref[...].astype(F32) + acc + bias_ref[...]
    hid_ref[...] = hidden
    normal, _ = norm_of(hidden)
    z = (normal * gain[...] + lbias[...]).astype(BF16)
    z_ref[...] = z
    uup_ref[...] = (dot(z, aup_ref[...]) * sel).astype(BF16)


def mlp_body(
    rows, place, z_ref, gown_ref, gnear_ref, gfar_ref, uup_ref, sel_ref, hid_ref, wup_ref,
    wdn_ref, bup_own, bup_near, bup_far, adn_own, adn_near, adn_far, upb_ref, bdn_ref, aup_ref,
    dnb_ref, gain,
    own_ref, near_ref, far_ref, ghb_ref, ekeep_ref, esend_ref,
    down_acc, dz_acc, udn_acc, eup_acc, edn_ref, uup_t, edn_t, gy_ref, hid_buf, hid_sem,
):
    total, width = z_ref.shape
    step = pl.program_id(0)
    blocks = [slice(i, i + rows) for i in range(0, total, rows)]

    fetch = pltpu.make_async_copy(hid_ref, hid_buf, hid_sem)

    @pl.when(step == 0)
    def _():
        fetch.start()
        for b in blocks:
            left, right = both_halves(place, gown_ref[b, :], gnear_ref[b, :], gfar_ref[b, :])
            gy = jnp.concatenate([left, right], axis=1)
            gy_ref[b, :] = gy
            edn_ref[b, :] = (dot(gy, bdn_ref[...], NT) * sel_ref[b, :]).astype(BF16)
        edn_t[...] = edn_ref[...].T
        uup_t[...] = uup_ref[...].T
        down_acc[...] = jnp.zeros_like(down_acc)
        dz_acc[...] = jnp.zeros_like(dz_acc)
        udn_acc[...] = jnp.zeros_like(udn_acc)
        eup_acc[...] = jnp.zeros_like(eup_acc)

    chunk = upb_ref.shape[1]
    wup = wup_ref[...].reshape(width, chunk)
    wdn = wdn_ref[...].reshape(width, chunk)
    parts = pl.num_programs(0) // 2
    y = step // parts

    def adapter(own_ref, near_ref, far_ref):
        near, far = near_ref[...], far_ref[...]
        other = jnp.concatenate([chosen(place[2], near, far), chosen(place[2], far, near)])
        return jnp.where(place[3] == y, own_ref[...], other)

    bup = adapter(bup_own, bup_near, bup_far)
    adn = adapter(adn_own, adn_near, adn_far)
    pre = dot(z_ref[...], wup) + dot(uup_ref[...], bup) + upb_ref[...]
    d_act = dot(gy_ref[...], wdn) + dot(edn_ref[...], adn)
    bent = (0.5 * GELU_SCALE) * pre
    turn = jnp.tanh(bent)
    q = 0.5 + 0.5 * turn
    act = (pre * q).astype(BF16)
    d_up = (d_act * (q + q * (bent * (1.0 - turn)))).astype(BF16)
    down_acc[...] += dot(act, wdn, NT)
    dz_acc[...] += dot(d_up, wup, NT)
    udn_acc[...] += dot(act, adn, NT)
    eup_acc[...] += dot(d_up, bup, NT)
    hidden_half = parts * chunk
    for i, (low, high) in enumerate(((uup_t, d_up), (edn_t, act))):
        found = split_rows(place, dot(low[...], high).astype(BF16))
        lanes = pl.ds(pl.multiple_of(i * hidden_half + step % parts * chunk, chunk), chunk)
        ekeep_ref[y, :, lanes], esend_ref[y, :, lanes] = found

    @pl.when(step == pl.num_programs(0) - 1)
    def _():
        fetch.wait()
        gbdn = gaup = 0.0
        for b in blocks:
            sel = sel_ref[b, :]
            e_up = (eup_acc[b, :] * sel).astype(BF16)
            u_dn = (udn_acc[b, :] * sel).astype(BF16)
            hidden = hid_buf[b, :]
            y = hidden + down_acc[b, :] + dot(u_dn, bdn_ref[...]) + dnb_ref[...]
            halves_out(place, y.astype(BF16), b, own_ref, near_ref, far_ref)
            dz = dz_acc[b, :] + dot(e_up, aup_ref[...], NT)
            normal, inverse = norm_of(hidden)
            grad = gy_ref[b, :].astype(F32) + norm_pull(dz, normal, inverse, gain[...])
            ghb_ref[b, :] = grad.astype(BF16)
            gbdn = gbdn + dot_rows(u_dn, gy_ref[b, :])
            gaup = gaup + dot_rows(e_up, z_ref[b, :])
        half = width // 2
        for i, grad in enumerate((gaup, gbdn)):
            start = 2 * hidden_half + i * half
            for column in range(2):
                rows = split_rows(place, grad[:, column * half : (column + 1) * half].astype(BF16))
                lanes = slice(start, start + half)
                ekeep_ref[column, :, lanes], esend_ref[column, :, lanes] = rows


def split_rows(place, grad):
    part = grad.shape[0] // 2
    low, high = grad[:part], grad[part:]
    return chosen(place[2], low, high), chosen(place[2], high, low)


def out_back_body(
    place, g_ref, own_ref, keep_ref, mate_ref, r0, r1, r2, r3, a_ref, b_ref, sel_ref, u_ref,
    d_own, d_keep, d_send, g_keep, g_send, w_ref, e_ref, e_t,
):
    width = g_ref.shape[1]
    half = width // 2
    count = keep_ref.shape[0]
    y = pl.program_id(0)

    @pl.when(y == 0)
    def _():
        def store(row, column, block):
            w_ref[column, row] = block

        settle(place, (r0, r1, r2, r3), True, store)
        e = (dot(g_ref[...], b_ref[...], NT) * sel_ref[...]).astype(BF16)
        e_ref[...] = e
        e_t[...] = e.T
        gb = dot(u_ref[...].T, g_ref[...]).astype(BF16)
        for column in range(2):
            rows = split_rows(place, gb[:, column * half : (column + 1) * half])
            g_keep[column, :, half:], g_send[column, :, half:] = rows

    w = w_ref[y].reshape(width, half)
    d = (dot(g_ref[...], w) + dot(e_ref[...], a_ref[0])).astype(BF16)
    d_own[...] = d[: 2 * count]

    shared = jnp.where(place[2] == y, keep_ref[...], mate_ref[...])
    ga = dot(e_t[...], jnp.concatenate([own_ref[...], shared])).astype(BF16)
    g_keep[y, :, :half], g_send[y, :, :half] = split_rows(place, ga)

    @pl.when(place[2] == y)
    def _():
        d_keep[...] = d[2 * count :]

    @pl.when(place[2] != y)
    def _():
        d_send[...] = d[2 * count :]


def shared_halves(place, keep, mate):
    return chosen(place[2], keep, mate), chosen(place[2], mate, keep)


def qkv_grads_body(
    place, left_ref, right_ref, keep_ref, mate_ref, b_ref, sel_ref, u_ref, z_ref, e_ref,
    keep_out, send_out,
):
    half = left_ref.shape[2]
    part = sel_ref.shape[1] // 2
    shared = shared_halves(place, keep_ref[0], mate_ref[0])
    u_t = u_ref[...].T

    def put(grad, y, i):
        low, high = grad[:part], grad[part:]
        keep_out[y, i, 0] = chosen(place[2], low, high)
        send_out[y, i, 0] = chosen(place[2], high, low)

    low = 0.0
    for y, own_ref in enumerate((left_ref, right_ref)):
        d = jnp.concatenate([own_ref[0], shared[y]])
        low = low + dot(d, b_ref[y], NT)
        put(dot(u_t, d).astype(BF16), y, 0)
    e = (low * sel_ref[...]).astype(BF16)
    e_ref[...] = e
    ga = dot(e.T, z_ref[...]).astype(BF16)
    for y in range(2):
        put(ga[:, y * half : (y + 1) * half], y, 1)


def qkv_back_body(
    shared, place, left_ref, right_ref, p0, p1, p2, p3, r0, r1, r2, r3, a_ref, e_ref, x_ref,
    gh_ref, gain, own_out, near_out, far_out, w_ref,
):
    width = x_ref.shape[1]
    settle_qkv(place, (p0, p1, p2, p3), (r0, r1, r2, r3), w_ref)
    dz = dot(e_ref[...], a_ref[...], NT)
    for k in range(3):
        left, right = left_ref[k], right_ref[k]
        if shared:
            left, right = shared_halves(place, left, right)
        d = jnp.concatenate([left, right], axis=1)
        dz = dz + dot(d, w_ref[k].reshape(width, width), NT)
    normal, inverse = norm_of(x_ref[...].astype(F32))
    grad = gh_ref[...].astype(F32) + norm_pull(dz, normal, inverse, gain[...])
    halves_out(place, grad.astype(BF16), slice(None), own_out, near_out, far_out)


def on_chip_pair(
    mesh_shape, tokens, cotangent, ln1_gain, ln1_bias, ln2_gain, ln2_bias, w_qkv, qv_bias, w_out,
    out_bias, w_up, up_bias, w_down, down_bias, adapter_ids, a_qkv, b_qkv, a_out, b_out, a_up,
    b_up, a_down, b_down,
):
    n_row, n_col = mesh_shape
    count, half = tokens.shape
    width = half * 2
    stack = b_out.shape[0]
    part = stack // 2
    hidden_half = w_up.shape[1]
    hidden = hidden_half * 2
    length = count // adapter_ids.shape[0]
    cut = length // 2
    heads = width // HD
    tb = -(-(length + 1) // 32) * 16
    own_rows, total = 2 * tb, 3 * tb
    scale = HD ** (-0.5)
    both = ("row", "col")
    row, col = lax.axis_index("row"), lax.axis_index("col")
    core, side, n_far = row % 2, row // 2 % 2, n_row // 4
    place = jnp.stack([row // 4, side, core, col]).astype(jnp.int32)

    def device(r, c):
        return r * n_col + c

    far_swaps = [[] for _ in range(n_far.bit_length() - 1)]
    far_turns = [[] for _ in range(n_far - 1)]
    ring_in, ring_back, cross, cores, cols_swap, sides_swap = [], [], [], [], [], []
    for r in range(n_row):
        for c in range(n_col):
            k, mate = r % 2, r + 1 - 2 * (r % 2)
            cores.append((device(r, c), device(mate, c)))
            cols_swap.append((device(r, c), device(r, 1 - c)))
            sides_swap.append((device(r, c), device(r ^ 2, c)))
            for turn, pairs in enumerate(far_turns):
                pairs.append((device(r, c), device((r + 4 * (turn + 1)) % n_row, c)))
            for bit, pairs in enumerate(far_swaps):
                pairs.append((device(r, c), device(r ^ (4 << bit), c)))
            if k != c:
                ring_in.append((device(r, c), device(r, 1 - c)))
                ring_back.append((device(r, c), device(mate, c)))
                cross.append((device(r, c), device(mate, 1 - c)))
            else:
                ring_in.append((device(r, c), device(mate, c)))
                ring_back.append((device(r, c), device(r, 1 - c)))

    def move(values, pairs):
        return lax.ppermute(values, both, pairs)

    def pick(pair, index):
        return jnp.where(index == 0, pair[0], pair[1])

    def ordered(mine, other, index, axis):
        return jnp.where(
            index == 0,
            jnp.concatenate([mine, other], axis),
            jnp.concatenate([other, mine], axis),
        )

    def tie(*values):
        return lax.optimization_barrier(values)

    thirds = [struct((total, half), BF16)] * 3
    third_specs = [fixed((total, half))] * 3

    def spread(values):
        return call(
            functools.partial(spread_body, length, cut, own_rows, tb),
            (1,),
            [SPOT, fixed((count, half))],
            third_specs,
            thirds,
            scratch=[pltpu.VMEM((count, half), F32)],
        )(place, values)

    def join(own, near, far, kind):
        return call(
            functools.partial(join_body, length, cut, own_rows, len(own)),
            (1,),
            [SPOT] + [fixed(t.shape) for t in (*own, *near, *far)],
            fixed((count, half)),
            struct((count, half), kind),
            scratch=[pltpu.VMEM((count, half), F32)],
            us=3,
        )(place, *own, *near, *far)

    x_own, x_near, x_far = spread(tokens)
    x_near, x_far, w_qkv, w_out = tie(x_near, x_far, w_qkv, w_out)
    mine_first = jnp.concatenate(
        [jnp.swapaxes(w_qkv, 0, 1).reshape(-1, 3 * half), w_out.T], axis=1
    )
    mine_second = jnp.concatenate([w_up, w_down.T], axis=1)
    adapt_first = jnp.concatenate(
        [jnp.swapaxes(b_qkv, 0, 1).reshape(stack, 3 * half), a_out.T], axis=1
    )
    adapt_second = jnp.concatenate([b_up, a_down.T], axis=1)
    deep = width // n_row

    def turned(block):
        return jnp.stack([block] + [move(block, pairs) for pairs in far_turns])

    def doubled(found, pairs):
        return jnp.concatenate([found, move(found, pairs)])

    def part_of(values):
        return lax.dynamic_slice_in_dim(values, core * part, part, 0)

    def widened(values, near, far):
        return ordered(values[None], ordered(near, far, core, 0)[None], col, 0)

    x_near, x_far = move(x_near, ring_in), move(x_far, cross)
    near0, near1 = turned(mine_first[:, :width]), turned(mine_first[:, width:])
    near0, x_near, x_far, mine_second = tie(near0, x_near, x_far, mine_second)
    near0, near1 = tie(near0, near1)
    x_parts = (x_own, x_near, x_far)
    big_second = lax.all_gather(mine_second, both, axis=0, tiled=False)
    big_second = big_second.reshape(n_row, n_col, deep, 2 * hidden_half)
    near0, near1 = doubled(near0, sides_swap), doubled(near1, cols_swap)
    ad_near = move(part_of(adapt_first), cols_swap)
    biases = jnp.concatenate([qv_bias[0], qv_bias[1], up_bias])[None]
    bias_pair = ordered(biases, move(biases, cols_swap), col, 0)
    ids = jnp.where(core == col, adapter_ids, move(adapter_ids, cores))
    g_own, g_near, g_far = spread(cotangent)
    near0, near1, bias_pair, ids, ad_near = tie(near0, near1, bias_pair, ids, ad_near)
    ad_first = widened(adapt_first, ad_near, move(ad_near, cores))
    last0, last1 = move(near0, cols_swap), move(near1, sides_swap)
    far0, far1 = move(near0, cores), move(near1, cores)
    adapt_part = part_of(adapt_second)
    valid = jnp.arange(own_rows)[:, None]
    here, there = jnp.where(core == 0, cut, length - cut), jnp.where(core == 0, length - cut, cut)

    def mask_of(good):
        return jnp.broadcast_to(jnp.where(good, 0.0, -1e30), (own_rows, 2 * HD)).astype(BF16)

    mask_own = mask_of(valid < length)
    mask_shared = mask_of((valid < here) | ((valid >= tb) & (valid < tb + there)))
    last0, last1, far0, far1, ad_first, g_near, g_far = tie(
        last0, last1, far0, far1, ad_first, g_near, g_far
    )
    last0, adapt_part, adapt_second, mask_own, mask_shared = tie(
        last0, adapt_part, adapt_second, mask_own, mask_shared
    )
    ad_near = move(adapt_part, cols_swap)
    blocks0 = (near0, last0, far0, move(last0, cores))
    blocks1 = (near1, last1, far1, move(last1, cores))
    qv_rows = jnp.stack(
        [
            bias_pair[:, :half].reshape(1, width),
            jnp.zeros((1, width), F32),
            bias_pair[:, half:width].reshape(1, width),
        ]
    )
    up_row = bias_pair[:, width:].reshape(1, hidden)

    owners = lax.iota(jnp.int32, stack) // RANK
    own_id = jnp.where(core == 0, ids[0], ids[2])
    places = lax.iota(jnp.int32, total)[:, None]
    sel = (jnp.where(places < own_rows, own_id, ids[1]) == owners[None]).astype(F32)

    gain1, bias1, gain2, bias2 = (t[None] for t in (ln1_gain, ln1_bias, ln2_gain, ln2_bias))

    rows_block = pl.BlockSpec((tb, width), lambda i: (i, 0))
    sel_block = pl.BlockSpec((tb, stack), lambda i: (i, 0))
    every = fixed((total, width))
    thin = fixed((total, stack))
    vec = fixed((1, width))
    pieces0 = [fixed((n_row // 2, deep, width))] * 4
    pieces1 = [fixed((n_row // 2, deep, half))] * 4
    pieces_out = [
        pl.BlockSpec(
            (n_row // 2, deep, half), lambda *_: (0, 0, 1), pipeline_mode=pl.Buffered(1)
        )
    ] * 4
    w_qkv_room = [pltpu.VMEM((3, n_row, deep, width), BF16)]
    w_out_room = [pltpu.VMEM((n_row, deep, width), BF16)]
    ad_out_spec = pl.BlockSpec(
        (n_col, stack, half), lambda *_: (0, 0, 3), pipeline_mode=pl.Buffered(1)
    )
    low_k = pl.BlockSpec((total, stack), lambda k: (0, k))
    shared_k = pl.BlockSpec((1, tb, half), lambda k: (k, 0, 0))
    ad_k = pl.BlockSpec((n_col, stack, half), lambda k: (0, 0, k))
    shared_struct = struct((3, tb, half), BF16)
    half_rows = struct((tb, half), BF16)

    third_rows = pl.BlockSpec((tb, half), lambda i: (i, 0))
    low_block = pl.BlockSpec((tb, 3 * stack), lambda i: (i, 0))
    all_three = pl.BlockSpec((3, tb, width), lambda i: (0, i, 0))
    shared_three = fixed((3, tb, half))
    x, z1, u_qkv, qkv, qkv_keep, qkv_send = call(
        functools.partial(qkv_body, scale),
        (3,),
        [
            SPOT, third_rows, third_rows, third_rows, vec, vec, *pieces0, *pieces1,
            fixed((width, 3 * stack)),
            pl.BlockSpec(
                (n_col, stack, 3 * half), lambda i: (0, 0, 0), pipeline_mode=pl.Buffered(1)
            ),
            fixed((3, 1, width)), sel_block,
        ],
        [rows_block, rows_block, low_block, all_three, shared_three, shared_three],
        [
            struct((total, width), BF16),
            struct((total, width), BF16),
            struct((total, 3 * stack), BF16),
            struct((3, total, width), BF16),
            shared_struct,
            shared_struct,
        ],
        scratch=w_qkv_room,
    )(place, *x_parts, gain1, bias1, *blocks0, *blocks1, a_qkv, ad_first, qv_rows, sel)

    qkv_mate = move(qkv_send, cores)
    qkv, g_near, g_far = tie(qkv, g_near, g_far)
    g_near, g_far = move(g_near, ring_in), move(g_far, cross)

    head_p = pl.BlockSpec((2, own_rows, own_rows), lambda h: (h, 0, 0))
    pair_k = pl.BlockSpec((3, tb, 2 * HD), lambda h: (0, 0, h))
    pair_rows = pl.BlockSpec((tb, 2 * HD), lambda h: (0, h))
    wide = 4 * HD
    att_own, p_own = call(
        attend_body,
        (width // wide,),
        [pl.BlockSpec((1, own_rows, wide), lambda h, k=k: (k, 0, h)) for k in range(3)]
        + [fixed((own_rows, 2 * HD))],
        [
            pl.BlockSpec((own_rows, wide), lambda h: (0, h)),
            pl.BlockSpec((4, own_rows, own_rows), lambda h: (h, 0, 0)),
        ],
        [struct((own_rows, width), BF16), struct((heads, own_rows, own_rows), BF16)],
    )(qkv, qkv, qkv, mask_own)
    qkv_mate, att_own = tie(qkv_mate, att_own)
    wide_k = pl.BlockSpec((3, tb, wide), lambda h: (0, 0, h))
    wide_rows = pl.BlockSpec((tb, wide), lambda h: (0, h))
    att_keep, att_send, p_sh = call(
        attend_shared_body,
        (half // wide,),
        [wide_k, wide_k, fixed((own_rows, 2 * HD))],
        [wide_rows, wide_rows, pl.BlockSpec((4, own_rows, own_rows), lambda h: (h, 0, 0))],
        [half_rows, half_rows, struct((heads // 2, own_rows, own_rows), BF16)],
    )(qkv_keep, qkv_mate, mask_shared)
    att_send, ad_near = tie(att_send, ad_near)
    att_mate = move(att_send, cores)
    g_parts = (g_own, g_near, g_far)
    ad_second = (adapt_second, ad_near, move(ad_near, cores))

    own_block = pl.BlockSpec((tb, width), lambda i: (jnp.minimum(i, 1), 0))
    shared_rows = fixed((tb, half))
    hid, z2, u_out, u_up = call(
        out_body,
        (3,),
        [
            SPOT, own_block, shared_rows, shared_rows, rows_block, *pieces_out,
            ad_out_spec, fixed((stack, width)), vec, vec, vec, fixed((width, stack)), sel_block,
        ],
        [rows_block, rows_block, sel_block, sel_block],
        [
            struct((total, width), F32),
            struct((total, width), BF16),
            struct((total, stack), BF16),
            struct((total, stack), BF16),
        ],
        scratch=w_out_room,
    )(
        place, att_own, att_keep, att_mate, x, *blocks1, ad_first, b_out, out_bias[None],
        gain2, bias2, a_up, sel,
    )

    chunk = half
    parts = hidden_half // chunk

    def w_spec(shift):
        return pl.BlockSpec(
            (n_row, 1, deep, chunk), lambda j: (0, j // parts, 0, j % parts + shift)
        )

    def ad_specs(shift):
        return [
            pl.BlockSpec((rows, chunk), lambda j: (0, j % parts + shift))
            for rows in (stack, part, part)
        ]

    early_half = fixed((2, part, 2 * hidden_half + 2 * half))
    early_struct = struct((2, part, 2 * hidden_half + 2 * half), BF16)
    y_own, y_near, y_far, ghb, early_keep, early_send = call(
        functools.partial(mlp_body, tb),
        (2 * parts,),
        [SPOT, every]
        + third_specs
        + [
            thin, thin, pl.BlockSpec(memory_space=pl.ANY), w_spec(0), w_spec(parts), *ad_specs(0), *ad_specs(parts),
            pl.BlockSpec((1, chunk), lambda j: (0, j)), fixed((stack, width)),
            fixed((width, stack)), vec, vec,
        ],
        third_specs + [every, early_half, early_half],
        thirds
        + [struct((total, width), BF16), early_struct, early_struct],
        scratch=[
            pltpu.VMEM((total, width), F32),
            pltpu.VMEM((total, width), F32),
            pltpu.VMEM((total, stack), F32),
            pltpu.VMEM((total, stack), F32),
            pltpu.VMEM((total, stack), BF16),
            pltpu.VMEM((stack, total), BF16),
            pltpu.VMEM((stack, total), BF16),
            pltpu.VMEM((total, width), BF16),
            pltpu.VMEM((total, width), F32),
            pltpu.SemaphoreType.DMA,
        ],
    )(
        place, z2, *g_parts, u_up, sel, hid, big_second, big_second, *ad_second, *ad_second, up_row,
        b_down, a_up, down_bias[None], gain2,
    )

    def added(kept, sent):
        return (kept.astype(F32) + sent.astype(F32)).astype(BF16)

    quarter = part // 2

    def quarter_of(values, index):
        return lax.dynamic_slice_in_dim(values, index * quarter, quarter, 1)

    def side_sent(values):
        return move(quarter_of(values, 1 - side), sides_swap)

    early_sent = move(early_send, cores)
    y_near, y_far = move(y_near, ring_back), move(y_far, cross)
    out_half = fixed((2, part, width))
    d_att, d_keep, d_send, out_keep, out_send = call(
        out_back_body,
        (2,),
        [
            SPOT, every, pl.BlockSpec((own_rows, half), lambda i: (0, i)), shared_rows,
            shared_rows, *pieces_out,
            pl.BlockSpec((1, stack, half), lambda i: (i, 0, 3)), fixed((stack, width)), thin, thin,
        ],
        [
            pl.BlockSpec((own_rows, half), lambda i: (0, i)), shared_rows, shared_rows, out_half,
            out_half,
        ],
        [
            struct((own_rows, width), BF16),
            half_rows,
            half_rows,
            struct((2, part, width), BF16),
            struct((2, part, width), BF16),
        ],
        scratch=[
            pltpu.VMEM((2, n_row, deep, half), BF16),
            pltpu.VMEM((total, stack), BF16),
            pltpu.VMEM((stack, total), BF16),
        ],
    )(place, ghb, att_own, att_keep, att_mate, *blocks1, ad_first, b_out, sel, u_out)

    d_mate = move(d_send, cores)
    early_sum = jnp.concatenate(
        [added(early_keep, early_sent), added(out_keep, move(out_send, cores))], axis=2
    )
    d_mate, early_sum = tie(d_mate, early_sum)
    early_sent = side_sent(early_sum)

    g_keep, g_send = call(
        functools.partial(attend_back_shared_body, scale),
        (heads // 4,),
        [pair_k, pair_k, head_p, pair_rows, pair_rows, pair_rows, pair_rows],
        [pair_k, pair_k],
        [shared_struct, shared_struct],
        us=8,
    )(qkv_keep, qkv_mate, p_sh, att_keep, att_send, d_keep, d_mate)
    d_att, g_send = tie(d_att, g_send)
    g_mate = move(g_send, cores)
    quarters = heads // 4

    def own_back(shift, d_out):
        return call(
            functools.partial(attend_back_body, scale),
            (quarters,),
            [
                pl.BlockSpec((1, own_rows, 2 * HD), lambda h, k=k: (k, 0, h + shift))
                for k in range(3)
            ]
            + [
                pl.BlockSpec((2, own_rows, own_rows), lambda h: (h + shift, 0, 0)),
                pl.BlockSpec((own_rows, 2 * HD), lambda h: (0, h + shift)),
                pl.BlockSpec((own_rows, 2 * HD), lambda h: (0, h + shift)),
            ],
            pl.BlockSpec((3, own_rows, 2 * HD), lambda h: (0, 0, h)),
            struct((3, own_rows, half), BF16),
            us=9,
        )(qkv, qkv, qkv, p_own, att_own, d_out)

    d_left = own_back(0, d_att)
    early_sum = added(quarter_of(early_sum, side), early_sent)
    d_left, d_att, early_sum, y_near, y_far = tie(d_left, d_att, early_sum, y_near, y_far)
    early_sent = move(pick(early_sum, 1 - col), cols_swap)
    d_right = own_back(quarters, d_att)

    grad_spec = pl.BlockSpec((2, 2, 1, part, half), lambda k: (0, 0, k, 0, 0))
    grad_struct = struct((2, 2, 3, part, half), BF16)
    early_sum = added(pick(early_sum, col), early_sent)
    d_right, early_sum = tie(d_right, early_sum)
    early_sent = move(early_sum, far_swaps[0])
    half_k = pl.BlockSpec((1, own_rows, half), lambda k: (k, 0, 0))
    e_qkv, q_kept, q_sent = call(
        qkv_grads_body,
        (3,),
        [SPOT, half_k, half_k, shared_k, shared_k, ad_k, thin, low_k, every],
        [low_k, grad_spec, grad_spec],
        [struct((total, 3 * stack), BF16), grad_struct, grad_struct],
        us=7,
    )(place, d_left, d_right, g_keep, g_mate, ad_first, sel, u_qkv, z1)

    def side_of(values, index):
        return jnp.where(index == 0, values[:, 0], values[:, 1])

    sums = added(q_kept, move(q_sent, cores)).reshape(2, 2, 3 * part, half)
    early_sum = added(early_sum, early_sent)
    sums, e_qkv, early_sum = tie(sums, e_qkv, early_sum)
    early_sent = move(early_sum, far_swaps[-1])
    q_sent = move(side_of(sums, 1 - side), sides_swap)

    def token_rows(block, left, right):
        at = block % 2
        d_spec = pl.BlockSpec((3, tb, half), lambda i: (0, at, 0), pipeline_mode=pl.Buffered(1))
        rows = pl.BlockSpec((tb, width), lambda i: (block, 0), pipeline_mode=pl.Buffered(1))
        low = pl.BlockSpec((tb, 3 * stack), lambda i: (block, 0), pipeline_mode=pl.Buffered(1))
        return call(
            functools.partial(qkv_back_body, block == 2),
            (1,),
            [
                SPOT, d_spec, d_spec, *pieces0, *pieces1, fixed((width, 3 * stack)), low, rows,
                rows, vec,
            ],
            [shared_rows] * 3,
            [half_rows] * 3,
            scratch=w_qkv_room,
            us=6,
        )(place, left, right, *blocks0, *blocks1, a_qkv, e_qkv, x, ghb, gain1)

    t_own, t_near, t_far = [], [], []

    def sent_rows(own, near, far):
        t_own.append(own)
        t_near.append(move(near, ring_back))
        t_far.append(move(far, cross))

    rows_own, rows_near, rows_far = token_rows(0, d_left, d_right)
    q_sent, rows_near, rows_far = tie(q_sent, rows_near, rows_far)
    sums = added(side_of(sums, side), q_sent)
    sums, d_left, d_right = tie(sums, d_left, d_right)
    q_sent = move(pick(sums, 1 - col), cols_swap)
    sent_rows(rows_own, rows_near, rows_far)
    rows_own, rows_near, rows_far = token_rows(1, d_left, d_right)
    q_sent, rows_near, rows_far, early_sent = tie(q_sent, rows_near, rows_far, early_sent)
    early_sum = added(early_sum, early_sent)
    sums = added(pick(sums, col), q_sent)
    sums, g_keep, g_mate = tie(sums, g_keep, g_mate)
    q_sent = move(sums, far_swaps[1])
    sent_rows(rows_own, rows_near, rows_far)
    edge = 2 * hidden_half
    whole = edge + 4 * half
    split_lanes = [slice(edge, edge + 2 * half), slice(edge + 3 * half, whole)]
    rest = jnp.concatenate([early_sum[:, lanes] for lanes in split_lanes], axis=1)
    rest = move(rest, cols_swap)
    rows_own, rows_near, rows_far = token_rows(2, g_keep, g_mate)
    early_sum = jnp.concatenate([early_sum, rest], axis=1)
    q_sent, rows_near, rows_far, early_sum, y_own, t_near[0], t_far[0] = tie(
        q_sent, rows_near, rows_far, early_sum, y_own, t_near[0], t_far[0]
    )
    sums = added(sums, q_sent)
    q_sent = move(sums, far_swaps[0])
    sent_rows(rows_own, rows_near, rows_far)
    early_sent = move(early_sum, sides_swap)
    layer_out = join([y_own], [y_near], [y_far], BF16)
    q_sent, layer_out, t_near[1], t_far[1] = tie(q_sent, layer_out, t_near[1], t_far[1])
    sums = added(sums, q_sent)
    for pairs in far_swaps[2:]:
        sums = added(sums, move(sums, pairs))
    side_sums = move(sums, sides_swap)
    early_sum = ordered(early_sum, early_sent, side, 0)
    side_sums, t_near[2], t_far[2], early_sum = tie(
        side_sums, t_near[2], t_far[2], early_sum
    )
    early_sent = move(early_sum, cores)
    tokens_grad = join(t_own, t_near, t_far, F32)
    mine = ordered(early_sum, early_sent, core, 0).astype(F32)
    sums = ordered(sums[None], side_sums[None], side, 0)
    a_sent = move(sums[1:], cols_swap)
    own_starts = (edge, edge + half, edge + 3 * half)
    a_up_sum, b_down_sum, b_out_sum = (
        ordered(
            mine[:, start : start + half],
            mine[:, whole + i * half : whole + (i + 1) * half],
            col,
            1,
        )
        for i, start in enumerate(own_starts)
    )
    a_out_sum, a_up_sum = mine[:, edge + 2 * half : edge + 3 * half].T, a_up_sum.T
    b_up_sum, a_down_sum = mine[:, :hidden_half], mine[:, hidden_half:edge].T
    a_sent, tokens_grad, a_out_sum, a_up_sum, b_up_sum, a_down_sum, b_down_sum, b_out_sum = tie(
        a_sent, tokens_grad, a_out_sum, a_up_sum, b_up_sum, a_down_sum, b_down_sum, b_out_sum
    )
    every_sum = jnp.concatenate([sums[:1], ordered(sums[1:], a_sent, col, 0)])
    every_sum = every_sum.reshape(3, 3, part, half)
    every_sum = ordered(every_sum, move(every_sum, cores), core, 2).reshape(3, 3 * stack, half)
    b_sum = every_sum[0].reshape(3, stack, half).astype(F32)
    a_sum = jnp.concatenate([every_sum[1].T, every_sum[2].T]).astype(F32)
    return (
        layer_out,
        tokens_grad,
        a_sum,
        b_sum,
        a_out_sum,
        b_out_sum,
        a_up_sum,
        b_up_sum,
        a_down_sum,
        b_down_sum,
    )


def solution(mesh):
    placed = (
        P("row", "col"),
        P("row", "col"),
        P(),
        P(),
        P(),
        P(),
        P(None, "row", "col"),
        P(None, "col"),
        P("col", "row"),
        P(),
        P("row", "col"),
        P("col"),
        P("col", "row"),
        P(),
        P("row"),
        P(),
        P(None, None, "col"),
        P("col", None),
        P(),
        P(),
        P(None, "col"),
        P("col", None),
        P(),
    )
    shape = (mesh.shape["row"], mesh.shape["col"])
    paired = shape[1] == 2 and shape[0] >= 16 and shape[0] & (shape[0] - 1) == 0
    return jax.shard_map(
        functools.partial(on_chip_pair, shape) if paired else on_device,
        mesh=mesh,
        in_specs=placed,
        out_specs=(
            P("row", "col"),
            P("row", "col"),
            P(),
            P(None, None, "col"),
            P("col", None),
            P(),
            P(),
            P(None, "col"),
            P("col", None),
            P(),
        ),
        check_vma=False,
    )
```

```python
import functools

import jax
import jax.numpy as jnp
from jax import lax
from jax.experimental import pallas as pl
from jax.experimental.pallas import tpu as pltpu
from jax.sharding import PartitionSpec as P

HD = 64
RANK = 16


EPS = 1e-05
GELU_SCALE = 1.702


def column_sums(first, second):
    return lax.psum((first, second), "col")


def gather_features(values):
    return lax.all_gather(values, "col", axis=1, tiled=True)


def sum_partials(terms):
    return lax.psum_scatter(
        terms.astype(jnp.bfloat16), "col", scatter_dimension=1, tiled=True
    ).astype(jnp.float32)


def norm_split(values, feature_width):
    first, second = column_sums(jnp.sum(values, axis=1), jnp.sum(values * values, axis=1))
    centre = first / feature_width
    inverse = lax.rsqrt(second / feature_width - centre * centre + EPS)
    return ((values - centre[:, None]) * inverse[:, None], inverse)


def norm_back(grad_normed, normal_rows, inverse, gain_part, feature_width):
    scaled = grad_normed * gain_part
    first, second = column_sums(jnp.sum(scaled, axis=1), jnp.sum(scaled * normal_rows, axis=1))
    return inverse[:, None] * (
        scaled - first[:, None] / feature_width - normal_rows * second[:, None] / feature_width
    )


def select_rows(low_rank, onehot, image_len):
    image_count, stack_width = onehot.shape
    shaped = low_rank.reshape(image_count, image_len, -1, stack_width)
    return (shaped * onehot[:, None, None, :]).reshape(low_rank.shape).astype(jnp.bfloat16)


def mult(form, first, second):
    return jnp.einsum(form, first, second, preferred_element_type=jnp.float32)


def on_device(
    tokens,
    cotangent,
    ln1_gain,
    ln1_bias,
    ln2_gain,
    ln2_bias,
    w_qkv,
    qv_bias,
    w_out,
    out_bias,
    w_up,
    up_bias,
    w_down,
    down_bias,
    adapter_ids,
    a_qkv,
    b_qkv,
    a_out,
    b_out,
    a_up,
    b_up,
    a_down,
    b_down,
):
    row_count, part_width = tokens.shape
    feature_width = a_qkv.shape[0]
    stack_width = a_qkv.shape[1] // 3
    image_count = adapter_ids.shape[0]
    image_len = row_count // image_count
    head_count = part_width // HD
    scale = HD ** (-0.5)
    offset = lax.axis_index("col") * part_width

    def own_part(values, axis):
        return lax.dynamic_slice_in_dim(values, offset, part_width, axis)

    owners = lax.iota(jnp.int32, stack_width) // RANK
    onehot = (adapter_ids[:, None] == owners[None, :]).astype(jnp.float32)
    wide_qkv, wide_out, wide_up, wide_down = (
        lax.all_gather(w_qkv, "row", axis=1, tiled=True),
        lax.all_gather(w_out, "row", axis=1, tiled=True),
        lax.all_gather(w_up, "row", axis=0, tiled=True),
        lax.all_gather(w_down, "row", axis=1, tiled=True),
    )
    inputs = tokens.astype(jnp.float32)
    normal_one, inverse_one = norm_split(inputs, feature_width)
    normed_part = (normal_one * own_part(ln1_gain, 0) + own_part(ln1_bias, 0)).astype(jnp.bfloat16)
    normed_one = gather_features(normed_part)
    projected = mult("td,kde->kte", normed_one, wide_qkv)
    kept_qkv = select_rows(mult("td,dj->tj", normed_one, a_qkv), onehot, image_len)
    projected = projected + mult("tkj,kje->kte", kept_qkv.reshape(row_count, 3, stack_width), b_qkv)
    bias_rows = jnp.stack([qv_bias[0], jnp.zeros_like(qv_bias[0]), qv_bias[1]])[:, None, :]
    qkv = (projected + bias_rows).astype(jnp.bfloat16)
    shaped = qkv.reshape(3, image_count, image_len, head_count, HD)
    queries, key_rows, value_rows = (shaped[0], shaped[1], shaped[2])
    scores = mult("bqhd,bkhd->bhqk", queries, key_rows) * scale
    highest = jnp.max(scores, axis=-1, keepdims=True)
    log_total = highest + jnp.log(jnp.sum(jnp.exp(scores - highest), axis=-1, keepdims=True))
    weights_low = jnp.exp(scores - log_total).astype(jnp.bfloat16)
    attended = mult("bhqk,bkhd->bqhd", weights_low, value_rows)
    attended = attended.reshape(row_count, part_width).astype(jnp.bfloat16)
    kept_out = select_rows(mult("tc,cj->tj", attended, a_out), onehot, image_len)
    out_terms = mult("tc,cd->td", attended, wide_out) + mult("tj,jd->td", kept_out, b_out)
    hidden = inputs + sum_partials(out_terms) + own_part(out_bias, 0)
    normal_two, inverse_two = norm_split(hidden, feature_width)
    normed_part_two = (normal_two * own_part(ln2_gain, 0) + own_part(ln2_bias, 0)).astype(
        jnp.bfloat16
    )
    normed_two = gather_features(normed_part_two)
    kept_up = select_rows(mult("td,dj->tj", normed_two, a_up), onehot, image_len)
    pre_up = mult("td,df->tf", normed_two, wide_up) + mult("tj,jf->tf", kept_up, b_up) + up_bias
    logistic = jax.nn.sigmoid(GELU_SCALE * pre_up)
    activated = (pre_up * logistic).astype(jnp.bfloat16)
    kept_down = select_rows(mult("tf,fj->tj", activated, a_down), onehot, image_len)
    down_terms = mult("tf,fd->td", activated, wide_down) + mult("tj,jd->td", kept_down, b_down)
    layer_out = (hidden + sum_partials(down_terms) + own_part(down_bias, 0)).astype(jnp.bfloat16)
    wide_qkv, wide_out, wide_up, wide_down = (
        lax.all_gather(w_qkv, "row", axis=1, tiled=True),
        lax.all_gather(w_out, "row", axis=1, tiled=True),
        lax.all_gather(w_up, "row", axis=0, tiled=True),
        lax.all_gather(w_down, "row", axis=1, tiled=True),
    )
    grad_layer = cotangent.astype(jnp.float32)
    grad_full = gather_features(cotangent)
    d_low_down = select_rows(mult("td,jd->tj", grad_full, b_down), onehot, image_len)
    d_activated = mult("td,fd->tf", grad_full, wide_down) + mult("tj,fj->tf", d_low_down, a_down)
    grad_b_down = mult("tj,td->jd", kept_down, grad_full)
    grad_a_down = mult("tf,tj->fj", activated, d_low_down)
    d_pre_up = (
        d_activated * (logistic + GELU_SCALE * pre_up * logistic * (1.0 - logistic))
    ).astype(jnp.bfloat16)
    d_low_up = select_rows(mult("tf,jf->tj", d_pre_up, b_up), onehot, image_len)
    grad_b_up = mult("tj,tf->jf", kept_up, d_pre_up)
    grad_a_up = mult("td,tj->dj", normed_two, d_low_up)
    normed_two_terms = mult("tf,df->td", d_pre_up, wide_up) + mult("tj,dj->td", d_low_up, a_up)
    d_normed_two = sum_partials(normed_two_terms)
    grad_hidden = grad_layer + norm_back(
        d_normed_two, normal_two, inverse_two, own_part(ln2_gain, 0), feature_width
    )
    hidden_full_grad = gather_features(grad_hidden.astype(jnp.bfloat16))
    d_low_out = select_rows(mult("td,jd->tj", hidden_full_grad, b_out), onehot, image_len)
    d_attended = mult("td,cd->tc", hidden_full_grad, wide_out) + mult("tj,cj->tc", d_low_out, a_out)
    grad_b_out = mult("tj,td->jd", kept_out, hidden_full_grad)
    grad_a_out = mult("tc,tj->cj", attended, d_low_out)
    d_heads = d_attended.astype(jnp.bfloat16).reshape(image_count, image_len, head_count, HD)
    scores_again = mult("bqhd,bkhd->bhqk", queries, key_rows) * scale
    weights_again = jnp.exp(scores_again - log_total)
    weights_again_low = weights_again.astype(jnp.bfloat16)
    d_weights = mult("bqhd,bkhd->bhqk", d_heads, value_rows)
    d_values = mult("bhqk,bqhd->bkhd", weights_again_low, d_heads)
    d_scores = weights_again * (
        d_weights - jnp.sum(weights_again * d_weights, axis=-1, keepdims=True)
    )
    d_scores = d_scores.astype(jnp.bfloat16)
    d_queries = scale * mult("bhqk,bkhd->bqhd", d_scores, key_rows)
    d_keys = scale * mult("bhqk,bqhd->bkhd", d_scores, queries)
    d_qkv = (
        jnp.stack([d_queries, d_keys, d_values])
        .reshape(3, row_count, part_width)
        .astype(jnp.bfloat16)
    )
    d_low_qkv = mult("kte,kje->tkj", d_qkv, b_qkv)
    d_low_qkv = select_rows(d_low_qkv.reshape(row_count, 3 * stack_width), onehot, image_len)
    grad_b_qkv = mult("tkj,kte->kje", kept_qkv.reshape(row_count, 3, stack_width), d_qkv)
    grad_a_qkv = mult("td,tj->dj", normed_one, d_low_qkv)
    normed_one_terms = mult("kte,kde->td", d_qkv, wide_qkv) + mult("tj,dj->td", d_low_qkv, a_qkv)
    d_normed_one = sum_partials(normed_one_terms)
    tokens_grad = grad_hidden + norm_back(
        d_normed_one, normal_one, inverse_one, own_part(ln1_gain, 0), feature_width
    )
    grad_a_qkv, grad_b_out, grad_a_up, grad_b_down = lax.psum(
        (grad_a_qkv, grad_b_out, grad_a_up, grad_b_down), ("row", "col")
    )
    grad_b_qkv, grad_a_out, grad_b_up, grad_a_down = (
        lax.psum(grad_b_qkv.astype(jnp.bfloat16), "row").astype(jnp.float32),
        lax.psum(grad_a_out.astype(jnp.bfloat16), "row").astype(jnp.float32),
        lax.psum(grad_b_up.astype(jnp.bfloat16), "row").astype(jnp.float32),
        lax.psum(grad_a_down.astype(jnp.bfloat16), "row").astype(jnp.float32),
    )
    return (
        layer_out,
        tokens_grad,
        grad_a_qkv,
        grad_b_qkv,
        grad_a_out,
        grad_b_out,
        grad_a_up,
        grad_b_up,
        grad_a_down,
        grad_b_down,
    )


NT = (((1,), (1,)), ((), ()))
NN = (((1,), (0,)), ((), ()))
F32 = jnp.float32
BF16 = jnp.bfloat16
VMEM_SMALL, VMEM_LARGE = 36 * 1024 * 1024, 60 * 1024 * 1024
SPOT = pl.BlockSpec(memory_space=pltpu.SMEM)


def dot(first, second, dims=NN):
    return lax.dot_general(first, second, dims, preferred_element_type=F32)


def dot_rows(first, second):
    return dot(first.T, second)


def call(body, grid, in_specs, out_specs, out_shape, scratch=(), us=None):
    return pl.pallas_call(
        body,
        grid=grid,
        in_specs=in_specs,
        out_specs=out_specs,
        out_shape=out_shape,
        scratch_shapes=list(scratch),
        compiler_params=pltpu.CompilerParams(
            dimension_semantics=("arbitrary",) * len(grid),
            vmem_limit_bytes=VMEM_LARGE if us is None else VMEM_SMALL,
        ),
        cost_estimate=None
        if us is None
        else pl.CostEstimate(
            flops=us * 900_000_000, bytes_accessed=1_000_000, transcendentals=0
        ),
    )


def fixed(shape):
    zeros = (0,) * len(shape)
    return pl.BlockSpec(shape, lambda *_: zeros, pipeline_mode=pl.Buffered(1))


def struct(shape, kind):
    return jax.ShapeDtypeStruct(shape, kind)


def norm_of(values):
    centred = values - jnp.mean(values, axis=1, keepdims=True)
    inverse = lax.rsqrt(jnp.mean(centred * centred, axis=1, keepdims=True) + EPS)
    return centred * inverse, inverse


def norm_pull(grad, normal, inverse, gain):
    scaled = grad * gain
    return inverse * (
        scaled
        - jnp.mean(scaled, axis=1, keepdims=True)
        - normal * jnp.mean(scaled * normal, axis=1, keepdims=True)
    )


def settle(place, pieces, side_first, store):
    depth = pieces[0].shape[0]
    n_far = depth // 2
    for group, piece in enumerate(pieces):
        for index in range(depth):
            other, outer, inner, back = (
                group // 2, group % 2, index // n_far, index % n_far
            )
            x_off, y_off = (outer, inner) if side_first else (inner, outer)
            far = lax.rem(place[0] + (n_far - back), n_far)
            x = place[1] if x_off == 0 else 1 - place[1]
            core = place[2] if other == 0 else 1 - place[2]
            y = place[3] if y_off == 0 else 1 - place[3]
            store(far * 4 + x * 2 + core, y, piece[index])


def settle_qkv(place, pieces0, pieces1, w_ref):
    half = pieces1[0].shape[2]

    def lanes(y):
        return pl.ds(pl.multiple_of(y * half, half), half)

    def first(row, y, block):
        w_ref[0, row, :, lanes(y)] = block[:, :half]
        w_ref[1, row, :, lanes(y)] = block[:, half:]

    def last(row, y, block):
        w_ref[2, row, :, lanes(y)] = block

    settle(place, pieces0, False, first)
    settle(place, pieces1, True, last)


def settle_out(place, pieces1, w_ref):
    half = pieces1[0].shape[2]

    def store(row, y, block):
        w_ref[row, :, pl.ds(pl.multiple_of(y * half, half), half)] = block

    settle(place, pieces1, True, store)


def chosen(index, first, second):
    return jnp.where(index == 0, first, second)


def both_halves(place, own, near, far):
    diagonal = place[2] == place[3]
    mine = jnp.where(diagonal, own, near)
    other = jnp.where(diagonal, near, far)
    return chosen(place[3], mine, other), chosen(place[3], other, mine)


def halves_out(place, values, rows, own_ref, near_ref, far_ref):
    half = values.shape[1] // 2
    left, right = values[:, :half], values[:, half:]
    mine, other = chosen(place[3], left, right), chosen(place[3], right, left)
    own_ref[rows, :] = mine
    near_ref[rows, :] = jnp.where(place[2] == place[3], other, mine)
    far_ref[rows, :] = other


def spread_body(length, cut, own_rows, tb, place, t_ref, own_ref, near_ref, far_ref, wide_ref):
    wide_ref[...] = t_ref[...].astype(F32)

    def put(ref, start, shared, shared_count):
        ref[:length, :] = wide_ref[start : start + length, :].astype(BF16)
        ref[own_rows : own_rows + shared_count, :] = wide_ref[
            shared : shared + shared_count, :
        ].astype(BF16)

    for ref, index in ((own_ref, place[2]), (near_ref, 1 - place[3]), (far_ref, 1 - place[2])):
        ref[...] = jnp.zeros_like(ref)

        @pl.when(index == 0)
        def _():
            put(ref, 0, length, cut)

        @pl.when(index == 1)
        def _():
            put(ref, 2 * length, length + cut, length - cut)


def join_body(length, cut, own_rows, pieces, place, *refs):
    *in_refs, out_ref, wide_ref = refs

    def whole(part):
        found = [ref[...] for ref in in_refs[part * pieces : (part + 1) * pieces]]
        return found[0] if pieces == 1 else jnp.concatenate(found)

    own, near, far = whole(0), whole(1), whole(2)
    diagonal = place[2] == place[3]
    mine = jnp.where(diagonal, own, near)
    mate = jnp.where(diagonal, near, far)
    first = chosen(place[2], mine, mate).astype(F32)
    second = chosen(place[2], mate, mine).astype(F32)
    wide_ref[:length, :] = first[:length]
    wide_ref[length : length + cut, :] = first[own_rows : own_rows + cut]
    wide_ref[length + cut : 2 * length, :] = second[own_rows : own_rows + length - cut]
    wide_ref[2 * length :, :] = second[:length]
    out_ref[...] = wide_ref[...].astype(out_ref.dtype)


def qkv_body(
    scale, place, own_ref, near_ref, far_ref, gain, bias, p0, p1, p2, p3, r0, r1, r2, r3, a_ref,
    b_ref, qv_ref, sel_ref, x_ref, z_ref, u_ref, out_ref, keep_out, send_out, w_ref,
):
    width = x_ref.shape[1]
    half = width // 2
    stack = sel_ref.shape[1]

    @pl.when(pl.program_id(0) == 0)
    def _():
        settle_qkv(place, (p0, p1, p2, p3), (r0, r1, r2, r3), w_ref)

    left, right = both_halves(place, own_ref[...], near_ref[...], far_ref[...])
    x = jnp.concatenate([left, right], axis=1)
    x_ref[...] = x
    normal, _ = norm_of(x.astype(F32))
    z = (normal * gain[...] + bias[...]).astype(BF16)
    z_ref[...] = z
    low = dot(z, a_ref[...])
    for k in range(3):
        kept = (low[:, k * stack : (k + 1) * stack] * sel_ref[...]).astype(BF16)
        u_ref[:, k * stack : (k + 1) * stack] = kept
        w = w_ref[k].reshape(width, width)
        parts = []
        for y in range(2):
            lanes = slice(y * half, (y + 1) * half)
            acc = dot(z, w[:, lanes]) + dot(kept, b_ref[y, :, k * half : (k + 1) * half])
            out = (acc + qv_ref[k, :, lanes]).astype(BF16)
            if k == 0:
                out = out * jnp.asarray(scale, BF16)
            out_ref[k, :, lanes] = out
            parts.append(out)
        keep_out[k] = chosen(place[2], parts[0], parts[1])
        send_out[k] = chosen(place[2], parts[1], parts[0])


def attend_pairs(pairs, mask, p_ref):
    lane = lax.broadcasted_iota(jnp.int32, mask.shape, 1)
    one, zero = jnp.ones_like(mask), jnp.zeros_like(mask)
    work = []
    for q, k, v in pairs:
        for spare, here in ((HD, lane < HD), (0, lane >= HD)):
            mine = jnp.where(here, q, jnp.where(lane == spare, one, zero))
            work.append((mine, jnp.where(lane == spare, mask, k), v))
    scores, parts = [dot(work[0][0], work[0][1], NT)], []
    for i, (_, _, v) in enumerate(work):
        if i + 1 < len(work):
            scores.append(dot(work[i + 1][0], work[i + 1][1], NT))
        s = scores[i]
        e = jnp.exp(s - jnp.max(s, axis=1, keepdims=True))
        p = (e * (1.0 / jnp.sum(e, axis=1, keepdims=True))).astype(BF16)
        p_ref[i] = p
        parts.append(dot(p, v))
    return [
        jnp.where(lane < HD, parts[i], parts[i + 1]).astype(BF16) for i in range(0, len(parts), 2)
    ]


def pair_lanes(ref):
    return [slice(i, i + 2 * HD) for i in range(0, ref.shape[-1], 2 * HD)]


def attend_body(q_ref, k_ref, v_ref, mask_ref, out_ref, p_ref):
    lanes = pair_lanes(out_ref)
    pairs = [(q_ref[0, :, at], k_ref[0, :, at], v_ref[0, :, at]) for at in lanes]
    for at, out in zip(lanes, attend_pairs(pairs, mask_ref[...], p_ref)):
        out_ref[:, at] = out


def attend_shared_body(mine_ref, mate_ref, mask_ref, keep_ref, send_ref, p_ref):
    lanes = pair_lanes(keep_ref)
    pairs = [
        [jnp.concatenate([mine_ref[i, :, at], mate_ref[i, :, at]]) for i in range(3)]
        for at in lanes
    ]
    count = keep_ref.shape[0]
    for at, out in zip(lanes, attend_pairs(pairs, mask_ref[...], p_ref)):
        keep_ref[:, at] = out[:count]
        send_ref[:, at] = out[count:]


def attend_back_one(scale, q, k, v, p_ref, att, do):
    low_lanes = lax.broadcasted_iota(jnp.int32, q.shape, 1) < HD
    zero = jnp.zeros_like(q)
    product = att.astype(F32) * do.astype(F32)
    do_t, q_t = do.T, q.T
    places = (low_lanes, ~low_lanes)
    dp = [dot(jnp.where(here, do, zero), v, NT) for here in places]
    dv = [dot(do_t[h * HD : (h + 1) * HD], p_ref[h]) for h in range(2)]
    ds = []
    for h, here in enumerate(places):
        delta = jnp.sum(jnp.where(here, product, 0.0), axis=1, keepdims=True)
        ds.append((p_ref[h].astype(F32) * (dp[h] - delta)).astype(BF16))
    dq = sum(dot(ds[h], jnp.where(here, k, zero)) for h, here in enumerate(places))
    dk = [dot(q_t[h * HD : (h + 1) * HD], ds[h]) for h in range(2)]
    dk, dv = (jnp.concatenate(t).astype(BF16).T for t in (dk, dv))
    return (dq * scale).astype(BF16), dk, dv


def attend_back_body(scale, q_ref, k_ref, v_ref, p_ref, att_ref, do_ref, out_ref):
    parts = attend_back_one(
        scale, q_ref[0], k_ref[0], v_ref[0], p_ref, att_ref[...], do_ref[...]
    )
    for i in range(3):
        out_ref[i] = parts[i]


def attend_back_shared_body(
    scale, mine_ref, mate_ref, p_ref, att_keep, att_send, do_keep, do_mate, keep_ref, send_ref
):
    q, k, v = (jnp.concatenate([mine_ref[i], mate_ref[i]]) for i in range(3))
    att = jnp.concatenate([att_keep[...], att_send[...]])
    do = jnp.concatenate([do_keep[...], do_mate[...]])
    parts = attend_back_one(scale, q, k, v, p_ref, att, do)
    count = keep_ref.shape[1]
    for i in range(3):
        keep_ref[i] = parts[i][:count]
        send_ref[i] = parts[i][count:]


def out_body(
    place, own_ref, keep_ref, mate_ref, x_ref, r0, r1, r2, r3, a_ref, b_ref, bias_ref, gain,
    lbias, aup_ref, sel_ref, hid_ref, z_ref, u_ref, uup_ref, w_ref,
):
    width = x_ref.shape[1]
    half = width // 2

    @pl.when(pl.program_id(0) == 0)
    def _():
        settle_out(place, (r0, r1, r2, r3), w_ref)

    keep, mate = keep_ref[...], mate_ref[...]
    shared = jnp.concatenate(
        [chosen(place[2], keep, mate), chosen(place[2], mate, keep)], axis=1
    )
    att = jnp.where(pl.program_id(0) < 2, own_ref[...], shared)
    sel = sel_ref[...]
    low = dot(att[:, :half], a_ref[0], NT) + dot(att[:, half:], a_ref[1], NT)
    kept = (low * sel).astype(BF16)
    u_ref[...] = kept
    acc = dot(att, w_ref[...].reshape(width, width), NT) + dot(kept, b_ref[...])
    hidden = x_ref[...].astype(F32) + acc + bias_ref[...]
    hid_ref[...] = hidden
    normal, _ = norm_of(hidden)
    z = (normal * gain[...] + lbias[...]).astype(BF16)
    z_ref[...] = z
    uup_ref[...] = (dot(z, aup_ref[...]) * sel).astype(BF16)


def mlp_body(
    rows, place, z_ref, gown_ref, gnear_ref, gfar_ref, uup_ref, sel_ref, hid_ref, wup_ref,
    wdn_ref, bup_own, bup_near, bup_far, adn_own, adn_near, adn_far, upb_ref, bdn_ref, aup_ref,
    dnb_ref, gain,
    own_ref, near_ref, far_ref, ghb_ref, ekeep_ref, esend_ref,
    down_acc, dz_acc, udn_acc, eup_acc, edn_ref, uup_t, edn_t, gy_ref, hid_buf, hid_sem,
):
    total, width = z_ref.shape
    step = pl.program_id(0)
    blocks = [slice(i, i + rows) for i in range(0, total, rows)]

    fetch = pltpu.make_async_copy(hid_ref, hid_buf, hid_sem)

    @pl.when(step == 0)
    def _():
        fetch.start()
        for b in blocks:
            left, right = both_halves(place, gown_ref[b, :], gnear_ref[b, :], gfar_ref[b, :])
            gy = jnp.concatenate([left, right], axis=1)
            gy_ref[b, :] = gy
            edn_ref[b, :] = (dot(gy, bdn_ref[...], NT) * sel_ref[b, :]).astype(BF16)
        edn_t[...] = edn_ref[...].T
        uup_t[...] = uup_ref[...].T
        down_acc[...] = jnp.zeros_like(down_acc)
        dz_acc[...] = jnp.zeros_like(dz_acc)
        udn_acc[...] = jnp.zeros_like(udn_acc)
        eup_acc[...] = jnp.zeros_like(eup_acc)

    chunk = upb_ref.shape[1]
    wup = wup_ref[...].reshape(width, chunk)
    wdn = wdn_ref[...].reshape(width, chunk)
    parts = pl.num_programs(0) // 2
    y = step // parts

    def adapter(own_ref, near_ref, far_ref):
        near, far = near_ref[...], far_ref[...]
        other = jnp.concatenate([chosen(place[2], near, far), chosen(place[2], far, near)])
        return jnp.where(place[3] == y, own_ref[...], other)

    bup = adapter(bup_own, bup_near, bup_far)
    adn = adapter(adn_own, adn_near, adn_far)
    pre = dot(z_ref[...], wup) + dot(uup_ref[...], bup) + upb_ref[...]
    d_act = dot(gy_ref[...], wdn) + dot(edn_ref[...], adn)
    bent = (0.5 * GELU_SCALE) * pre
    turn = jnp.tanh(bent)
    q = 0.5 + 0.5 * turn
    act = (pre * q).astype(BF16)
    d_up = (d_act * (q + q * (bent * (1.0 - turn)))).astype(BF16)
    down_acc[...] += dot(act, wdn, NT)
    dz_acc[...] += dot(d_up, wup, NT)
    udn_acc[...] += dot(act, adn, NT)
    eup_acc[...] += dot(d_up, bup, NT)
    hidden_half = parts * chunk
    for i, (low, high) in enumerate(((uup_t, d_up), (edn_t, act))):
        found = split_rows(place, dot(low[...], high).astype(BF16))
        lanes = pl.ds(pl.multiple_of(i * hidden_half + step % parts * chunk, chunk), chunk)
        ekeep_ref[y, :, lanes], esend_ref[y, :, lanes] = found

    @pl.when(step == pl.num_programs(0) - 1)
    def _():
        fetch.wait()
        gbdn = gaup = 0.0
        for b in blocks:
            sel = sel_ref[b, :]
            e_up = (eup_acc[b, :] * sel).astype(BF16)
            u_dn = (udn_acc[b, :] * sel).astype(BF16)
            hidden = hid_buf[b, :]
            y = hidden + down_acc[b, :] + dot(u_dn, bdn_ref[...]) + dnb_ref[...]
            halves_out(place, y.astype(BF16), b, own_ref, near_ref, far_ref)
            dz = dz_acc[b, :] + dot(e_up, aup_ref[...], NT)
            normal, inverse = norm_of(hidden)
            grad = gy_ref[b, :].astype(F32) + norm_pull(dz, normal, inverse, gain[...])
            ghb_ref[b, :] = grad.astype(BF16)
            gbdn = gbdn + dot_rows(u_dn, gy_ref[b, :])
            gaup = gaup + dot_rows(e_up, z_ref[b, :])
        half = width // 2
        for i, grad in enumerate((gaup, gbdn)):
            start = 2 * hidden_half + i * half
            for column in range(2):
                rows = split_rows(place, grad[:, column * half : (column + 1) * half].astype(BF16))
                lanes = slice(start, start + half)
                ekeep_ref[column, :, lanes], esend_ref[column, :, lanes] = rows


def split_rows(place, grad):
    part = grad.shape[0] // 2
    low, high = grad[:part], grad[part:]
    return chosen(place[2], low, high), chosen(place[2], high, low)


def out_back_body(
    place, g_ref, own_ref, keep_ref, mate_ref, r0, r1, r2, r3, a_ref, b_ref, sel_ref, u_ref,
    d_own, d_keep, d_send, g_keep, g_send, w_ref, e_ref, e_t,
):
    width = g_ref.shape[1]
    half = width // 2
    count = keep_ref.shape[0]
    y = pl.program_id(0)

    @pl.when(y == 0)
    def _():
        def store(row, column, block):
            w_ref[column, row] = block

        settle(place, (r0, r1, r2, r3), True, store)
        e = (dot(g_ref[...], b_ref[...], NT) * sel_ref[...]).astype(BF16)
        e_ref[...] = e
        e_t[...] = e.T
        gb = dot(u_ref[...].T, g_ref[...]).astype(BF16)
        for column in range(2):
            rows = split_rows(place, gb[:, column * half : (column + 1) * half])
            g_keep[column, :, half:], g_send[column, :, half:] = rows

    w = w_ref[y].reshape(width, half)
    d = (dot(g_ref[...], w) + dot(e_ref[...], a_ref[0])).astype(BF16)
    d_own[...] = d[: 2 * count]

    shared = jnp.where(place[2] == y, keep_ref[...], mate_ref[...])
    ga = dot(e_t[...], jnp.concatenate([own_ref[...], shared])).astype(BF16)
    g_keep[y, :, :half], g_send[y, :, :half] = split_rows(place, ga)

    @pl.when(place[2] == y)
    def _():
        d_keep[...] = d[2 * count :]

    @pl.when(place[2] != y)
    def _():
        d_send[...] = d[2 * count :]


def shared_halves(place, keep, mate):
    return chosen(place[2], keep, mate), chosen(place[2], mate, keep)


def qkv_grads_body(
    place, left_ref, right_ref, keep_ref, mate_ref, b_ref, sel_ref, u_ref, z_ref, e_ref,
    keep_out, send_out,
):
    half = left_ref.shape[2]
    part = sel_ref.shape[1] // 2
    shared = shared_halves(place, keep_ref[0], mate_ref[0])
    u_t = u_ref[...].T

    def put(grad, y, i):
        low, high = grad[:part], grad[part:]
        keep_out[y, i, 0] = chosen(place[2], low, high)
        send_out[y, i, 0] = chosen(place[2], high, low)

    low = 0.0
    for y, own_ref in enumerate((left_ref, right_ref)):
        d = jnp.concatenate([own_ref[0], shared[y]])
        low = low + dot(d, b_ref[y], NT)
        put(dot(u_t, d).astype(BF16), y, 0)
    e = (low * sel_ref[...]).astype(BF16)
    e_ref[...] = e
    ga = dot(e.T, z_ref[...]).astype(BF16)
    for y in range(2):
        put(ga[:, y * half : (y + 1) * half], y, 1)


def qkv_back_body(
    shared, place, left_ref, right_ref, p0, p1, p2, p3, r0, r1, r2, r3, a_ref, e_ref, x_ref,
    gh_ref, gain, own_out, near_out, far_out, w_ref,
):
    width = x_ref.shape[1]
    settle_qkv(place, (p0, p1, p2, p3), (r0, r1, r2, r3), w_ref)
    dz = dot(e_ref[...], a_ref[...], NT)
    for k in range(3):
        left, right = left_ref[k], right_ref[k]
        if shared:
            left, right = shared_halves(place, left, right)
        d = jnp.concatenate([left, right], axis=1)
        dz = dz + dot(d, w_ref[k].reshape(width, width), NT)
    normal, inverse = norm_of(x_ref[...].astype(F32))
    grad = gh_ref[...].astype(F32) + norm_pull(dz, normal, inverse, gain[...])
    halves_out(place, grad.astype(BF16), slice(None), own_out, near_out, far_out)


def on_chip_pair(
    mesh_shape, tokens, cotangent, ln1_gain, ln1_bias, ln2_gain, ln2_bias, w_qkv, qv_bias, w_out,
    out_bias, w_up, up_bias, w_down, down_bias, adapter_ids, a_qkv, b_qkv, a_out, b_out, a_up,
    b_up, a_down, b_down,
):
    n_row, n_col = mesh_shape
    count, half = tokens.shape
    width = half * 2
    stack = b_out.shape[0]
    part = stack // 2
    hidden_half = w_up.shape[1]
    hidden = hidden_half * 2
    length = count // adapter_ids.shape[0]
    cut = length // 2
    heads = width // HD
    tb = -(-(length + 1) // 32) * 16
    own_rows, total = 2 * tb, 3 * tb
    scale = HD ** (-0.5)
    both = ("row", "col")
    row, col = lax.axis_index("row"), lax.axis_index("col")
    core, side, n_far = row % 2, row // 2 % 2, n_row // 4
    place = jnp.stack([row // 4, side, core, col]).astype(jnp.int32)

    def device(r, c):
        return r * n_col + c

    far_swaps = [[] for _ in range(n_far.bit_length() - 1)]
    far_turns = [[] for _ in range(n_far - 1)]
    ring_in, ring_back, cross, cores, cols_swap, sides_swap = [], [], [], [], [], []
    for r in range(n_row):
        for c in range(n_col):
            k, mate = r % 2, r + 1 - 2 * (r % 2)
            cores.append((device(r, c), device(mate, c)))
            cols_swap.append((device(r, c), device(r, 1 - c)))
            sides_swap.append((device(r, c), device(r ^ 2, c)))
            for turn, pairs in enumerate(far_turns):
                pairs.append((device(r, c), device((r + 4 * (turn + 1)) % n_row, c)))
            for bit, pairs in enumerate(far_swaps):
                pairs.append((device(r, c), device(r ^ (4 << bit), c)))
            if k != c:
                ring_in.append((device(r, c), device(r, 1 - c)))
                ring_back.append((device(r, c), device(mate, c)))
                cross.append((device(r, c), device(mate, 1 - c)))
            else:
                ring_in.append((device(r, c), device(mate, c)))
                ring_back.append((device(r, c), device(r, 1 - c)))

    def move(values, pairs):
        return lax.ppermute(values, both, pairs)

    def pick(pair, index):
        return jnp.where(index == 0, pair[0], pair[1])

    def ordered(mine, other, index, axis):
        return jnp.where(
            index == 0,
            jnp.concatenate([mine, other], axis),
            jnp.concatenate([other, mine], axis),
        )

    def tie(*values):
        return lax.optimization_barrier(values)

    thirds = [struct((total, half), BF16)] * 3
    third_specs = [fixed((total, half))] * 3

    def spread(values):
        return call(
            functools.partial(spread_body, length, cut, own_rows, tb),
            (1,),
            [SPOT, fixed((count, half))],
            third_specs,
            thirds,
            scratch=[pltpu.VMEM((count, half), F32)],
        )(place, values)

    def join(own, near, far, kind):
        return call(
            functools.partial(join_body, length, cut, own_rows, len(own)),
            (1,),
            [SPOT] + [fixed(t.shape) for t in (*own, *near, *far)],
            fixed((count, half)),
            struct((count, half), kind),
            scratch=[pltpu.VMEM((count, half), F32)],
            us=3,
        )(place, *own, *near, *far)

    x_own, x_near, x_far = spread(tokens)
    x_near, x_far, w_qkv, w_out = tie(x_near, x_far, w_qkv, w_out)
    mine_first = jnp.concatenate(
        [jnp.swapaxes(w_qkv, 0, 1).reshape(-1, 3 * half), w_out.T], axis=1
    )
    mine_second = jnp.concatenate([w_up, w_down.T], axis=1)
    adapt_first = jnp.concatenate(
        [jnp.swapaxes(b_qkv, 0, 1).reshape(stack, 3 * half), a_out.T], axis=1
    )
    adapt_second = jnp.concatenate([b_up, a_down.T], axis=1)
    deep = width // n_row

    def turned(block):
        return jnp.stack([block] + [move(block, pairs) for pairs in far_turns])

    def doubled(found, pairs):
        return jnp.concatenate([found, move(found, pairs)])

    def part_of(values):
        return lax.dynamic_slice_in_dim(values, core * part, part, 0)

    def widened(values, near, far):
        return ordered(values[None], ordered(near, far, core, 0)[None], col, 0)

    x_near, x_far = move(x_near, ring_in), move(x_far, cross)
    near0, near1 = turned(mine_first[:, :width]), turned(mine_first[:, width:])
    near0, x_near, x_far, mine_second = tie(near0, x_near, x_far, mine_second)
    near0, near1 = tie(near0, near1)
    x_parts = (x_own, x_near, x_far)
    big_second = lax.all_gather(mine_second, both, axis=0, tiled=False)
    big_second = big_second.reshape(n_row, n_col, deep, 2 * hidden_half)
    near0, near1 = doubled(near0, sides_swap), doubled(near1, cols_swap)
    ad_near = move(part_of(adapt_first), cols_swap)
    biases = jnp.concatenate([qv_bias[0], qv_bias[1], up_bias])[None]
    bias_pair = ordered(biases, move(biases, cols_swap), col, 0)
    ids = jnp.where(core == col, adapter_ids, move(adapter_ids, cores))
    g_own, g_near, g_far = spread(cotangent)
    near0, near1, bias_pair, ids, ad_near = tie(near0, near1, bias_pair, ids, ad_near)
    ad_first = widened(adapt_first, ad_near, move(ad_near, cores))
    last0, last1 = move(near0, cols_swap), move(near1, sides_swap)
    far0, far1 = move(near0, cores), move(near1, cores)
    adapt_part = part_of(adapt_second)
    valid = jnp.arange(own_rows)[:, None]
    here, there = jnp.where(core == 0, cut, length - cut), jnp.where(core == 0, length - cut, cut)

    def mask_of(good):
        return jnp.broadcast_to(jnp.where(good, 0.0, -1e30), (own_rows, 2 * HD)).astype(BF16)

    mask_own = mask_of(valid < length)
    mask_shared = mask_of((valid < here) | ((valid >= tb) & (valid < tb + there)))
    last0, last1, far0, far1, ad_first, g_near, g_far = tie(
        last0, last1, far0, far1, ad_first, g_near, g_far
    )
    last0, adapt_part, adapt_second, mask_own, mask_shared = tie(
        last0, adapt_part, adapt_second, mask_own, mask_shared
    )
    ad_near = move(adapt_part, cols_swap)
    blocks0 = (near0, last0, far0, move(last0, cores))
    blocks1 = (near1, last1, far1, move(last1, cores))
    qv_rows = jnp.stack(
        [
            bias_pair[:, :half].reshape(1, width),
            jnp.zeros((1, width), F32),
            bias_pair[:, half:width].reshape(1, width),
        ]
    )
    up_row = bias_pair[:, width:].reshape(1, hidden)

    owners = lax.iota(jnp.int32, stack) // RANK
    own_id = jnp.where(core == 0, ids[0], ids[2])
    places = lax.iota(jnp.int32, total)[:, None]
    sel = (jnp.where(places < own_rows, own_id, ids[1]) == owners[None]).astype(F32)

    gain1, bias1, gain2, bias2 = (t[None] for t in (ln1_gain, ln1_bias, ln2_gain, ln2_bias))

    rows_block = pl.BlockSpec((tb, width), lambda i: (i, 0))
    sel_block = pl.BlockSpec((tb, stack), lambda i: (i, 0))
    every = fixed((total, width))
    thin = fixed((total, stack))
    vec = fixed((1, width))
    pieces0 = [fixed((n_row // 2, deep, width))] * 4
    pieces1 = [fixed((n_row // 2, deep, half))] * 4
    pieces_out = [
        pl.BlockSpec(
            (n_row // 2, deep, half), lambda *_: (0, 0, 1), pipeline_mode=pl.Buffered(1)
        )
    ] * 4
    w_qkv_room = [pltpu.VMEM((3, n_row, deep, width), BF16)]
    w_out_room = [pltpu.VMEM((n_row, deep, width), BF16)]
    ad_out_spec = pl.BlockSpec(
        (n_col, stack, half), lambda *_: (0, 0, 3), pipeline_mode=pl.Buffered(1)
    )
    low_k = pl.BlockSpec((total, stack), lambda k: (0, k))
    shared_k = pl.BlockSpec((1, tb, half), lambda k: (k, 0, 0))
    ad_k = pl.BlockSpec((n_col, stack, half), lambda k: (0, 0, k))
    shared_struct = struct((3, tb, half), BF16)
    half_rows = struct((tb, half), BF16)

    third_rows = pl.BlockSpec((tb, half), lambda i: (i, 0))
    low_block = pl.BlockSpec((tb, 3 * stack), lambda i: (i, 0))
    all_three = pl.BlockSpec((3, tb, width), lambda i: (0, i, 0))
    shared_three = fixed((3, tb, half))
    x, z1, u_qkv, qkv, qkv_keep, qkv_send = call(
        functools.partial(qkv_body, scale),
        (3,),
        [
            SPOT, third_rows, third_rows, third_rows, vec, vec, *pieces0, *pieces1,
            fixed((width, 3 * stack)),
            pl.BlockSpec(
                (n_col, stack, 3 * half), lambda i: (0, 0, 0), pipeline_mode=pl.Buffered(1)
            ),
            fixed((3, 1, width)), sel_block,
        ],
        [rows_block, rows_block, low_block, all_three, shared_three, shared_three],
        [
            struct((total, width), BF16),
            struct((total, width), BF16),
            struct((total, 3 * stack), BF16),
            struct((3, total, width), BF16),
            shared_struct,
            shared_struct,
        ],
        scratch=w_qkv_room,
    )(place, *x_parts, gain1, bias1, *blocks0, *blocks1, a_qkv, ad_first, qv_rows, sel)

    qkv_mate = move(qkv_send, cores)
    qkv, g_near, g_far = tie(qkv, g_near, g_far)
    g_near, g_far = move(g_near, ring_in), move(g_far, cross)

    head_p = pl.BlockSpec((2, own_rows, own_rows), lambda h: (h, 0, 0))
    pair_k = pl.BlockSpec((3, tb, 2 * HD), lambda h: (0, 0, h))
    pair_rows = pl.BlockSpec((tb, 2 * HD), lambda h: (0, h))
    wide = 4 * HD
    att_own, p_own = call(
        attend_body,
        (width // wide,),
        [pl.BlockSpec((1, own_rows, wide), lambda h, k=k: (k, 0, h)) for k in range(3)]
        + [fixed((own_rows, 2 * HD))],
        [
            pl.BlockSpec((own_rows, wide), lambda h: (0, h)),
            pl.BlockSpec((4, own_rows, own_rows), lambda h: (h, 0, 0)),
        ],
        [struct((own_rows, width), BF16), struct((heads, own_rows, own_rows), BF16)],
    )(qkv, qkv, qkv, mask_own)
    qkv_mate, att_own = tie(qkv_mate, att_own)
    wide_k = pl.BlockSpec((3, tb, wide), lambda h: (0, 0, h))
    wide_rows = pl.BlockSpec((tb, wide), lambda h: (0, h))
    att_keep, att_send, p_sh = call(
        attend_shared_body,
        (half // wide,),
        [wide_k, wide_k, fixed((own_rows, 2 * HD))],
        [wide_rows, wide_rows, pl.BlockSpec((4, own_rows, own_rows), lambda h: (h, 0, 0))],
        [half_rows, half_rows, struct((heads // 2, own_rows, own_rows), BF16)],
    )(qkv_keep, qkv_mate, mask_shared)
    att_send, ad_near = tie(att_send, ad_near)
    att_mate = move(att_send, cores)
    g_parts = (g_own, g_near, g_far)
    ad_second = (adapt_second, ad_near, move(ad_near, cores))

    own_block = pl.BlockSpec((tb, width), lambda i: (jnp.minimum(i, 1), 0))
    shared_rows = fixed((tb, half))
    hid, z2, u_out, u_up = call(
        out_body,
        (3,),
        [
            SPOT, own_block, shared_rows, shared_rows, rows_block, *pieces_out,
            ad_out_spec, fixed((stack, width)), vec, vec, vec, fixed((width, stack)), sel_block,
        ],
        [rows_block, rows_block, sel_block, sel_block],
        [
            struct((total, width), F32),
            struct((total, width), BF16),
            struct((total, stack), BF16),
            struct((total, stack), BF16),
        ],
        scratch=w_out_room,
    )(
        place, att_own, att_keep, att_mate, x, *blocks1, ad_first, b_out, out_bias[None],
        gain2, bias2, a_up, sel,
    )

    chunk = half
    parts = hidden_half // chunk

    def w_spec(shift):
        return pl.BlockSpec(
            (n_row, 1, deep, chunk), lambda j: (0, j // parts, 0, j % parts + shift)
        )

    def ad_specs(shift):
        return [
            pl.BlockSpec((rows, chunk), lambda j: (0, j % parts + shift))
            for rows in (stack, part, part)
        ]

    early_half = fixed((2, part, 2 * hidden_half + 2 * half))
    early_struct = struct((2, part, 2 * hidden_half + 2 * half), BF16)
    y_own, y_near, y_far, ghb, early_keep, early_send = call(
        functools.partial(mlp_body, tb),
        (2 * parts,),
        [SPOT, every]
        + third_specs
        + [
            thin, thin, pl.BlockSpec(memory_space=pl.ANY), w_spec(0), w_spec(parts), *ad_specs(0), *ad_specs(parts),
            pl.BlockSpec((1, chunk), lambda j: (0, j)), fixed((stack, width)),
            fixed((width, stack)), vec, vec,
        ],
        third_specs + [every, early_half, early_half],
        thirds
        + [struct((total, width), BF16), early_struct, early_struct],
        scratch=[
            pltpu.VMEM((total, width), F32),
            pltpu.VMEM((total, width), F32),
            pltpu.VMEM((total, stack), F32),
            pltpu.VMEM((total, stack), F32),
            pltpu.VMEM((total, stack), BF16),
            pltpu.VMEM((stack, total), BF16),
            pltpu.VMEM((stack, total), BF16),
            pltpu.VMEM((total, width), BF16),
            pltpu.VMEM((total, width), F32),
            pltpu.SemaphoreType.DMA,
        ],
    )(
        place, z2, *g_parts, u_up, sel, hid, big_second, big_second, *ad_second, *ad_second, up_row,
        b_down, a_up, down_bias[None], gain2,
    )

    def added(kept, sent):
        return (kept.astype(F32) + sent.astype(F32)).astype(BF16)

    quarter = part // 2

    def quarter_of(values, index):
        return lax.dynamic_slice_in_dim(values, index * quarter, quarter, 1)

    def side_sent(values):
        return move(quarter_of(values, 1 - side), sides_swap)

    early_sent = move(early_send, cores)
    y_near, y_far = move(y_near, ring_back), move(y_far, cross)
    out_half = fixed((2, part, width))
    d_att, d_keep, d_send, out_keep, out_send = call(
        out_back_body,
        (2,),
        [
            SPOT, every, pl.BlockSpec((own_rows, half), lambda i: (0, i)), shared_rows,
            shared_rows, *pieces_out,
            pl.BlockSpec((1, stack, half), lambda i: (i, 0, 3)), fixed((stack, width)), thin, thin,
        ],
        [
            pl.BlockSpec((own_rows, half), lambda i: (0, i)), shared_rows, shared_rows, out_half,
            out_half,
        ],
        [
            struct((own_rows, width), BF16),
            half_rows,
            half_rows,
            struct((2, part, width), BF16),
            struct((2, part, width), BF16),
        ],
        scratch=[
            pltpu.VMEM((2, n_row, deep, half), BF16),
            pltpu.VMEM((total, stack), BF16),
            pltpu.VMEM((stack, total), BF16),
        ],
    )(place, ghb, att_own, att_keep, att_mate, *blocks1, ad_first, b_out, sel, u_out)

    d_mate = move(d_send, cores)
    early_sum = jnp.concatenate(
        [added(early_keep, early_sent), added(out_keep, move(out_send, cores))], axis=2
    )
    d_mate, early_sum = tie(d_mate, early_sum)
    early_sent = side_sent(early_sum)

    g_keep, g_send = call(
        functools.partial(attend_back_shared_body, scale),
        (heads // 4,),
        [pair_k, pair_k, head_p, pair_rows, pair_rows, pair_rows, pair_rows],
        [pair_k, pair_k],
        [shared_struct, shared_struct],
        us=8,
    )(qkv_keep, qkv_mate, p_sh, att_keep, att_send, d_keep, d_mate)
    d_att, g_send = tie(d_att, g_send)
    g_mate = move(g_send, cores)
    quarters = heads // 4

    def own_back(shift, d_out):
        return call(
            functools.partial(attend_back_body, scale),
            (quarters,),
            [
                pl.BlockSpec((1, own_rows, 2 * HD), lambda h, k=k: (k, 0, h + shift))
                for k in range(3)
            ]
            + [
                pl.BlockSpec((2, own_rows, own_rows), lambda h: (h + shift, 0, 0)),
                pl.BlockSpec((own_rows, 2 * HD), lambda h: (0, h + shift)),
                pl.BlockSpec((own_rows, 2 * HD), lambda h: (0, h + shift)),
            ],
            pl.BlockSpec((3, own_rows, 2 * HD), lambda h: (0, 0, h)),
            struct((3, own_rows, half), BF16),
            us=9,
        )(qkv, qkv, qkv, p_own, att_own, d_out)

    d_left = own_back(0, d_att)
    early_sum = added(quarter_of(early_sum, side), early_sent)
    d_left, d_att, early_sum, y_near, y_far = tie(d_left, d_att, early_sum, y_near, y_far)
    early_sent = move(pick(early_sum, 1 - col), cols_swap)
    d_right = own_back(quarters, d_att)

    grad_spec = pl.BlockSpec((2, 2, 1, part, half), lambda k: (0, 0, k, 0, 0))
    grad_struct = struct((2, 2, 3, part, half), BF16)
    early_sum = added(pick(early_sum, col), early_sent)
    d_right, early_sum = tie(d_right, early_sum)
    early_sent = move(early_sum, far_swaps[0])
    half_k = pl.BlockSpec((1, own_rows, half), lambda k: (k, 0, 0))
    e_qkv, q_kept, q_sent = call(
        qkv_grads_body,
        (3,),
        [SPOT, half_k, half_k, shared_k, shared_k, ad_k, thin, low_k, every],
        [low_k, grad_spec, grad_spec],
        [struct((total, 3 * stack), BF16), grad_struct, grad_struct],
        us=7,
    )(place, d_left, d_right, g_keep, g_mate, ad_first, sel, u_qkv, z1)

    def side_of(values, index):
        return jnp.where(index == 0, values[:, 0], values[:, 1])

    sums = added(q_kept, move(q_sent, cores)).reshape(2, 2, 3 * part, half)
    early_sum = added(early_sum, early_sent)
    sums, e_qkv, early_sum = tie(sums, e_qkv, early_sum)
    early_sent = move(early_sum, far_swaps[-1])
    q_sent = move(side_of(sums, 1 - side), sides_swap)

    def token_rows(block, left, right):
        at = block % 2
        d_spec = pl.BlockSpec((3, tb, half), lambda i: (0, at, 0), pipeline_mode=pl.Buffered(1))
        rows = pl.BlockSpec((tb, width), lambda i: (block, 0), pipeline_mode=pl.Buffered(1))
        low = pl.BlockSpec((tb, 3 * stack), lambda i: (block, 0), pipeline_mode=pl.Buffered(1))
        return call(
            functools.partial(qkv_back_body, block == 2),
            (1,),
            [
                SPOT, d_spec, d_spec, *pieces0, *pieces1, fixed((width, 3 * stack)), low, rows,
                rows, vec,
            ],
            [shared_rows] * 3,
            [half_rows] * 3,
            scratch=w_qkv_room,
            us=6,
        )(place, left, right, *blocks0, *blocks1, a_qkv, e_qkv, x, ghb, gain1)

    t_own, t_near, t_far = [], [], []

    def sent_rows(own, near, far):
        t_own.append(own)
        t_near.append(move(near, ring_back))
        t_far.append(move(far, cross))

    rows_own, rows_near, rows_far = token_rows(0, d_left, d_right)
    q_sent, rows_near, rows_far = tie(q_sent, rows_near, rows_far)
    sums = added(side_of(sums, side), q_sent)
    sums, d_left, d_right = tie(sums, d_left, d_right)
    q_sent = move(pick(sums, 1 - col), cols_swap)
    sent_rows(rows_own, rows_near, rows_far)
    rows_own, rows_near, rows_far = token_rows(1, d_left, d_right)
    q_sent, rows_near, rows_far, early_sent = tie(q_sent, rows_near, rows_far, early_sent)
    early_sum = added(early_sum, early_sent)
    sums = added(pick(sums, col), q_sent)
    sums, g_keep, g_mate = tie(sums, g_keep, g_mate)
    q_sent = move(sums, far_swaps[1])
    sent_rows(rows_own, rows_near, rows_far)
    edge = 2 * hidden_half
    whole = edge + 4 * half
    split_lanes = [slice(edge, edge + 2 * half), slice(edge + 3 * half, whole)]
    rest = jnp.concatenate([early_sum[:, lanes] for lanes in split_lanes], axis=1)
    rest = move(rest, cols_swap)
    rows_own, rows_near, rows_far = token_rows(2, g_keep, g_mate)
    early_sum = jnp.concatenate([early_sum, rest], axis=1)
    q_sent, rows_near, rows_far, early_sum, y_own = tie(
        q_sent, rows_near, rows_far, early_sum, y_own
    )
    sums = added(sums, q_sent)
    q_sent = move(sums, far_swaps[0])
    sent_rows(rows_own, rows_near, rows_far)
    early_sent = move(early_sum, sides_swap)
    layer_out = join([y_own], [y_near], [y_far], BF16)
    q_sent, layer_out, *gone = tie(q_sent, layer_out, *t_near[:2], *t_far[:2])
    t_near, t_far = gone[:2] + t_near[2:], gone[2:] + t_far[2:]
    sums = added(sums, q_sent)
    for pairs in far_swaps[2:]:
        sums = added(sums, move(sums, pairs))
    side_sums = move(sums, sides_swap)
    early_sum = ordered(early_sum, early_sent, side, 0)
    side_sums, t_near[2], t_far[2], early_sum = tie(
        side_sums, t_near[2], t_far[2], early_sum
    )
    early_sent = move(early_sum, cores)
    tokens_grad = join(t_own, t_near, t_far, F32)
    mine = ordered(early_sum, early_sent, core, 0).astype(F32)
    sums = ordered(sums[None], side_sums[None], side, 0)
    a_sent = move(sums[1:], cols_swap)
    own_starts = (edge, edge + half, edge + 3 * half)
    a_up_sum, b_down_sum, b_out_sum = (
        ordered(
            mine[:, start : start + half],
            mine[:, whole + i * half : whole + (i + 1) * half],
            col,
            1,
        )
        for i, start in enumerate(own_starts)
    )
    a_out_sum, a_up_sum = mine[:, edge + 2 * half : edge + 3 * half].T, a_up_sum.T
    b_up_sum, a_down_sum = mine[:, :hidden_half], mine[:, hidden_half:edge].T
    a_sent, tokens_grad, a_out_sum, a_up_sum, b_up_sum, a_down_sum, b_down_sum, b_out_sum = tie(
        a_sent, tokens_grad, a_out_sum, a_up_sum, b_up_sum, a_down_sum, b_down_sum, b_out_sum
    )
    every_sum = jnp.concatenate([sums[:1], ordered(sums[1:], a_sent, col, 0)])
    every_sum = every_sum.reshape(3, 3, part, half)
    every_sum = ordered(every_sum, move(every_sum, cores), core, 2).reshape(3, 3 * stack, half)
    b_sum = every_sum[0].reshape(3, stack, half).astype(F32)
    a_sum = jnp.concatenate([every_sum[1].T, every_sum[2].T]).astype(F32)
    return (
        layer_out,
        tokens_grad,
        a_sum,
        b_sum,
        a_out_sum,
        b_out_sum,
        a_up_sum,
        b_up_sum,
        a_down_sum,
        b_down_sum,
    )


def solution(mesh):
    placed = (
        P("row", "col"),
        P("row", "col"),
        P(),
        P(),
        P(),
        P(),
        P(None, "row", "col"),
        P(None, "col"),
        P("col", "row"),
        P(),
        P("row", "col"),
        P("col"),
        P("col", "row"),
        P(),
        P("row"),
        P(),
        P(None, None, "col"),
        P("col", None),
        P(),
        P(),
        P(None, "col"),
        P("col", None),
        P(),
    )
    shape = (mesh.shape["row"], mesh.shape["col"])
    paired = shape[1] == 2 and shape[0] >= 16 and shape[0] & (shape[0] - 1) == 0
    return jax.shard_map(
        functools.partial(on_chip_pair, shape) if paired else on_device,
        mesh=mesh,
        in_specs=placed,
        out_specs=(
            P("row", "col"),
            P("row", "col"),
            P(),
            P(None, None, "col"),
            P("col", None),
            P(),
            P(),
            P(None, "col"),
            P("col", None),
            P(),
        ),
        check_vma=False,
    )
```
